128 devices in a mesh: grp: 4 (over x), mem: 32 (over z, y, core).
Axes of the slice: x: 4, y: 4, z: 4, core: 2. Of those that a mesh axis runs over, the one named last changes fastest.
Arguments:
- embeddings: float32 [32768, 768], P(('grp', 'mem')), may hold values from -6 to 6
- cluster_ids: int32 [32768, 1], P(('grp', 'mem')), may hold values from 0 to 3; in each aligned block of 256 rows (0 to 255, 256 to 511, ...) at most 128 rows name the same one
Outputs:
- nearest: float32 [32768], P(('grp', 'mem'))
The draws below stay inside these ranges and needn't reach their ends.
Inputs may be any that keep to these rules, and one draw needn't show every extreme that they name: `cluster_ids`: among the rows of one device no cluster id appears more than 128 times, and some cluster reaches 128 on some device.
All inputs are finite; a program needn't handle non-finite values.
Results may differ from the reference program's by a relative error of at most 0.0011.
Values may be sent and summed in bfloat16 or wider, within the bound.
A program may use at most 64 MiB of HBM per device.

```python
import math
import jax
import jax.numpy as jnp
import numpy as np
from jax import lax

D = 768
ROWS_DEV = 256
CL_GRP = 1
K = 4
MOST = 128
ROWS = 32768
N_GRP = 4


def level_of(rng, shape, shards, low, top_value):
    def one(position, parts):
        draws = jax.random.uniform(jax.random.fold_in(jax.random.fold_in(rng, 6), position), (parts,), jnp.float32, low / len(shards), top_value / len(shards))
        return jnp.repeat(jnp.exp(draws), shape[position] // parts).reshape((-1,) + (1,) * (len(shape) - position - 1))

    factor_of = one(*shards[0])
    for cut in shards[1:]:
        factor_of = factor_of * one(*cut)
    return factor_of


def deal_out(key, own, number, rows, number_of, top, limit, lean):
    order = jax.random.permutation(key, number_of)
    heavy_load, ordinary = shares(number_of, rows * top, limit, lean, True), shares(number_of, rows * top, limit, lean, False)
    places = jnp.arange(number_of)

    def named(lengths, turn):
        used = int((lengths > 0).sum())
        fixed = max(1, used // 4)
        shifted = fixed + (places - fixed + turn * (used - fixed)) % max(1, number_of - fixed)
        return jnp.zeros((number_of,), jnp.int32).at[order[jnp.where(places < fixed, places, shifted)]].set(jnp.asarray(lengths, jnp.int32))

    lengths = jnp.where(number % 4 == 0, named(heavy_load, number // 4), named(ordinary, number - number // 4 - 1))
    mixed = jax.random.permutation(jax.random.fold_in(own, 3), number_of)
    source_of, receiver = mixed[0:number_of // 2 * 2:2], mixed[1:number_of // 2 * 2:2]
    slack = jnp.minimum(lengths[source_of] - 1, limit - lengths[receiver]) // 2
    slack = jnp.where((source_of == order[0]) | (receiver == order[0]) | (lengths[receiver] == 0), 0, jnp.maximum(slack, 0))
    shifted = jax.random.randint(jax.random.fold_in(own, 4), (number_of // 2,), 0, 1 << 20) % (slack + 1)
    lengths = lengths.at[source_of].add(-shifted).at[receiver].add(shifted)
    items = jnp.searchsorted(jnp.cumsum(lengths), jnp.arange(rows * top), side="right").astype(jnp.int32)
    listing = items.reshape(top, rows).T
    listing = listing[jax.random.permutation(jax.random.fold_in(own, 1), rows)]
    turn = jax.random.randint(jax.random.fold_in(own, 2), (rows, 1), 0, top)
    return jnp.take_along_axis(listing, (jnp.arange(top)[None, :] + turn) % top, axis=1)


def shares(count, total, most, slope, full):
    loads = [(1 << 20) // math.isqrt(grade ** slope) + 1 for grade in range(1, count + 1)]
    largest = most if full else min(most, max(-(-total // count), total * loads[0] // sum(loads)))
    least = 1 if total - largest >= count - 1 else 0
    given, surplus = [largest] + [least] * (count - 1), total - largest - least * (count - 1)
    while surplus > 0:
        free = [i for i in range(1, count) if given[i] < largest] or [i for i in range(1, count) if given[i] < most]
        whole, budget = sum([loads[i] for i in free]), surplus
        for i in free:
            extra = min(most - given[i], max(1, budget * loads[i] // whole), surplus)
            given[i] = given[i] + extra
            surplus = surplus - extra
    return np.array(given)


def noise(stream_key, extent, scale, reach, cuts=(), held_as=jnp.bfloat16):
    loudness = level_of(stream_key, extent, cuts, -0.22, 0.18) if cuts else 1.0
    array = jax.random.normal(stream_key, extent, jnp.float32) * scale * loudness
    return jnp.minimum(jnp.maximum(array, -reach), reach).astype(held_as)


def setup_inputs(seed: int = 0) -> dict:
    seeds = jax.random.split(jax.random.key(seed), 3)
    embeddings = noise(seeds[0], (ROWS, D), 1.0, 6.0, ((0, 128),), jnp.float32)
    cluster_ids_keys = jax.random.split(jax.random.fold_in(seeds[1], 1), ROWS // ROWS_DEV)
    cluster_ids_turns = jax.random.permutation(jax.random.fold_in(seeds[1], 3), ROWS // ROWS_DEV)
    cluster_ids = jax.vmap(lambda own, number: deal_out(jax.random.fold_in(seeds[1], 2), own, number, ROWS_DEV, K, 1, MOST, 2))(cluster_ids_keys, cluster_ids_turns).reshape((ROWS, 1))
    return {"embeddings": embeddings, "cluster_ids": cluster_ids}


FILL = -4.0

def reference(embeddings, cluster_ids):
    count = embeddings.shape[0]
    squares = lax.optimization_barrier(jnp.sum(embeddings * embeddings, axis=1, keepdims=True))
    unit = (embeddings * lax.rsqrt(squares + 1e-06)).astype(jnp.bfloat16).astype(jnp.float32)
    labels = cluster_ids[:, 0].astype(jnp.int32)
    clusters = N_GRP * CL_GRP
    onehot = (labels[:, None] == jnp.arange(clusters, dtype=jnp.int32)[None, :]).astype(jnp.int32)
    running = jnp.cumsum(onehot.reshape(count // ROWS_DEV, ROWS_DEV, clusters), axis=1).reshape(count, clusters)
    ranks = lax.optimization_barrier(jnp.sum(onehot * (running - 1), axis=1)).astype(jnp.int32)
    device = jnp.arange(count, dtype=jnp.int32) // ROWS_DEV
    places = (device * MOST + ranks).astype(jnp.int32)
    total = count // ROWS_DEV * MOST
    padded = jnp.zeros((clusters, total, embeddings.shape[1]), jnp.float32).at[labels, places].set(unit)
    present = jnp.zeros((clusters, total), jnp.float32).at[labels, places].set(1.0)
    block = 512 if total % 512 == 0 else total

    def one_cluster(pair):
        members, alive = pair

        def one_block(start):
            rows = lax.dynamic_slice_in_dim(members, start, block, 0)
            sims = jnp.dot(rows, members.T, precision=lax.Precision.HIGHEST, preferred_element_type=jnp.float32)
            row_index = start + jnp.arange(block, dtype=jnp.int32)
            keep = (alive[None, :] > 0) & (row_index[:, None] != jnp.arange(total, dtype=jnp.int32)[None, :])
            return lax.optimization_barrier(jnp.max(jnp.where(keep, sims, FILL), axis=1))
        starts = jnp.arange(0, total, block, dtype=jnp.int32)
        return lax.map(one_block, starts).reshape(total)
    best = lax.map(one_cluster, (padded, present))
    return best[labels, places]
```

```python
import functools

import jax
import jax.numpy as jnp
from jax import lax
from jax.experimental import pallas as pl
from jax.experimental.pallas import tpu as pltpu
from jax.sharding import PartitionSpec as P

FILL = -4.0
MESH = pl.DeviceIdType.MESH
SIDE = 4
DIRS = ((1, 0, 0), (3, 0, 0), (0, 1, 0), (0, 3, 0), (0, 0, 1), (0, 0, 3))

OFFSETS = (
    (0, 0, 0),
    (0, 0, 2),
    (2, 0, 2),
    (0, 0, 3),
    (3, 0, 0),
    (0, 1, 0),
    (1, 1, 0),
    (0, 2, 0),
    (1, 2, 0),
    (0, 3, 0),
    (2, 0, 1),
    (3, 0, 1),
)

FIRST_SENDS = (
    ((0, 3, 5), (0, 4, 1), (0, 9, 3), (1, 3, 5), (1, 4, 1), (1, 5, 2), (0, 5, 2), (1, 9, 3)),
    ((1, 5, 2), (0, 3, 5), (0, 4, 1), (0, 5, 2), (0, 9, 3), (1, 3, 5), (1, 4, 1), (1, 9, 3)),
)

STEPS = (
    (((('o', 0),), (('o', 0),)), ((0, 0), (0, 0))),
    (((('a', 3, 0, ((1, 5),)), ('a', 4, 0, ((11, 4),)), ('a', 9, 0, ((7, 3),)), ('a', 11, 0, ((10, 1),)), ('a', 3, 1, ((1, 5),)), ('a', 4, 1, ((11, 4),)), ('a', 5, 1, ((6, 0),)), ('a', 7, 0, ((8, 0),))), (('a', 5, 1, ((6, 0), (7, 2))), ('a', 3, 0, ((1, 5),)), ('a', 4, 0, ((11, 4),)), ('a', 5, 0, ((6, 0),)), ('a', 9, 0, ((7, 3),)))), ((0, 3), (0, 5))),
    (((), (('a', 6, 1, ()), ('a', 6, 0, ((8, 2),)), ('a', 11, 0, ((10, 1),)))), ((0, 4), (0, 6))),
    (((('a', 5, 0, ((6, 0),)), ('a', 9, 1, ((7, 3),))), (('a', 3, 1, ((1, 5),)), ('a', 4, 1, ((11, 4),)))), ((0, 5), (0, 3))),
    (((('o', 5),), ()), ((5, 3), (0, 4))),
    (((('a', 6, 1, ((8, 2),)), ('a', 11, 1, ((10, 1),))), (('o', 3),)), ((5, 9), (3, 6))),
    (((('o', 3),), (('o', 4),)), ((3, 9), (4, 3))),
    (((('o', 4),), ()), ((4, 3), (4, 6))),
    (((('a', 1, 0, ()), ('a', 10, 0, ((2, 4),))), (('a', 7, 0, ()), ('a', 7, 1, ((8, 0),)), ('o', 5))), ((4, 5), (5, 3))),
    (((), ()), ((3, 11), (0, 7))),
    (((('a', 6, 0, ()),), (('a', 11, 1, ((10, 1),)),)), ((5, 11), (3, 7))),
    (((), ()), ((3, 6), (4, 7))),
    (((), ()), ((4, 6), (3, 11))),
    (((('a', 7, 1, ()), ('o', 11)), (('a', 1, 0, ()), ('a', 8, 0, ()), ('a', 10, 0, ((2, 4),)))), ((11, 6), (5, 11))),
    (((), (('o', 11),)), ((11, 9), (11, 6))),
    (((('a', 2, 0, ()), ('a', 8, 0, ())), ()), ((3, 7), (11, 7))),
    (((), (('o', 6),)), ((4, 7), (6, 7))),
    (((('o', 6),), (('a', 9, 1, ()),)), ((6, 7), (3, 9))),
    (((('a', 1, 1, ()), ('a', 8, 1, ()), ('a', 10, 1, ((2, 4),))), ()), ((11, 7), (11, 9))),
    (((), (('a', 2, 0, ()), ('a', 8, 1, ()))), ((0, 1), (3, 8))),
    (((), ()), ((0, 10), (4, 8))),
    (((('f', 0),), (('f', 4),)), ((3, 8), (11, 8))),
    (((), (('a', 1, 1, ()), ('a', 10, 1, ((2, 4),)))), ((3, 10), (0, 1))),
    (((('f', 3),), ()), ((4, 8), (0, 10))),
    (((('f', 4), ('a', 2, 1, ())), (('f', 0),)), ((5, 1), (3, 10))),
    (((), (('f', 3),)), ((6, 1), (5, 1))),
    (((), ()), ((6, 10), (6, 1))),
    (((('o', 7),), ()), ((7, 1), (6, 10))),
    (((), (('a', 2, 1, ()), ('o', 7))), ((11, 1), (7, 1))),
    (((), (('o', 8),)), ((11, 8), (8, 1))),
    (((('f', 11), ('o', 9)), (('f', 8), ('o', 9))), ((9, 10), (9, 10))),
    (((('f', 9), ('f', 10), ('o', 8)), (('f', 9), ('f', 10))), ((8, 1), (11, 1))),
    (((('f', 8), ('o', 1)), (('f', 11), ('o', 1))), ((1, 2), (1, 2))),
    (((('f', 1),), (('f', 1),)), ((5, 2), (5, 2))),
    (((('f', 5),), (('f', 5),)), ((6, 2), (6, 2))),
    (((('f', 6),), (('f', 6),)), ((7, 2), (7, 2))),
    (((('f', 2), ('f', 7)), (('f', 2), ('f', 7))), None),
)


SLOTS = len(OFFSETS)


def greeted():
    both = set()
    for x, y, z in OFFSETS:
        both.add((x, y, z))
        both.add(((-x) % SIDE, (-y) % SIDE, (-z) % SIDE))
    near = [(d, 0) for d in DIRS if d not in both]
    far = [(d, k) for d in sorted(both) for k in (0, 1) if any(d) or k]
    return near + far


def kernel(chunks, emb_ref, lab_ref, out_ref, emb, buf, labels, label_rows, row_best, column_best, outgoing,
           incoming, load_sem, send_sem, recv_sem, give_sem, take_sem, label_send, label_recv, result_send,
           result_recv):
    rows, width = emb.shape
    part = rows // chunks
    gx = lax.axis_index("grp")
    mem = lax.axis_index("mem")
    core = lax.rem(mem, 2)
    other = 1 - core
    gy = lax.rem(mem // 2, SIDE)
    gz = mem // (2 * SIDE)
    xs = [lax.rem(gx + k, SIDE) for k in range(SIDE)]
    ys = [lax.rem(gy + k, SIDE) for k in range(SIDE)]
    zs = [lax.rem(gz + k, SIDE) for k in range(SIDE)]

    def at(offset, on):
        x, y, z = (k % SIDE for k in offset)
        return (xs[x], (zs[z] * SIDE + ys[y]) * 2 + on)

    load = pltpu.make_async_copy(emb_ref, emb, load_sem)
    load.start()
    barrier = pltpu.get_barrier_semaphore()
    friends = greeted()
    for offset, flip in friends:
        pl.semaphore_signal(barrier, inc=1, device_id=at(offset, other if flip else core), device_id_type=MESH)

    def chunk_of(slot, h, on):
        return buf.at[slot, on, pl.ds(h * part, part)]

    def relay(source, target, h, direction):
        return pltpu.make_async_remote_copy(
            src_ref=chunk_of(source, h, core), dst_ref=chunk_of(target, h, core),
            send_sem=send_sem.at[target, h], recv_sem=recv_sem.at[target, h],
            device_id=at(DIRS[direction], core), device_id_type=MESH)

    def share(slot, h, on):
        return pltpu.make_async_remote_copy(
            src_ref=chunk_of(slot, h, on), dst_ref=chunk_of(slot, h, on),
            send_sem=give_sem.at[slot, h], recv_sem=take_sem.at[slot, h],
            device_id=at((0, 0, 0), other), device_id_type=MESH)

    labels[0, core] = lab_ref[...].astype(jnp.float32)
    load.wait()

    def normalise(h):
        e = emb[pl.ds(h * part, part)]
        squares = jnp.sum(e * e, axis=1, keepdims=True)
        buf[0, core, pl.ds(h * part, part)] = (e * lax.rsqrt(squares + 1e-06)).astype(jnp.bfloat16)

    for h in range(chunks):
        normalise(h)
    pl.semaphore_wait(barrier, len(friends))

    for which in (0, 1):
        @pl.when(core == which)
        def _(which=which):
            for h, target, direction in FIRST_SENDS[which]:
                relay(0, target, h, direction).start()

    for h in range(chunks):
        share(0, h, core).start()

    def tell(slot, on, flip):
        return pltpu.make_async_remote_copy(
            src_ref=labels.at[0, core], dst_ref=labels.at[slot, core],
            send_sem=label_send.at[slot, flip], recv_sem=label_recv.at[1 if slot else 0],
            device_id=at(OFFSETS[slot], on), device_id_type=MESH)

    tell(0, other, 1).start()
    for slot in range(1, SLOTS):
        tell(slot, core, 0).start()
        tell(slot, other, 1).start()

    def clear(slot, carry):
        row_best[slot] = jnp.full(row_best.shape[1:], FILL, jnp.float32)
        column_best[slot] = jnp.full(column_best.shape[1:], FILL, jnp.float32)
        return carry

    lax.fori_loop(0, SLOTS, clear, 0)

    pltpu.make_async_copy(labels.at[0, other], labels.at[0, other], label_recv.at[0]).wait()
    rest = labels.at[pl.ds(1, SLOTS - 1)]
    pltpu.make_async_copy(rest, rest, label_recv.at[1]).wait()

    def spread(slot, carry):
        for unit in (0, 1):
            line = jnp.broadcast_to(labels[slot, unit], (128, rows))
            label_rows[slot, pl.ds(unit * rows, rows)] = line.T
        return carry

    lax.fori_loop(0, SLOTS, spread, 0)

    def tile(i, j, own=False):
        sims = lax.dot_general(buf[i].reshape(2 * rows, width), buf[j, core], (((1,), (1,)), ((), ())),
                               preferred_element_type=jnp.float32)
        names = label_rows[i]
        best = row_best[i]
        if own:
            row_at = lax.broadcasted_iota(jnp.int32, (2 * rows, 128), 0) - core * rows
            column_at = lax.broadcasted_iota(jnp.int32, (2 * rows, 128), 1)
        for k in range(rows // 128):
            lanes = slice(k * 128, (k + 1) * 128)
            keep = names == labels[j, core, :, lanes]
            if own:
                keep = keep & (row_at != column_at + k * 128)
            scores = jnp.where(keep, sims[:, lanes], FILL)
            best = jnp.maximum(best, scores)
            column_best[j, :, lanes] = jnp.maximum(
                column_best[j, :, lanes], jnp.max(scores.reshape(2 * rows // 8, 8, 128), axis=0))
        row_best[i] = best

    def answer(slot, unit):
        back = tuple(-k for k in OFFSETS[slot])
        return pltpu.make_async_remote_copy(
            src_ref=outgoing.at[slot, unit], dst_ref=incoming.at[slot, core],
            send_sem=result_send.at[slot, unit], recv_sem=result_recv.at[1 if slot else 0],
            device_id=at(back, unit), device_id_type=MESH)

    def finish(slot):
        by_row = jnp.max(row_best[slot].T, axis=0, keepdims=True)
        by_column = jnp.max(column_best[slot], axis=0, keepdims=True)
        for unit in (0, 1):
            mine = by_row[:, unit * rows:(unit + 1) * rows]
            outgoing[slot, unit] = jnp.where(core == unit, jnp.maximum(mine, by_column), mine)
        if slot:
            answer(slot, 0).start()
            answer(slot, 1).start()
        else:
            incoming[0, core] = outgoing[0, core]
            answer(0, other).start()

    for before, pair in STEPS:
        for which in (0, 1):
            if not before[which]:
                continue

            @pl.when(core == which)
            def _(todo=before[which]):
                for op in todo:
                    if op[0] == "a":
                        slot, h = op[1], op[2]
                        pltpu.make_async_copy(
                            chunk_of(slot, h, core), chunk_of(slot, h, core), recv_sem.at[slot, h]).wait()
                        for target, direction in op[3]:
                            relay(slot, target, h, direction).start()
                        share(slot, h, core).start()
                    elif op[0] == "o":
                        for h in range(chunks):
                            pltpu.make_async_copy(
                                chunk_of(op[1], h, other), chunk_of(op[1], h, other), take_sem.at[op[1], h]).wait()
                    else:
                        finish(op[1])
        if pair is not None:
            (i, j), (p, q) = pair
            tile(i + core * (p - i), j + core * (q - j), own=(i == j))

    pltpu.make_async_copy(incoming.at[0, other], incoming.at[0, other], result_recv.at[0]).wait()
    rest = incoming.at[pl.ds(1, SLOTS - 1)]
    pltpu.make_async_copy(rest, rest, result_recv.at[1]).wait()
    out_ref[...] = jnp.max(incoming[...].reshape(2 * SLOTS, 1, rows), axis=0)

    shared = {w: {op[1] for before, _ in STEPS for op in before[w] if op[0] == "o"} for w in (0, 1)}
    for which in (0, 1):
        @pl.when(core == which)
        def _(which=which):
            for slot in range(SLOTS):
                if slot not in shared[which]:
                    for h in range(chunks):
                        pltpu.make_async_copy(
                            chunk_of(slot, h, other), chunk_of(slot, h, other), take_sem.at[slot, h]).wait()
    for slot in range(SLOTS):
        for h in range(chunks):
            share(slot, h, core).wait_send()
            if slot:
                relay(0, slot, h, 0).wait_send()
        if slot:
            tell(slot, core, 0).wait_send()
            answer(slot, 0).wait_send()
            answer(slot, 1).wait_send()
        else:
            answer(0, other).wait_send()
        tell(slot, other, 1).wait_send()


def body(embeddings, cluster_ids):
    rows, width = embeddings.shape
    chunks = 1 + max(h for h, _, _ in FIRST_SENDS[0])
    copies = pltpu.SemaphoreType.DMA((SLOTS, chunks))
    pairs = pltpu.SemaphoreType.DMA((SLOTS, 2))
    best = pl.pallas_call(
        functools.partial(kernel, chunks),
        out_shape=jax.ShapeDtypeStruct((1, rows), jnp.float32),
        in_specs=[pl.BlockSpec(memory_space=pl.ANY), pl.BlockSpec(memory_space=pltpu.VMEM)],
        out_specs=pl.BlockSpec(memory_space=pltpu.VMEM),
        scratch_shapes=[
            pltpu.VMEM((rows, width), jnp.float32),
            pltpu.VMEM((SLOTS, 2, rows, width), jnp.bfloat16),
            pltpu.VMEM((SLOTS, 2, 1, rows), jnp.float32),
            pltpu.VMEM((SLOTS, 2 * rows, 128), jnp.float32),
            pltpu.VMEM((SLOTS, 2 * rows, 128), jnp.float32),
            pltpu.VMEM((SLOTS, 8, rows), jnp.float32),
            pltpu.VMEM((SLOTS, 2, 1, rows), jnp.float32),
            pltpu.VMEM((SLOTS, 2, 1, rows), jnp.float32),
            pltpu.SemaphoreType.DMA,
            copies, copies, copies, copies,
            pairs, pltpu.SemaphoreType.DMA((2,)),
            pairs, pltpu.SemaphoreType.DMA((2,)),
        ],
        compiler_params=pltpu.CompilerParams(
            collective_id=0, has_side_effects=True, vmem_limit_bytes=48 * 1024 * 1024),
    )(embeddings, cluster_ids.reshape(1, rows))
    return best.reshape(rows)


def solution(mesh):
    return jax.shard_map(
        body,
        mesh=mesh,
        in_specs=(P(("grp", "mem"), None), P(("grp", "mem"), None)),
        out_specs=P(("grp", "mem")),
        check_vma=False,
    )
```

```python
import functools

import jax
import jax.numpy as jnp
from jax import lax
from jax.experimental import pallas as pl
from jax.experimental.pallas import tpu as pltpu
from jax.sharding import PartitionSpec as P

FILL = -4.0
MESH = pl.DeviceIdType.MESH
SIDE = 4
VMEM_BYTES = 64 * 1024 * 1024 - 512 * 1024
DIRS = ((1, 0, 0), (3, 0, 0), (0, 1, 0), (0, 3, 0), (0, 0, 1), (0, 0, 3))

OFFSETS = (
    (0, 0, 0),
    (0, 0, 2),
    (2, 0, 2),
    (0, 0, 3),
    (3, 0, 0),
    (0, 1, 0),
    (1, 1, 0),
    (0, 2, 0),
    (1, 2, 0),
    (0, 3, 0),
    (2, 0, 1),
    (3, 0, 1),
)

FIRST_SENDS = (
    ((0, 3, 5), (0, 4, 1), (0, 9, 3), (1, 3, 5), (1, 4, 1), (1, 5, 2), (0, 5, 2), (1, 9, 3)),
    ((1, 5, 2), (0, 3, 5), (0, 4, 1), (0, 5, 2), (0, 9, 3), (1, 3, 5), (1, 4, 1), (1, 9, 3)),
)

STEPS = (
    (((('o', 0),), (('o', 0),)), ((0, 0), (0, 0))),
    (((('a', 3, 0, ((1, 5),)), ('a', 4, 0, ((11, 4),)), ('a', 9, 0, ((7, 3),)), ('a', 11, 0, ((10, 1),)), ('a', 3, 1, ((1, 5),)), ('a', 4, 1, ((11, 4),)), ('a', 5, 1, ((6, 0),)), ('a', 7, 0, ((8, 0),))), (('a', 5, 1, ((6, 0), (7, 2))), ('a', 3, 0, ((1, 5),)), ('a', 4, 0, ((11, 4),)), ('a', 5, 0, ((6, 0),)), ('a', 9, 0, ((7, 3),)))), ((0, 3), (0, 5))),
    (((), (('a', 6, 1, ()), ('a', 6, 0, ((8, 2),)), ('a', 11, 0, ((10, 1),)))), ((0, 4), (0, 6))),
    (((('a', 5, 0, ((6, 0),)), ('a', 9, 1, ((7, 3),))), (('a', 3, 1, ((1, 5),)), ('a', 4, 1, ((11, 4),)))), ((0, 5), (0, 3))),
    (((('o', 5),), ()), ((5, 3), (0, 4))),
    (((('a', 6, 1, ((8, 2),)), ('a', 11, 1, ((10, 1),))), (('o', 3),)), ((5, 9), (3, 6))),
    (((('o', 3),), (('o', 4),)), ((3, 9), (4, 3))),
    (((('o', 4),), ()), ((4, 3), (4, 6))),
    (((('a', 1, 0, ()), ('a', 10, 0, ((2, 4),))), (('a', 7, 0, ()), ('a', 7, 1, ((8, 0),)), ('o', 5))), ((4, 5), (5, 3))),
    (((), ()), ((3, 11), (0, 7))),
    (((('a', 6, 0, ()),), (('a', 11, 1, ((10, 1),)),)), ((5, 11), (3, 7))),
    (((), ()), ((3, 6), (4, 7))),
    (((), ()), ((4, 6), (3, 11))),
    (((('a', 7, 1, ()), ('o', 11)), (('a', 1, 0, ()), ('a', 8, 0, ()), ('a', 10, 0, ((2, 4),)))), ((11, 6), (5, 11))),
    (((), (('o', 11),)), ((11, 9), (11, 6))),
    (((('a', 2, 0, ()), ('a', 8, 0, ())), ()), ((3, 7), (11, 7))),
    (((), (('o', 6),)), ((4, 7), (6, 7))),
    (((('o', 6),), (('a', 9, 1, ()),)), ((6, 7), (3, 9))),
    (((('a', 1, 1, ()), ('a', 8, 1, ()), ('a', 10, 1, ((2, 4),))), ()), ((11, 7), (11, 9))),
    (((), (('a', 2, 0, ()), ('a', 8, 1, ()))), ((0, 1), (3, 8))),
    (((), ()), ((0, 10), (4, 8))),
    (((('f', 0),), (('f', 4),)), ((3, 8), (11, 8))),
    (((), (('a', 1, 1, ()), ('a', 10, 1, ((2, 4),)))), ((3, 10), (0, 1))),
    (((('f', 3),), ()), ((4, 8), (0, 10))),
    (((('f', 4), ('a', 2, 1, ())), (('f', 0),)), ((5, 1), (3, 10))),
    (((), (('f', 3),)), ((6, 1), (5, 1))),
    (((), ()), ((6, 10), (6, 1))),
    (((('o', 7),), ()), ((7, 1), (6, 10))),
    (((), (('a', 2, 1, ()), ('o', 7))), ((11, 1), (7, 1))),
    (((), (('o', 8),)), ((11, 8), (8, 1))),
    (((('f', 11), ('o', 9)), (('f', 8), ('o', 9))), ((9, 10), (9, 10))),
    (((('f', 9), ('f', 10), ('o', 8)), (('f', 9), ('f', 10))), ((8, 1), (11, 1))),
    (((('f', 8), ('o', 1)), (('f', 11), ('o', 1))), ((1, 2), (1, 2))),
    (((('f', 1),), (('f', 1),)), ((5, 2), (5, 2))),
    (((('f', 5),), (('f', 5),)), ((6, 2), (6, 2))),
    (((('f', 6),), (('f', 6),)), ((7, 2), (7, 2))),
    (((('f', 2), ('f', 7)), (('f', 2), ('f', 7))), None),
)


SLOTS = len(OFFSETS)


def greeted():
    both = set()
    for x, y, z in OFFSETS:
        both.add((x, y, z))
        both.add(((-x) % SIDE, (-y) % SIDE, (-z) % SIDE))
    near = [(d, 0) for d in DIRS if d not in both]
    far = [(d, k) for d in sorted(both) for k in (0, 1) if any(d) or k]
    return near + far


def packed(values, bits):
    return sum(v << (bits * n) for n, v in enumerate(values))


def digit(word, n, bits):
    return lax.rem(lax.shift_right_logical(word, bits * n), 1 << bits)


def lookup(values, n):
    words = [packed(values[k:k + 7], 4) for k in range(0, len(values), 7)]
    word = jnp.int32(words[0])
    for k, w in enumerate(words[1:], 1):
        word = jnp.where(n >= 7 * k, jnp.int32(w), word)
    return digit(word, lax.rem(n, 7), 4)


NONE = 15


def finishing(which):
    waiting, at_step = [], []
    for before, pair in STEPS:
        waiting += [op[1] for op in before[which] if op[0] == "f"]
        if pair is not None:
            at_step.append(waiting.pop(0) if waiting else NONE)
    return at_step, waiting


def kernel(chunks, emb_ref, lab_ref, out_ref, emb, ids, buf, labels, label_rows, row_best, column_best, outgoing,
           incoming, load_sem, send_sem, recv_sem, give_sem, take_sem, label_send,
           label_recv, result_send, result_recv):
    rows, width = emb.shape
    part = rows // chunks
    load = pltpu.make_async_copy(emb_ref, emb, load_sem.at[0])
    load.start()
    load_ids = pltpu.make_async_copy(lab_ref, ids, load_sem.at[1])
    load_ids.start()
    gx = lax.axis_index("grp")
    mem = lax.axis_index("mem")
    core = lax.rem(mem, 2)
    other = 1 - core
    gy = lax.rem(mem // 2, SIDE)
    gz = mem // (2 * SIDE)
    xs = [lax.rem(gx + k, SIDE) for k in range(SIDE)]
    ys = [lax.rem(gy + k, SIDE) for k in range(SIDE)]
    zs = [lax.rem(gz + k, SIDE) for k in range(SIDE)]

    def at(offset, on):
        x, y, z = (k % SIDE for k in offset)
        return (xs[x], (zs[z] * SIDE + ys[y]) * 2 + on)

    barrier = pltpu.get_barrier_semaphore()
    friends = greeted()
    for offset, flip in friends:
        pl.semaphore_signal(barrier, inc=1, device_id=at(offset, other if flip else core), device_id_type=MESH)

    def chunk_of(slot, h, on):
        return buf.at[slot, on, pl.ds(h * part, part)]

    def relay(source, target, h, direction):
        return pltpu.make_async_remote_copy(
            src_ref=chunk_of(source, h, core), dst_ref=chunk_of(target, h, core),
            send_sem=send_sem.at[target, h], recv_sem=recv_sem.at[target, h],
            device_id=at(DIRS[direction], core), device_id_type=MESH)

    def share(slot, h, on):
        return pltpu.make_async_remote_copy(
            src_ref=chunk_of(slot, h, on), dst_ref=chunk_of(slot, h, on),
            send_sem=give_sem.at[slot, h], recv_sem=take_sem.at[slot, h],
            device_id=at((0, 0, 0), other), device_id_type=MESH)

    load_ids.wait()
    labels[0, core] = ids[...].astype(jnp.float32)
    load.wait()
    for h in range(chunks):
        e = emb[pl.ds(h * part, part)]
        squares = jnp.sum(e * e, axis=1, keepdims=True)
        buf[0, core, pl.ds(h * part, part)] = (e * lax.rsqrt(squares + 1e-06)).astype(jnp.bfloat16)
    pl.semaphore_wait(barrier, len(friends))

    for which in (0, 1):
        @pl.when(core == which)
        def _(which=which):
            for h, target, direction in FIRST_SENDS[which]:
                relay(0, target, h, direction).start()

    for h in range(chunks):
        share(0, h, core).start()

    def tell(slot, on, flip):
        return pltpu.make_async_remote_copy(
            src_ref=labels.at[0, core], dst_ref=labels.at[slot, core],
            send_sem=label_send.at[slot, flip], recv_sem=label_recv.at[1 if slot else 0],
            device_id=at(OFFSETS[slot], on), device_id_type=MESH)

    tell(0, other, 1).start()
    for slot in range(1, SLOTS):
        tell(slot, core, 0).start()
        tell(slot, other, 1).start()

    def clear(slot, carry):
        row_best[slot] = jnp.full(row_best.shape[1:], FILL, jnp.float32)
        column_best[slot] = jnp.full(column_best.shape[1:], FILL, jnp.float32)
        return carry

    lax.fori_loop(0, SLOTS, clear, 0)

    pltpu.make_async_copy(labels.at[0, other], labels.at[0, other], label_recv.at[0]).wait()
    rest = labels.at[pl.ds(1, SLOTS - 1)]
    pltpu.make_async_copy(rest, rest, label_recv.at[1]).wait()

    def spread(slot, carry):
        for unit in (0, 1):
            line = jnp.broadcast_to(labels[slot, unit], (128, rows))
            label_rows[slot, pl.ds(unit * rows, rows)] = line.T
        return carry

    lax.fori_loop(0, SLOTS, spread, 0)

    def tile(i, j, own=False):
        sims = lax.dot_general(buf[i].reshape(2 * rows, width), buf[j, core], (((1,), (1,)), ((), ())),
                               preferred_element_type=jnp.float32)
        names = label_rows[i]
        best = row_best[i]
        if own:
            row_at = lax.broadcasted_iota(jnp.int32, (2 * rows, 128), 0) - core * rows
            column_at = lax.broadcasted_iota(jnp.int32, (2 * rows, 128), 1)
        for k in range(rows // 128):
            lanes = slice(k * 128, (k + 1) * 128)
            keep = names == labels[j, core, :, lanes]
            if own:
                keep = keep & (row_at != column_at + k * 128)
            scores = jnp.where(keep, sims[:, lanes], FILL)
            best = jnp.maximum(best, scores)
            column_best[j, :, lanes] = jnp.maximum(
                column_best[j, :, lanes], jnp.max(scores.reshape(2 * rows // 8, 8, 128), axis=0))
        row_best[i] = best

    def answer(slot, unit):
        x, y, z = (SIDE - digit(jnp.int32(packed([o[k] for o in OFFSETS], 2)), slot, 2) for k in range(3))
        x, y, z = lax.rem(gx + x, SIDE), lax.rem(gy + y, SIDE), lax.rem(gz + z, SIDE)
        return pltpu.make_async_remote_copy(
            src_ref=outgoing.at[slot, unit], dst_ref=incoming.at[slot, core],
            send_sem=result_send.at[slot, unit], recv_sem=result_recv.at[1],
            device_id=(x, (z * SIDE + y) * 2 + unit), device_id_type=MESH)

    def answer_chip():
        return pltpu.make_async_remote_copy(
            src_ref=outgoing.at[0, other], dst_ref=incoming.at[0, core],
            send_sem=result_send.at[0, 0], recv_sem=result_recv.at[0],
            device_id=at((0, 0, 0), other), device_id_type=MESH)

    def arrived(slot, h, onward):
        pltpu.make_async_copy(chunk_of(slot, h, core), chunk_of(slot, h, core), recv_sem.at[slot, h]).wait()
        for target, direction in onward:
            relay(slot, target, h, direction).start()
        share(slot, h, core).start()

    def taken(slot):
        for h in range(chunks):
            pltpu.make_async_copy(
                chunk_of(slot, h, other), chunk_of(slot, h, other), take_sem.at[slot, h]).wait()

    def finish(slot):
        by_row = jnp.max(row_best[slot].T, axis=0, keepdims=True)
        by_column = jnp.max(column_best[slot], axis=0, keepdims=True)
        for unit in (0, 1):
            mine = by_row[:, unit * rows:(unit + 1) * rows]
            outgoing[slot, unit] = jnp.where(core == unit, jnp.maximum(mine, by_column), mine)

        @pl.when(slot > 0)
        def _():
            answer(slot, 0).start()
            answer(slot, 1).start()

        @pl.when(slot == 0)
        def _():
            incoming[0, core] = outgoing[0, core]
            answer_chip().start()

    def handle(before):
        for which in (0, 1):
            todo = [op for op in before[which] if op[0] != "f"]
            if todo:
                @pl.when(core == which)
                def _(todo=todo):
                    for op in todo:
                        if op[0] == "a":
                            arrived(*op[1:])
                        else:
                            taken(op[1])

    ends = [finishing(0), finishing(1)]
    pairs = [pair for _, pair in STEPS if pair is not None]

    def chosen(values, n):
        return jnp.where(core == 0, lookup(values[0], n), lookup(values[1], n))

    taken(0)
    tile(0, 0, own=True)

    def step(n, carry):
        for g in range(0, len(pairs), 6):
            @pl.when(lax.div(n, 6) == g // 6)
            def _(g=g):
                for k in range(max(g, 1), min(g + 6, len(pairs))):
                    @pl.when(n == k)
                    def _(k=k):
                        handle(STEPS[k][0])
        ended = chosen([e[0] for e in ends], n)

        @pl.when(ended != NONE)
        def _():
            finish(ended)
        tile(chosen([[p[w][0] for p in pairs] for w in (0, 1)], n),
             chosen([[p[w][1] for p in pairs] for w in (0, 1)], n))
        return carry

    lax.fori_loop(1, len(pairs), step, 0)
    handle(STEPS[-1][0])
    left = max(len(e[1]) for e in ends)

    def last(n, carry):
        ended = chosen([(e[1] + [NONE] * left)[:left] for e in ends], n)

        @pl.when(ended != NONE)
        def _():
            finish(ended)
        return carry

    lax.fori_loop(0, left, last, 0)

    pltpu.make_async_copy(incoming.at[0, other], incoming.at[0, other], result_recv.at[0]).wait()
    rest = incoming.at[pl.ds(1, SLOTS - 1)]
    pltpu.make_async_copy(rest, rest, result_recv.at[1]).wait()
    out_ref[...] = jnp.max(incoming[...].reshape(2 * SLOTS, 1, rows), axis=0)

    shared = [{op[1] for before, _ in STEPS for op in before[w] if op[0] == "o"} for w in (0, 1)]
    for which in (0, 1):
        @pl.when(core == which)
        def _(which=which):
            for slot in range(SLOTS):
                if slot not in shared[which]:
                    taken(slot)
    for slot in range(SLOTS):
        for h in range(chunks):
            share(slot, h, core).wait_send()
            if slot:
                relay(0, slot, h, 0).wait_send()
        if slot:
            tell(slot, core, 0).wait_send()
            answer(slot, 0).wait_send()
            answer(slot, 1).wait_send()
        else:
            answer_chip().wait_send()
        tell(slot, other, 1).wait_send()


def body(embeddings, cluster_ids):
    rows, width = embeddings.shape
    chunks = 1 + max(h for h, _, _ in FIRST_SENDS[0])
    copies = pltpu.SemaphoreType.DMA((SLOTS, chunks))
    pairs = pltpu.SemaphoreType.DMA((SLOTS, 2))
    best = pl.pallas_call(
        functools.partial(kernel, chunks),
        out_shape=jax.ShapeDtypeStruct((1, rows), jnp.float32),
        in_specs=[pl.BlockSpec(memory_space=pl.ANY), pl.BlockSpec(memory_space=pl.ANY)],
        out_specs=pl.BlockSpec(memory_space=pltpu.VMEM),
        scratch_shapes=[
            pltpu.VMEM((rows, width), jnp.float32),
            pltpu.VMEM((1, rows), jnp.int32),
            pltpu.VMEM((SLOTS, 2, rows, width), jnp.bfloat16),
            pltpu.VMEM((SLOTS, 2, 1, rows), jnp.float32),
            pltpu.VMEM((SLOTS, 2 * rows, 128), jnp.float32),
            pltpu.VMEM((SLOTS, 2 * rows, 128), jnp.float32),
            pltpu.VMEM((SLOTS, 8, rows), jnp.float32),
            pltpu.VMEM((SLOTS, 2, 1, rows), jnp.float32),
            pltpu.VMEM((SLOTS, 2, 1, rows), jnp.float32),
            pltpu.SemaphoreType.DMA((2,)),
            copies, copies, copies, copies,
            pairs, pltpu.SemaphoreType.DMA((2,)),
            pairs, pltpu.SemaphoreType.DMA((2,)),
        ],
        compiler_params=pltpu.CompilerParams(
            collective_id=0, has_side_effects=True, vmem_limit_bytes=VMEM_BYTES),
    )(embeddings, cluster_ids.reshape(1, rows))
    return best.reshape(rows)


def solution(mesh):
    return jax.shard_map(
        body,
        mesh=mesh,
        in_specs=(P(("grp", "mem"), None), P(("grp", "mem"), None)),
        out_specs=P(("grp", "mem")),
        check_vma=False,
    )
```

```python
import functools

import jax
import jax.numpy as jnp
from jax import lax
from jax.experimental import pallas as pl
from jax.experimental.pallas import tpu as pltpu
from jax.sharding import PartitionSpec as P

FILL = -4.0
MESH = pl.DeviceIdType.MESH
SIDE = 4
VMEM_BYTES = 64 * 1024 * 1024 - 512 * 1024
DIRS = ((1, 0, 0), (3, 0, 0), (0, 1, 0), (0, 3, 0), (0, 0, 1), (0, 0, 3))

OFFSETS = (
    (0, 0, 0),
    (0, 0, 2),
    (2, 0, 2),
    (0, 0, 3),
    (3, 0, 0),
    (0, 1, 0),
    (1, 1, 0),
    (0, 2, 0),
    (1, 2, 0),
    (0, 3, 0),
    (2, 0, 1),
    (3, 0, 1),
)

FIRST_SENDS = (
    ((0, 4, 0, 1), (0, 9, 0, 3), (0, 3, 0, 5)),
    ((0, 5, 1, 2),),
)

LAST_SENDS = (
    ((1, 1), (2, 1), (7, 1), (8, 0), (8, 1), (10, 1)),
    ((1, 1), (2, 1), (8, 0), (8, 1), (9, 1), (10, 1)),
)

STEPS = (
    (((), 0, None, 0, 0),
     ((), 0, None, 0, 0)),
    (((('a', 3, 0), ('a', 4, 0), ('a', 9, 0), ('s', 4, 11, 0, 4), ('s', 0, 4, 1, 1, 4, 0), ('s', 0, 5, 1, 2), ('s', 9, 7, 0, 3, 9, 0), ('s', 0, 3, 1, 5, 3, 0), ('a', 11, 0), ('s', 0, 5, 0, 2, 5, 1), ('s', 0, 9, 1, 3, 7, 0), ('a', 3, 1), ('a', 4, 1), ('a', 5, 1), ('a', 7, 0)), None, None, 0, 3),
     ((('s', 0, 4, 0, 1), ('s', 0, 5, 0, 2, 5, 1), ('s', 0, 9, 0, 3), ('s', 0, 3, 0, 5), ('a', 5, 1), ('s', 5, 6, 1, 0), ('a', 3, 0), ('a', 4, 0), ('a', 5, 0), ('a', 9, 0)), None, None, 0, 5)),
    (((('s', 5, 6, 1, 0), ('s', 4, 11, 1, 4, 11, 0)), None, None, 0, 4),
     ((('s', 5, 6, 0, 0, 6, 1), ('s', 4, 11, 0, 4), ('a', 6, 1), ('s', 0, 4, 1, 1, 4, 0), ('s', 0, 3, 1, 5, 3, 0), ('a', 6, 0), ('a', 11, 0)), None, None, 0, 6)),
    (((('s', 11, 10, 0, 1, 4, 1), ('s', 3, 1, 0, 5, 3, 1), ('a', 5, 0), ('a', 9, 1)), None, None, 0, 5),
     ((('s', 5, 7, 1, 2, 5, 0), ('s', 9, 7, 0, 3, 9, 0), ('a', 3, 1), ('a', 4, 1)), None, None, 0, 3)),
    (((('s', 5, 6, 0, 0, 6, 1),), 5, None, 5, 3),
     ((('s', 4, 11, 1, 4, 11, 0),), None, None, 0, 4)),
    (((('a', 6, 1), ('a', 11, 1)), None, None, 5, 9),
     ((), 3, None, 3, 6)),
    (((('s', 9, 7, 1, 3, 9, 1),), 3, None, 3, 9),
     ((('s', 11, 10, 0, 1, 4, 1), ('s', 6, 8, 0, 2, 7, 1), ('s', 3, 1, 0, 5, 3, 1)), 4, None, 4, 3)),
    (((('a', 1, 0), ('a', 10, 0), ('s', 7, 8, 0, 0, 6, 0), ('s', 10, 2, 0, 4, 11, 1)), 4, None, 4, 3),
     ((('a', 7, 0), ('a', 7, 1)), None, None, 4, 6)),
    (((), None, None, 4, 5),
     ((), 5, None, 5, 3)),
    (((('a', 6, 0),), None, None, 3, 11),
     ((('a', 11, 1),), None, None, 0, 7)),
    (((('s', 11, 10, 1, 1, 10, 0), ('s', 6, 8, 1, 2, 5, 0), ('s', 3, 1, 1, 5, 1, 0)), None, None, 5, 11),
     ((('s', 0, 9, 1, 3, 7, 0),), None, None, 3, 7)),
    (((), None, None, 3, 6),
     ((), None, None, 4, 7)),
    (((('a', 7, 1),), None, None, 4, 6),
     ((('a', 1, 0), ('a', 8, 0), ('a', 10, 0), ('s', 7, 8, 1, 0, 6, 0), ('s', 10, 2, 0, 4, 11, 1)), None, None, 3, 11)),
    (((('a', 2, 0), ('a', 8, 0)), 11, None, 11, 6),
     ((), None, None, 5, 11)),
    (((), None, None, 11, 9),
     ((('s', 11, 10, 1, 1, 10, 0), ('s', 3, 1, 1, 5, 1, 0)), 11, None, 11, 6)),
    (((), None, None, 3, 7),
     ((), None, None, 11, 7)),
    (((('a', 1, 1), ('a', 8, 1), ('a', 10, 1), ('s', 10, 2, 1, 4, 2, 0)), None, None, 4, 7),
     ((('a', 9, 1),), 6, None, 6, 7)),
    (((), 6, None, 6, 7),
     ((('a', 2, 0), ('a', 8, 1)), None, None, 3, 9)),
    (((), None, None, 11, 7),
     ((), None, None, 11, 9)),
    (((), None, None, 0, 1),
     ((), None, None, 3, 8)),
    (((), None, None, 0, 10),
     ((('a', 1, 1), ('a', 10, 1), ('s', 10, 2, 1, 4, 2, 0)), None, None, 4, 8)),
    (((('a', 2, 1),), None, 0, 3, 8),
     ((), None, 4, 11, 8)),
    (((), None, None, 3, 10),
     ((), None, None, 0, 1)),
    (((), None, 3, 4, 8),
     ((), None, None, 0, 10)),
    (((), None, 4, 5, 1),
     ((), None, 0, 3, 10)),
    (((), None, None, 6, 1),
     ((('a', 2, 1),), None, 3, 5, 1)),
    (((), None, None, 6, 10),
     ((), None, None, 6, 1)),
    (((), 7, None, 7, 1),
     ((), None, None, 6, 10)),
    (((), None, None, 11, 1),
     ((), 7, None, 7, 1)),
    (((), None, None, 11, 8),
     ((), 8, None, 8, 1)),
    (((), 9, 11, 9, 10),
     ((), 9, 8, 9, 10)),
    (((), 8, 9, 8, 1),
     ((), None, 9, 11, 1)),
    (((), 1, 10, 1, 2),
     ((), 1, 10, 1, 2)),
    (((), None, 8, 5, 2),
     ((), None, 11, 5, 2)),
    (((), None, 1, 6, 2),
     ((), None, 1, 6, 2)),
    (((), None, 5, 7, 2),
     ((), None, 5, 7, 2)),
)

TAIL = (
    ((), (6, 7, 2)),
    ((), (6, 7, 2)),
)


SLOTS = len(OFFSETS)


def greeted():
    both = set()
    for x, y, z in OFFSETS:
        both.add((x, y, z))
        both.add(((-x) % SIDE, (-y) % SIDE, (-z) % SIDE))
    near = [(d, 0) for d in DIRS if d not in both]
    far = [(d, k) for d in sorted(both) for k in (0, 1) if any(d) or k]
    return near + far


def packed(values, bits):
    return sum(v << (bits * n) for n, v in enumerate(values))


def digit(word, n, bits):
    return lax.rem(lax.shift_right_logical(word, bits * n), 1 << bits)


def lookup(values, n):
    words = [packed(values[k:k + 7], 4) for k in range(0, len(values), 7)]
    word = jnp.int32(words[0])
    for k, w in enumerate(words[1:], 1):
        word = jnp.where(n >= 7 * k, jnp.int32(w), word)
    return digit(word, lax.rem(n, 7), 4)


NONE = 15


def column(which, place):
    return [NONE if pair[which][place] is None else pair[which][place] for pair in STEPS]


def kernel(chunks, emb_ref, lab_ref, out_ref, emb, ids, buf, labels, label_rows, row_best, column_best, outgoing,
           incoming, load_sem, send_sem, recv_sem, give_sem, take_sem, label_send,
           label_recv, result_send, result_recv):
    rows, width = emb.shape
    part = rows // chunks
    load = pltpu.make_async_copy(emb_ref, emb, load_sem.at[0])
    load.start()
    load_ids = pltpu.make_async_copy(lab_ref, ids, load_sem.at[1])
    load_ids.start()
    gx = lax.axis_index("grp")
    mem = lax.axis_index("mem")
    core = lax.rem(mem, 2)
    other = 1 - core
    gy = lax.rem(mem // 2, SIDE)
    gz = mem // (2 * SIDE)
    xs = [lax.rem(gx + k, SIDE) for k in range(SIDE)]
    ys = [lax.rem(gy + k, SIDE) for k in range(SIDE)]
    zs = [lax.rem(gz + k, SIDE) for k in range(SIDE)]

    def at(offset, on):
        x, y, z = (k % SIDE for k in offset)
        return (xs[x], (zs[z] * SIDE + ys[y]) * 2 + on)

    barrier = pltpu.get_barrier_semaphore()
    friends = greeted()
    for offset, flip in friends:
        pl.semaphore_signal(barrier, inc=1, device_id=at(offset, other if flip else core), device_id_type=MESH)

    def chunk_of(slot, h, on):
        return buf.at[slot, on, pl.ds(h * part, part)]

    def relay(source, target, h, direction):
        return pltpu.make_async_remote_copy(
            src_ref=chunk_of(source, h, core), dst_ref=chunk_of(target, h, core),
            send_sem=send_sem.at[target, h], recv_sem=recv_sem.at[target, h],
            device_id=at(DIRS[direction], core), device_id_type=MESH)

    def share(slot, h, on):
        return pltpu.make_async_remote_copy(
            src_ref=chunk_of(slot, h, on), dst_ref=chunk_of(slot, h, on),
            send_sem=give_sem.at[slot, h], recv_sem=take_sem.at[slot, h],
            device_id=at((0, 0, 0), other), device_id_type=MESH)

    load_ids.wait()
    labels[0, core] = ids[...].astype(jnp.float32)
    load.wait()
    for h in range(chunks):
        e = emb[pl.ds(h * part, part)]
        squares = jnp.sum(e * e, axis=1, keepdims=True)
        buf[0, core, pl.ds(h * part, part)] = (e * lax.rsqrt(squares + 1e-06)).astype(jnp.bfloat16)

    def clear(slot, carry):
        row_best[slot] = jnp.full(row_best.shape[1:], FILL, jnp.float32)
        column_best[slot] = jnp.full(column_best.shape[1:], FILL, jnp.float32)
        return carry

    lax.fori_loop(0, SLOTS, clear, 0)
    pl.semaphore_wait(barrier, len(friends))

    for which in (0, 1):
        @pl.when(core == which)
        def _(which=which):
            for move in FIRST_SENDS[which]:
                relay(*move).start()

    for h in range(chunks):
        share(0, h, core).start()

    def tell(slot, on, flip):
        return pltpu.make_async_remote_copy(
            src_ref=labels.at[0, core], dst_ref=labels.at[slot, core],
            send_sem=label_send.at[slot, flip], recv_sem=label_recv.at[1 if slot else 0],
            device_id=at(OFFSETS[slot], on), device_id_type=MESH)

    tell(0, other, 1).start()
    for slot in range(1, SLOTS):
        tell(slot, core, 0).start()
        tell(slot, other, 1).start()

    pltpu.make_async_copy(labels.at[0, other], labels.at[0, other], label_recv.at[0]).wait()
    rest = labels.at[pl.ds(1, SLOTS - 1)]
    pltpu.make_async_copy(rest, rest, label_recv.at[1]).wait()

    def spread(slot):
        for unit in (0, 1):
            line = jnp.broadcast_to(labels[slot, unit], (128, rows))
            label_rows[slot, pl.ds(unit * rows, rows)] = line.T

    def tile(i, j, own=False):
        sims = lax.dot_general(buf[i].reshape(2 * rows, width), buf[j, core], (((1,), (1,)), ((), ())),
                               preferred_element_type=jnp.float32)
        names = label_rows[i]
        best = row_best[i]
        if own:
            row_at = lax.broadcasted_iota(jnp.int32, (2 * rows, 128), 0) - core * rows
            column_at = lax.broadcasted_iota(jnp.int32, (2 * rows, 128), 1)
        for k in range(rows // 128):
            lanes = slice(k * 128, (k + 1) * 128)
            keep = names == labels[j, core, :, lanes]
            if own:
                keep = keep & (row_at != column_at + k * 128)
            scores = jnp.where(keep, sims[:, lanes], FILL)
            best = jnp.maximum(best, scores)
            column_best[j, :, lanes] = jnp.maximum(
                column_best[j, :, lanes], jnp.max(scores.reshape(2 * rows // 8, 8, 128), axis=0))
        row_best[i] = best

    def answer(slot, unit):
        x, y, z = (SIDE - digit(jnp.int32(packed([o[k] for o in OFFSETS], 2)), slot, 2) for k in range(3))
        x, y, z = lax.rem(gx + x, SIDE), lax.rem(gy + y, SIDE), lax.rem(gz + z, SIDE)
        return pltpu.make_async_remote_copy(
            src_ref=outgoing.at[slot, unit], dst_ref=incoming.at[slot, core],
            send_sem=result_send.at[slot, unit], recv_sem=result_recv.at[1],
            device_id=(x, (z * SIDE + y) * 2 + unit), device_id_type=MESH)

    def answer_chip():
        return pltpu.make_async_remote_copy(
            src_ref=outgoing.at[0, other], dst_ref=incoming.at[0, core],
            send_sem=result_send.at[0, 0], recv_sem=result_recv.at[0],
            device_id=at((0, 0, 0), other), device_id_type=MESH)

    def arrived(slot, h):
        pltpu.make_async_copy(chunk_of(slot, h, core), chunk_of(slot, h, core), recv_sem.at[slot, h]).wait()
        share(slot, h, core).start()

    def sent(slot, h):
        relay(0, slot, h, 0).wait_send()

    def taken(slot):
        for h in range(chunks):
            pltpu.make_async_copy(
                chunk_of(slot, h, other), chunk_of(slot, h, other), take_sem.at[slot, h]).wait()

    def finish(slot):
        by_row = jnp.max(row_best[slot].T, axis=0, keepdims=True)
        by_column = jnp.max(column_best[slot], axis=0, keepdims=True)
        for unit in (0, 1):
            mine = by_row[:, unit * rows:(unit + 1) * rows]
            outgoing[slot, unit] = jnp.where(core == unit, jnp.maximum(mine, by_column), mine)

        @pl.when(slot > 0)
        def _():
            answer(slot, 0).start()
            answer(slot, 1).start()

        @pl.when(slot == 0)
        def _():
            incoming[0, core] = outgoing[0, core]
            answer_chip().start()

    def moves(n):
        for which in (0, 1):
            todo = STEPS[n][which][0]
            if todo:
                @pl.when(core == which)
                def _(todo=todo):
                    for op in todo:
                        if op[0] == "a":
                            arrived(*op[1:])
                        else:
                            if len(op) > 5:
                                sent(*op[5:])
                            relay(*op[1:5]).start()

    def chosen(place, n):
        return jnp.where(core == 0, lookup(column(0, place), n), lookup(column(1, place), n))

    taken(0)
    spread(0)
    tile(0, 0, own=True)

    def step(n, carry):
        for g in range(0, len(STEPS), 6):
            @pl.when(lax.div(n, 6) == g // 6)
            def _(g=g):
                for k in range(max(g, 1), min(g + 6, len(STEPS))):
                    @pl.when(n == k)
                    def _(k=k):
                        moves(k)
        opened, ended = chosen(1, n), chosen(2, n)

        @pl.when(opened != NONE)
        def _():
            spread(opened)
            taken(opened)

        @pl.when(ended != NONE)
        def _():
            finish(ended)

        tile(chosen(3, n), chosen(4, n))
        return carry

    lax.fori_loop(1, len(STEPS), step, 0)
    left = max(len(t[1]) for t in TAIL)

    def last(n, carry):
        ends = [(list(t[1]) + [NONE] * left)[:left] for t in TAIL]
        ended = jnp.where(core == 0, lookup(ends[0], n), lookup(ends[1], n))

        @pl.when(ended != NONE)
        def _():
            finish(ended)
        return carry

    lax.fori_loop(0, left, last, 0)

    pltpu.make_async_copy(incoming.at[0, other], incoming.at[0, other], result_recv.at[0]).wait()
    rest = incoming.at[pl.ds(1, SLOTS - 1)]
    pltpu.make_async_copy(rest, rest, result_recv.at[1]).wait()
    out_ref[...] = jnp.max(incoming[...].reshape(2 * SLOTS, 1, rows), axis=0)

    for which in (0, 1):
        @pl.when(core == which)
        def _(which=which):
            for slot in range(SLOTS):
                if slot not in column(which, 1):
                    taken(slot)
            for move in LAST_SENDS[which]:
                sent(*move)
    for slot in range(SLOTS):
        for h in range(chunks):
            share(slot, h, core).wait_send()
        if slot:
            tell(slot, core, 0).wait_send()
            answer(slot, 0).wait_send()
            answer(slot, 1).wait_send()
        else:
            answer_chip().wait_send()
        tell(slot, other, 1).wait_send()


def body(embeddings, cluster_ids):
    rows, width = embeddings.shape
    chunks = 1 + max(h for sends in LAST_SENDS for _, h in sends)
    copies = pltpu.SemaphoreType.DMA((SLOTS, chunks))
    pairs = pltpu.SemaphoreType.DMA((SLOTS, 2))
    best = pl.pallas_call(
        functools.partial(kernel, chunks),
        out_shape=jax.ShapeDtypeStruct((1, rows), jnp.float32),
        in_specs=[pl.BlockSpec(memory_space=pl.ANY), pl.BlockSpec(memory_space=pl.ANY)],
        out_specs=pl.BlockSpec(memory_space=pltpu.VMEM),
        scratch_shapes=[
            pltpu.VMEM((rows, width), jnp.float32),
            pltpu.VMEM((1, rows), jnp.int32),
            pltpu.VMEM((SLOTS, 2, rows, width), jnp.bfloat16),
            pltpu.VMEM((SLOTS, 2, 1, rows), jnp.float32),
            pltpu.VMEM((SLOTS, 2 * rows, 128), jnp.float32),
            pltpu.VMEM((SLOTS, 2 * rows, 128), jnp.float32),
            pltpu.VMEM((SLOTS, 8, rows), jnp.float32),
            pltpu.VMEM((SLOTS, 2, 1, rows), jnp.float32),
            pltpu.VMEM((SLOTS, 2, 1, rows), jnp.float32),
            pltpu.SemaphoreType.DMA((2,)),
            copies, copies, copies, copies,
            pairs, pltpu.SemaphoreType.DMA((2,)),
            pairs, pltpu.SemaphoreType.DMA((2,)),
        ],
        compiler_params=pltpu.CompilerParams(
            collective_id=0, has_side_effects=True, vmem_limit_bytes=VMEM_BYTES),
    )(embeddings, cluster_ids.reshape(1, rows))
    return best.reshape(rows)


def solution(mesh):
    return jax.shard_map(
        body,
        mesh=mesh,
        in_specs=(P(("grp", "mem"), None), P(("grp", "mem"), None)),
        out_specs=P(("grp", "mem")),
        check_vma=False,
    )
```

```python
import functools

import jax
import jax.numpy as jnp
from jax import lax
from jax.experimental import pallas as pl
from jax.experimental.pallas import tpu as pltpu
from jax.sharding import PartitionSpec as P

FILL = -4.0
MESH = pl.DeviceIdType.MESH
SIDE = 4
VMEM_BYTES = 64 * 1024 * 1024 - 512 * 1024
DIRS = ((1, 0, 0), (3, 0, 0), (0, 1, 0), (0, 3, 0), (0, 0, 1), (0, 0, 3))

OFFSETS = (
    (0, 0, 0),
    (0, 0, 2),
    (2, 0, 2),
    (0, 0, 3),
    (3, 0, 0),
    (0, 1, 0),
    (1, 1, 0),
    (0, 2, 0),
    (1, 2, 0),
    (0, 3, 0),
    (2, 0, 1),
    (3, 0, 1),
)

FIRST_SENDS = (
    ((0, 4, 0, 1), (0, 9, 0, 3), (0, 3, 0, 5)),
    ((0, 5, 1, 2),),
)

LAST_SENDS = (
    ((1, 1), (2, 1), (7, 1), (8, 0), (8, 1), (10, 1)),
    ((1, 1), (2, 1), (8, 0), (8, 1), (9, 1), (10, 1)),
)

STEPS = (
    (((), 0, None, 0, 0),
     ((), 0, None, 0, 0)),
    (((('a', 3, 0), ('a', 4, 0), ('a', 9, 0), ('s', 4, 11, 0, 4), ('s', 0, 4, 1, 1, 4, 0), ('s', 0, 5, 1, 2), ('s', 9, 7, 0, 3, 9, 0), ('s', 0, 3, 1, 5, 3, 0), ('a', 11, 0), ('s', 0, 5, 0, 2, 5, 1), ('s', 0, 9, 1, 3, 7, 0), ('a', 3, 1), ('a', 4, 1), ('a', 5, 1), ('a', 7, 0)), None, None, 0, 3),
     ((('s', 0, 4, 0, 1), ('s', 0, 5, 0, 2, 5, 1), ('s', 0, 9, 0, 3), ('s', 0, 3, 0, 5), ('a', 5, 1), ('s', 5, 6, 1, 0), ('a', 3, 0), ('a', 4, 0), ('a', 5, 0), ('a', 9, 0)), None, None, 0, 5)),
    (((('s', 5, 6, 1, 0), ('s', 4, 11, 1, 4, 11, 0)), None, None, 0, 4),
     ((('s', 5, 6, 0, 0, 6, 1), ('s', 4, 11, 0, 4), ('a', 6, 1), ('s', 0, 4, 1, 1, 4, 0), ('s', 0, 3, 1, 5, 3, 0), ('a', 6, 0), ('a', 11, 0)), None, None, 0, 6)),
    (((('s', 11, 10, 0, 1, 4, 1), ('s', 3, 1, 0, 5, 3, 1), ('a', 5, 0), ('a', 9, 1)), None, None, 0, 5),
     ((('s', 5, 7, 1, 2, 5, 0), ('s', 9, 7, 0, 3, 9, 0), ('a', 3, 1), ('a', 4, 1)), None, None, 0, 3)),
    (((('s', 5, 6, 0, 0, 6, 1),), 5, None, 5, 3),
     ((('s', 4, 11, 1, 4, 11, 0),), None, None, 0, 4)),
    (((('a', 6, 1), ('a', 11, 1)), None, None, 5, 9),
     ((), 3, None, 3, 6)),
    (((('s', 9, 7, 1, 3, 9, 1),), 3, None, 3, 9),
     ((('s', 11, 10, 0, 1, 4, 1), ('s', 6, 8, 0, 2, 7, 1), ('s', 3, 1, 0, 5, 3, 1)), 4, None, 4, 3)),
    (((('a', 1, 0), ('a', 10, 0), ('s', 7, 8, 0, 0, 6, 0), ('s', 10, 2, 0, 4, 11, 1)), 4, None, 4, 3),
     ((('a', 7, 0), ('a', 7, 1)), None, None, 4, 6)),
    (((), None, None, 4, 5),
     ((), 5, None, 5, 3)),
    (((('a', 6, 0),), None, None, 3, 11),
     ((('a', 11, 1),), None, None, 0, 7)),
    (((('s', 11, 10, 1, 1, 10, 0), ('s', 6, 8, 1, 2, 5, 0), ('s', 3, 1, 1, 5, 1, 0)), None, None, 5, 11),
     ((('s', 0, 9, 1, 3, 7, 0),), None, None, 3, 7)),
    (((), None, None, 3, 6),
     ((), None, None, 4, 7)),
    (((('a', 7, 1),), None, None, 4, 6),
     ((('a', 1, 0), ('a', 8, 0), ('a', 10, 0), ('s', 7, 8, 1, 0, 6, 0), ('s', 10, 2, 0, 4, 11, 1)), None, None, 3, 11)),
    (((('a', 2, 0), ('a', 8, 0)), 11, None, 11, 6),
     ((), None, None, 5, 11)),
    (((), None, None, 11, 9),
     ((('s', 11, 10, 1, 1, 10, 0), ('s', 3, 1, 1, 5, 1, 0)), 11, None, 11, 6)),
    (((), None, None, 3, 7),
     ((), None, None, 11, 7)),
    (((('a', 1, 1), ('a', 8, 1), ('a', 10, 1), ('s', 10, 2, 1, 4, 2, 0)), None, None, 4, 7),
     ((('a', 9, 1),), 6, None, 6, 7)),
    (((), 6, None, 6, 7),
     ((('a', 2, 0), ('a', 8, 1)), None, None, 3, 9)),
    (((), None, None, 11, 7),
     ((), None, None, 11, 9)),
    (((), None, None, 0, 1),
     ((), None, None, 3, 8)),
    (((), None, None, 0, 10),
     ((('a', 1, 1), ('a', 10, 1), ('s', 10, 2, 1, 4, 2, 0)), None, None, 4, 8)),
    (((('a', 2, 1),), None, 0, 3, 8),
     ((), None, 4, 11, 8)),
    (((), None, None, 3, 10),
     ((), None, None, 0, 1)),
    (((), None, 3, 4, 8),
     ((), None, None, 0, 10)),
    (((), None, 4, 5, 1),
     ((), None, 0, 3, 10)),
    (((), None, None, 6, 1),
     ((('a', 2, 1),), None, 3, 5, 1)),
    (((), None, None, 6, 10),
     ((), None, None, 6, 1)),
    (((), 7, None, 7, 1),
     ((), None, None, 6, 10)),
    (((), None, None, 11, 1),
     ((), 7, None, 7, 1)),
    (((), None, None, 11, 8),
     ((), 8, None, 8, 1)),
    (((), 9, 11, 9, 10),
     ((), 9, 8, 9, 10)),
    (((), 8, 9, 8, 1),
     ((), None, 9, 11, 1)),
    (((), 1, 10, 1, 2),
     ((), 1, 10, 1, 2)),
    (((), None, 8, 5, 2),
     ((), None, 11, 5, 2)),
    (((), None, 1, 6, 2),
     ((), None, 1, 6, 2)),
    (((), None, 5, 7, 2),
     ((), None, 5, 7, 2)),
)

TAIL = (
    ((), (6, 7, 2)),
    ((), (6, 7, 2)),
)


SLOTS = len(OFFSETS)


def greeted():
    both = set()
    for x, y, z in OFFSETS:
        both.add((x, y, z))
        both.add(((-x) % SIDE, (-y) % SIDE, (-z) % SIDE))
    near = [(d, 0) for d in DIRS if d not in both]
    far = [(d, k) for d in sorted(both) for k in (0, 1) if any(d) or k]
    return near + far


def packed(values, bits):
    return sum(v << (bits * n) for n, v in enumerate(values))


def digit(word, n, bits):
    return lax.rem(lax.shift_right_logical(word, bits * n), 1 << bits)


def lookup(values, n):
    words = [packed(values[k:k + 7], 4) for k in range(0, len(values), 7)]
    word = jnp.int32(words[0])
    for k, w in enumerate(words[1:], 1):
        word = jnp.where(n >= 7 * k, jnp.int32(w), word)
    return digit(word, lax.rem(n, 7), 4)


NONE = 15


def column(which, place):
    return [NONE if pair[which][place] is None else pair[which][place] for pair in STEPS]


def place():
    gx = lax.axis_index("grp")
    mem = lax.axis_index("mem")
    core = lax.rem(mem, 2)
    other = 1 - core
    gy = lax.rem(mem // 2, SIDE)
    gz = mem // (2 * SIDE)
    xs = [lax.rem(gx + k, SIDE) for k in range(SIDE)]
    ys = [lax.rem(gy + k, SIDE) for k in range(SIDE)]
    zs = [lax.rem(gz + k, SIDE) for k in range(SIDE)]

    def at(offset, on):
        x, y, z = (k % SIDE for k in offset)
        return (xs[x], (zs[z] * SIDE + ys[y]) * 2 + on)

    return core, other, gx, gy, gz, at


def gather(chunks, emb_ref, lab_ref, rows_ref, names_ref, emb, ids, buf, labels, load_sem, send_sem, recv_sem,
           give_sem, take_sem, label_send, label_recv, own_out, other_out):
    rows, width = emb.shape
    part = rows // chunks
    load = pltpu.make_async_copy(emb_ref, emb, load_sem.at[0])
    load.start()
    load_ids = pltpu.make_async_copy(lab_ref, ids, load_sem.at[1])
    load_ids.start()
    core, other, gx, gy, gz, at = place()
    barrier = pltpu.get_barrier_semaphore()
    friends = greeted()
    for offset, flip in friends:
        pl.semaphore_signal(barrier, inc=1, device_id=at(offset, other if flip else core), device_id_type=MESH)

    def chunk_of(slot, h, on):
        return buf.at[slot, on, pl.ds(h * part, part)]

    def relay(source, target, h, direction):
        return pltpu.make_async_remote_copy(
            src_ref=chunk_of(source, h, core), dst_ref=chunk_of(target, h, core),
            send_sem=send_sem.at[target, h], recv_sem=recv_sem.at[target, h],
            device_id=at(DIRS[direction], core), device_id_type=MESH)

    def share(slot, h, on):
        return pltpu.make_async_remote_copy(
            src_ref=chunk_of(slot, h, on), dst_ref=chunk_of(slot, h, on),
            send_sem=give_sem.at[slot, h], recv_sem=take_sem.at[slot, h],
            device_id=at((0, 0, 0), other), device_id_type=MESH)

    load_ids.wait()
    labels[0, core] = ids[...].astype(jnp.float32)
    load.wait()
    for h in range(chunks):
        e = emb[pl.ds(h * part, part)]
        squares = jnp.sum(e * e, axis=1, keepdims=True)
        buf[0, core, pl.ds(h * part, part)] = (e * lax.rsqrt(squares + 1e-06)).astype(jnp.bfloat16)

    pl.semaphore_wait(barrier, len(friends))

    for which in (0, 1):
        @pl.when(core == which)
        def _(which=which):
            for move in FIRST_SENDS[which]:
                relay(*move).start()

    for h in range(chunks):
        share(0, h, core).start()

    def tell(slot, on, flip):
        return pltpu.make_async_remote_copy(
            src_ref=labels.at[0, core], dst_ref=labels.at[slot, core],
            send_sem=label_send.at[slot, flip], recv_sem=label_recv.at[1 if slot else 0],
            device_id=at(OFFSETS[slot], on), device_id_type=MESH)

    tell(0, other, 1).start()
    for slot in range(1, SLOTS):
        tell(slot, core, 0).start()
        tell(slot, other, 1).start()

    def write_out(slot, h, on, sem):
        return pltpu.make_async_copy(
            chunk_of(slot, h, on), rows_ref.at[slot, on, pl.ds(h * part, part)], sem.at[slot, h])

    for h in range(chunks):
        write_out(0, h, core, own_out).start()

    pltpu.make_async_copy(labels.at[0, other], labels.at[0, other], label_recv.at[0]).wait()
    rest = labels.at[pl.ds(1, SLOTS - 1)]
    pltpu.make_async_copy(rest, rest, label_recv.at[1]).wait()

    def arrived(slot, h):
        pltpu.make_async_copy(chunk_of(slot, h, core), chunk_of(slot, h, core), recv_sem.at[slot, h]).wait()
        share(slot, h, core).start()
        write_out(slot, h, core, own_out).start()

    def sent(slot, h):
        relay(0, slot, h, 0).wait_send()

    def taken(slot):
        for h in range(chunks):
            pltpu.make_async_copy(
                chunk_of(slot, h, other), chunk_of(slot, h, other), take_sem.at[slot, h]).wait()
            write_out(slot, h, other, other_out).start()

    labels_out = pltpu.make_async_copy(labels, names_ref, load_sem.at[0])
    labels_out.start()
    for n in range(len(STEPS)):
        for which in (0, 1):
            todo = STEPS[n][which][0]
            first = [STEPS[n][which][1]] if STEPS[n][which][1] is not None else []
            if todo or first:
                @pl.when(core == which)
                def _(todo=todo, first=first):
                    for op in todo:
                        if op[0] == "a":
                            arrived(*op[1:])
                        else:
                            if len(op) > 5:
                                sent(*op[5:])
                            relay(*op[1:5]).start()
                    for slot in first:
                        taken(slot)

    for which in (0, 1):
        @pl.when(core == which)
        def _(which=which):
            for slot in range(SLOTS):
                if slot not in column(which, 1):
                    taken(slot)
            for move in LAST_SENDS[which]:
                sent(*move)
    for slot in range(SLOTS):
        for h in range(chunks):
            share(slot, h, core).wait_send()
            write_out(slot, h, core, own_out).wait()
            write_out(slot, h, other, other_out).wait()
        if slot:
            tell(slot, core, 0).wait_send()
        tell(slot, other, 1).wait_send()
    labels_out.wait()


def compare(rows_ref, names_ref, out_ref, buf, labels, label_rows, row_best, column_best, load_sem, names_sem):
    rows, width = buf.shape[2:]
    core = lax.rem(lax.axis_index("mem"), 2)
    names_in = pltpu.make_async_copy(names_ref, labels, names_sem)
    names_in.start()

    def bring(slot):
        return pltpu.make_async_copy(rows_ref.at[slot], buf.at[slot], load_sem.at[slot])

    order = []
    for pair in STEPS:
        for slot in pair[0][3:]:
            if slot not in order:
                order.append(slot)
    for slot in order:
        bring(slot).start()

    def clear(slot, carry):
        row_best[slot] = jnp.full(row_best.shape[1:], FILL, jnp.float32)
        column_best[slot] = jnp.full(column_best.shape[1:], FILL, jnp.float32)
        return carry

    lax.fori_loop(0, SLOTS, clear, 0)
    names_in.wait()

    def spread(slot, carry):
        for unit in (0, 1):
            line = jnp.broadcast_to(labels[slot, unit], (128, rows))
            label_rows[slot, pl.ds(unit * rows, rows)] = line.T
        return carry

    lax.fori_loop(0, SLOTS, spread, 0)

    def tile(i, j, own=False):
        sims = lax.dot_general(buf[i].reshape(2 * rows, width), buf[j, core], (((1,), (1,)), ((), ())),
                               preferred_element_type=jnp.float32)
        names = label_rows[i]
        best = row_best[i]
        if own:
            row_at = lax.broadcasted_iota(jnp.int32, (2 * rows, 128), 0) - core * rows
            column_at = lax.broadcasted_iota(jnp.int32, (2 * rows, 128), 1)
        for k in range(rows // 128):
            lanes = slice(k * 128, (k + 1) * 128)
            keep = names == labels[j, core, :, lanes]
            if own:
                keep = keep & (row_at != column_at + k * 128)
            scores = jnp.where(keep, sims[:, lanes], FILL)
            best = jnp.maximum(best, scores)
            column_best[j, :, lanes] = jnp.maximum(
                column_best[j, :, lanes], jnp.max(scores.reshape(2 * rows // 8, 8, 128), axis=0))
        row_best[i] = best

    seen, fresh = [0], [[NONE], [NONE]]
    for pair in STEPS[1:]:
        for k in (0, 1):
            slot = pair[0][3 + k]
            fresh[k].append(NONE if slot in seen else slot)
            seen.append(slot)
    bring(0).wait()
    tile(0, 0, own=True)

    def step(n, carry):
        for k in (0, 1):
            slot = lookup(fresh[k], n)

            @pl.when(slot != NONE)
            def _(slot=slot):
                bring(slot).wait()
        tile(lookup(column(0, 3), n), lookup(column(0, 4), n))
        return carry

    lax.fori_loop(1, len(STEPS), step, 0)

    def finish(slot, carry):
        by_row = jnp.max(row_best[slot].T, axis=0, keepdims=True)
        by_column = jnp.max(column_best[slot], axis=0, keepdims=True)
        for unit in (0, 1):
            mine = by_row[:, unit * rows:(unit + 1) * rows]
            out_ref[slot, unit] = jnp.where(core == unit, jnp.maximum(mine, by_column), mine)
        return carry

    lax.fori_loop(0, SLOTS, finish, 0)


def reply(found_ref, out_ref, incoming, result_send, result_recv):
    rows = out_ref.shape[1]
    core, other, gx, gy, gz, at = place()
    barrier = pltpu.get_barrier_semaphore()
    friends = greeted()
    for offset, flip in friends:
        pl.semaphore_signal(barrier, inc=1, device_id=at(offset, other if flip else core), device_id_type=MESH)
    incoming[0, core] = found_ref[0, core]
    pl.semaphore_wait(barrier, len(friends))

    def answer(slot, unit):
        return pltpu.make_async_remote_copy(
            src_ref=found_ref.at[slot, unit], dst_ref=incoming.at[slot, core],
            send_sem=result_send.at[slot, unit], recv_sem=result_recv.at[1 if slot else 0],
            device_id=at([-k for k in OFFSETS[slot]], unit), device_id_type=MESH)

    for slot in range(1, SLOTS):
        answer(slot, 0).start()
        answer(slot, 1).start()
    answer(0, other).start()
    pltpu.make_async_copy(incoming.at[0, other], incoming.at[0, other], result_recv.at[0]).wait()
    rest = incoming.at[pl.ds(1, SLOTS - 1)]
    pltpu.make_async_copy(rest, rest, result_recv.at[1]).wait()
    out_ref[...] = jnp.max(incoming[...].reshape(2 * SLOTS, 1, rows), axis=0)
    for slot in range(1, SLOTS):
        answer(slot, 0).wait_send()
        answer(slot, 1).wait_send()
    answer(0, other).wait_send()


def body(embeddings, cluster_ids):
    rows, width = embeddings.shape
    chunks = 1 + max(h for sends in LAST_SENDS for _, h in sends)
    copies = pltpu.SemaphoreType.DMA((SLOTS, chunks))
    pairs = pltpu.SemaphoreType.DMA((SLOTS, 2))
    anywhere = pl.BlockSpec(memory_space=pl.ANY)
    near = pl.BlockSpec(memory_space=pltpu.VMEM)
    units = jax.ShapeDtypeStruct((SLOTS, 2, rows, width), jnp.bfloat16)
    lines = jax.ShapeDtypeStruct((SLOTS, 2, 1, rows), jnp.float32)
    held, names = pl.pallas_call(
        functools.partial(gather, chunks),
        out_shape=(units, lines),
        in_specs=[anywhere, anywhere],
        out_specs=(anywhere, anywhere),
        scratch_shapes=[
            pltpu.VMEM((rows, width), jnp.float32),
            pltpu.VMEM((1, rows), jnp.int32),
            pltpu.VMEM(units.shape, units.dtype),
            pltpu.VMEM(lines.shape, lines.dtype),
            pltpu.SemaphoreType.DMA((2,)),
            copies, copies, copies, copies,
            pairs, pltpu.SemaphoreType.DMA((2,)),
            copies, copies,
        ],
        compiler_params=pltpu.CompilerParams(
            collective_id=0, has_side_effects=True, vmem_limit_bytes=VMEM_BYTES),
    )(embeddings, cluster_ids.reshape(1, rows))
    found = pl.pallas_call(
        compare,
        out_shape=lines,
        in_specs=[anywhere, anywhere],
        out_specs=near,
        scratch_shapes=[
            pltpu.VMEM(units.shape, units.dtype),
            pltpu.VMEM(lines.shape, lines.dtype),
            pltpu.VMEM((SLOTS, 2 * rows, 128), jnp.float32),
            pltpu.VMEM((SLOTS, 2 * rows, 128), jnp.float32),
            pltpu.VMEM((SLOTS, 8, rows), jnp.float32),
            pltpu.SemaphoreType.DMA((SLOTS,)),
            pltpu.SemaphoreType.DMA,
        ],
        compiler_params=pltpu.CompilerParams(vmem_limit_bytes=VMEM_BYTES),
    )(held, names)
    best = pl.pallas_call(
        reply,
        out_shape=jax.ShapeDtypeStruct((1, rows), jnp.float32),
        in_specs=[near],
        out_specs=near,
        scratch_shapes=[
            pltpu.VMEM(lines.shape, lines.dtype),
            pairs, pltpu.SemaphoreType.DMA((2,)),
        ],
        compiler_params=pltpu.CompilerParams(
            collective_id=1, has_side_effects=True, vmem_limit_bytes=VMEM_BYTES),
    )(found)
    return best.reshape(rows)


def solution(mesh):
    return jax.shard_map(
        body,
        mesh=mesh,
        in_specs=(P(("grp", "mem"), None), P(("grp", "mem"), None)),
        out_specs=P(("grp", "mem")),
        check_vma=False,
    )
```

```python
import functools

import jax
import jax.numpy as jnp
from jax import lax
from jax.experimental import pallas as pl
from jax.experimental.pallas import tpu as pltpu
from jax.sharding import PartitionSpec as P

FILL = -4.0
MESH = pl.DeviceIdType.MESH
SIDE = 4
VMEM_BYTES = 64 * 1024 * 1024 - 512 * 1024
DIRS = ((1, 0, 0), (3, 0, 0), (0, 1, 0), (0, 3, 0), (0, 0, 1), (0, 0, 3))

OFFSETS = (
    (0, 0, 0),
    (0, 3, 0),
    (0, 1, 0),
    (1, 1, 0),
    (0, 0, 1),
    (0, 1, 1),
    (0, 2, 1),
    (3, 3, 3),
    (0, 0, 3),
    (2, 0, 3),
    (3, 0, 3),
    (1, 1, 3),
)

SHARED = ((1, 7, 8, 9, 11), (1, 7, 8, 9, 11))

FIRST_SENDS = (
    ((0, 1, 0, 3), (0, 4, 0, 4), (0, 8, 0, 5)),
    ((0, 2, 0, 2),),
)

LAST_SENDS = (
    ((3, 0), (4, 1), (6, 1), (7, 1), (9, 1), (11, 0)),
    ((3, 1), (4, 1), (6, 1), (7, 1), (9, 1), (11, 1)),
)

STEPS = (
    (((('s', 0, 2, 1, 2), ('a', 1, 0), ('a', 4, 0), ('a', 8, 0), ('s', 8, 10, 0, 1), ('s', 0, 1, 1, 3, 1, 0), ('s', 0, 8, 1, 5, 8, 0), ('a', 2, 1), ('s', 2, 3, 1, 0), ('a', 10, 0), ('s', 0, 2, 0, 2, 2, 1), ('s', 10, 7, 0, 3, 1, 1), ('s', 2, 5, 1, 4, 4, 0), ('a', 1, 1), ('a', 8, 1)), 1, 8, None, 1, 8, 0),
     ((('s', 0, 1, 0, 3), ('s', 0, 4, 0, 4), ('s', 0, 8, 0, 5), ('a', 2, 0), ('s', 2, 3, 0, 0), ('s', 0, 2, 1, 2, 2, 0), ('s', 2, 5, 0, 4, 4, 0), ('a', 1, 0), ('a', 4, 0), ('a', 8, 0), ('s', 8, 10, 0, 1), ('a', 3, 0), ('s', 0, 8, 1, 5, 8, 0), ('a', 2, 1), ('a', 5, 0), ('s', 2, 3, 1, 0, 3, 0), ('a', 10, 0), ('t', 0)), 2, None, None, 0, 2, 12)),
    (((('s', 8, 10, 1, 1, 10, 0), ('a', 3, 1), ('s', 4, 5, 0, 2, 2, 0), ('a', 2, 0), ('a', 5, 1), ('a', 7, 0)), 2, None, None, 8, 2, 1),
     ((('s', 10, 7, 0, 3, 1, 0), ('s', 2, 5, 1, 4, 5, 0), ('s', 3, 11, 0, 5, 8, 1), ('t', 2)), None, None, None, 0, 2, 14)),
    (((('s', 2, 3, 0, 0, 3, 1), ('t', 2)), None, None, None, 0, 2, 14),
     ((('a', 8, 1),), 8, None, None, 2, 8, 0)),
    (((('a', 10, 1), ('s', 10, 7, 1, 3, 7, 0), ('s', 0, 4, 1, 4, 5, 1), ('s', 3, 11, 1, 5, 8, 1)), None, None, None, 0, 1, 10),
     ((('s', 8, 10, 1, 1, 10, 0), ('a', 3, 1)), None, None, None, 0, 8, 3)),
    (((), 10, None, None, 8, 10, 2),
     ((('s', 5, 6, 0, 2, 2, 1),), 3, None, None, 8, 3, 2)),
    (((('a', 5, 0), ('s', 10, 9, 0, 1, 10, 1)), None, None, None, 1, 10, 5),
     ((), None, None, None, 8, 3, 12)),
    (((), 5, None, None, 10, 5, 8),
     ((('a', 5, 1), ('a', 7, 0), ('a', 11, 0)), None, None, None, 8, 3, 14)),
    (((('a', 3, 0), ('s', 5, 6, 0, 2, 5, 0), ('s', 3, 11, 0, 5, 11, 1)), None, None, None, 10, 5, 14),
     ((), None, None, None, 3, 8, 5)),
    (((), None, None, None, 0, 1, 3),
     ((('a', 10, 1),), None, None, None, 0, 3, 10)),
    (((('a', 4, 1), ('a', 7, 1), ('a', 11, 1)), None, None, None, 5, 10, 3),
     ((('s', 0, 1, 1, 3, 7, 0), ('s', 0, 4, 1, 4, 5, 1)), 5, 10, None, 5, 10, 12)),
    (((), None, None, None, 2, 5, 7),
     ((('a', 6, 0), ('s', 10, 9, 0, 1, 10, 1)), None, None, None, 5, 10, 14)),
    (((('a', 9, 0),), 3, 4, None, 3, 4, 14),
     ((('t', 1),), None, None, None, 2, 3, 13)),
    (((('s', 5, 6, 1, 2, 6, 0),), 7, None, None, 4, 7, 3),
     ((('s', 10, 7, 1, 3, 1, 1), ('s', 3, 11, 1, 5, 11, 0), ('a', 1, 1), ('a', 4, 1)), 1, None, None, 1, 0, 14)),
    (((('a', 6, 0), ('a', 11, 0), ('s', 10, 9, 1, 1, 9, 0)), None, None, None, 8, 10, 4),
     ((), None, None, 14, 2, 3, 1)),
    (((), None, None, None, 1, 7, 11),
     ((('a', 9, 0),), None, None, None, 2, 3, 4)),
    (((), 11, None, None, 7, 11, 14),
     ((('s', 5, 6, 1, 2, 6, 0),), None, None, None, 5, 1, 13)),
    (((), None, None, None, 10, 0, 11),
     ((('a', 7, 1), ('a', 11, 1), ('s', 10, 9, 1, 1, 9, 0)), None, None, None, 8, 10, 4)),
    (((('a', 6, 1), ('t', 0)), None, None, None, 0, 3, 12),
     ((), None, None, None, 10, 1, 5)),
    (((), None, None, None, 0, 3, 12),
     ((('t', 4),), None, None, None, 0, 2, 16)),
    (((('a', 9, 1),), None, None, None, 5, 10, 12),
     ((), 4, None, None, 4, 5, 16)),
    (((), None, None, None, 3, 7, 6),
     ((('a', 6, 1),), None, None, None, 10, 0, 16)),
    (((), None, None, None, 0, 1, 9),
     ((), None, None, 16, 2, 3, 7)),
    (((('t', 4),), None, None, None, 0, 2, 16),
     ((('a', 9, 1),), 11, None, None, 4, 11, 13)),
    (((('t', 1),), None, None, None, 1, 2, 13),
     ((), None, None, 13, 5, 11, 7)),
    (((), None, None, 1, 3, 5, 13),
     ((), None, None, None, 10, 0, 11)),
    (((), None, None, None, 4, 5, 9),
     ((), None, None, None, 10, 11, 1)),
    (((), 6, None, 4, 5, 6, 16),
     ((('t', 3),), None, None, 10, 0, 2, 15)),
    (((), 9, None, None, 6, 9, 13),
     ((), None, None, 2, 3, 4, 15)),
    (((), None, None, 13, 6, 9, 14),
     ((), 7, None, None, 3, 7, 6)),
    (((), None, None, 14, 7, 8, 9),
     ((), 6, None, 3, 5, 6, 15)),
    (((), None, None, 7, 8, 9, 6),
     ((), None, None, 15, 0, 1, 9)),
    (((), None, None, 8, 9, 10, 16),
     ((), None, None, 0, 4, 5, 9)),
    (((), None, None, 6, 11, 9, 12),
     ((), None, None, 1, 7, 8, 9)),
    (((('t', 3),), None, None, 10, 0, 2, 15),
     ((), 9, None, 4, 8, 9, 6)),
    (((), None, None, 16, 3, 5, 15),
     ((), None, None, 5, 11, 9, 12)),
)

TAIL = (
    (11, 9, 12, 0, 2, 3, 5, 15),
    (7, 8, 6, 11, 9, 12),
)


SLOTS = len(OFFSETS)
EXTRA = len(SHARED[0])
HELD = SLOTS + EXTRA
NONE = 31


def lookup(values, n, bits=5):
    each = 30 // bits
    words = [sum(v << (bits * k) for k, v in enumerate(values[s:s + each])) for s in range(0, len(values), each)]
    word = jnp.int32(words[0])
    for k, w in enumerate(words[1:], 1):
        word = jnp.where(n >= each * k, jnp.int32(w), word)
    return lax.rem(lax.shift_right_logical(word, bits * lax.rem(n, each)), 1 << bits)


def column(which, place):
    return [NONE if pair[which][place] is None else pair[which][place] for pair in STEPS]


def kernel(chunks, emb_ref, lab_ref, out_ref, emb, ids, buf, labels, label_rows, row_best, column_best, outgoing,
           incoming, load_sem, send_sem, recv_sem, give_sem, take_sem, label_send, label_recv, label_give,
           label_take, result_send, result_recv):
    rows, width = emb.shape
    part = rows // chunks
    load = pltpu.make_async_copy(emb_ref, emb, load_sem.at[0])
    load.start()
    load_ids = pltpu.make_async_copy(lab_ref, ids, load_sem.at[1])
    load_ids.start()
    gx = lax.axis_index("grp")
    mem = lax.axis_index("mem")
    core = lax.rem(mem, 2)
    other = 1 - core
    gy = lax.rem(mem // 2, SIDE)
    gz = mem // (2 * SIDE)

    def at(offset, on):
        x, y, z = (lax.rem(g + k, SIDE) for g, k in zip((gx, gy, gz), offset))
        return (x, (z * SIDE + y) * 2 + on)

    barrier = pltpu.get_barrier_semaphore()
    for direction in DIRS:
        pl.semaphore_signal(barrier, inc=1, device_id=at(direction, core), device_id_type=MESH)
    pl.semaphore_signal(barrier, inc=1, device_id=at((0, 0, 0), other), device_id_type=MESH)

    def chunk_of(slot, h):
        return buf.at[slot, pl.ds(h * part, part)]

    def relay(source, target, h, direction):
        return pltpu.make_async_remote_copy(
            src_ref=chunk_of(source, h), dst_ref=chunk_of(target, h),
            send_sem=send_sem.at[target, h], recv_sem=recv_sem.at[target, h],
            device_id=at(DIRS[direction], core), device_id_type=MESH)

    def relay_label(source, target, direction):
        return pltpu.make_async_remote_copy(
            src_ref=labels.at[source], dst_ref=labels.at[target],
            send_sem=label_send.at[target], recv_sem=label_recv.at[target],
            device_id=at(DIRS[direction], core), device_id_type=MESH)

    def send(source, target, h, direction):
        if h == 0:
            relay_label(source, target, direction).start()
        relay(source, target, h, direction).start()

    def share(slot, k, h):
        return pltpu.make_async_remote_copy(
            src_ref=chunk_of(slot, h), dst_ref=chunk_of(SLOTS + k, h),
            send_sem=give_sem.at[k, h], recv_sem=take_sem.at[k, h],
            device_id=at((0, 0, 0), other), device_id_type=MESH)

    def share_label(slot, k):
        return pltpu.make_async_remote_copy(
            src_ref=labels.at[slot], dst_ref=labels.at[SLOTS + k],
            send_sem=label_give.at[k], recv_sem=label_take.at[k],
            device_id=at((0, 0, 0), other), device_id_type=MESH)

    def give(which, slot, h):
        if slot in SHARED[1 - which]:
            k = SHARED[1 - which].index(slot)
            if h == 0:
                share_label(slot, k).start()
            share(slot, k, h).start()

    load_ids.wait()
    labels[0] = ids[...].astype(jnp.float32)
    load.wait()
    for h in range(chunks):
        e = emb[pl.ds(h * part, part)]
        squares = jnp.sum(e * e, axis=1, keepdims=True)
        buf[0, pl.ds(h * part, part)] = (e * lax.rsqrt(squares + 1e-06)).astype(jnp.bfloat16)
    pl.semaphore_wait(barrier, len(DIRS) + 1)

    for which in (0, 1):
        @pl.when(core == which)
        def _(which=which):
            for move in FIRST_SENDS[which]:
                send(*move)
            for h in range(chunks):
                give(which, 0, h)

    def clear(slot, carry):
        column_best[slot] = jnp.full(column_best.shape[1:], FILL, jnp.float32)

        @pl.when(slot < SLOTS)
        def _():
            row_best[slot] = jnp.full(row_best.shape[1:], FILL, jnp.float32)
        return carry

    lax.fori_loop(0, HELD, clear, 0)

    def spread(slot):
        label_rows[slot] = jnp.broadcast_to(labels[slot], (128, rows)).T

    def tile(left, right, own=False):
        sims = lax.dot_general(jnp.concatenate([buf[a] for a in left], axis=0), buf[right], (((1,), (1,)), ((), ())),
                               preferred_element_type=jnp.float32)
        names = labels[right]
        tops = [row_best[a] for a in left]
        for k in range(rows // 128):
            lanes = slice(k * 128, (k + 1) * 128)
            high = column_best[right, :, lanes]
            for n, a in enumerate(left):
                keep = label_rows[a] == names[:, lanes]
                if own:
                    keep = keep & (lax.broadcasted_iota(jnp.int32, (rows, 128), 0)
                                   != lax.broadcasted_iota(jnp.int32, (rows, 128), 1) + k * 128)
                scores = jnp.where(keep, sims[n * rows:(n + 1) * rows, lanes], FILL)
                tops[n] = jnp.maximum(tops[n], scores)
                high = jnp.maximum(high, jnp.max(scores.reshape(rows // 8, 8, 128), axis=0))
            column_best[right, :, lanes] = high
        for n, a in enumerate(left):
            row_best[a] = tops[n]

    def answer(slot):
        offsets = [[OFFSETS[s] for s in tuple(range(SLOTS)) + SHARED[w]] for w in (0, 1)]
        back = [SIDE - jnp.where(core == 0, *(lookup([o[k] for o in offsets[w]], slot, 2) for w in (0, 1)))
                for k in range(3)]
        return pltpu.make_async_remote_copy(
            src_ref=outgoing.at[slot], dst_ref=incoming.at[slot],
            send_sem=result_send.at[slot], recv_sem=result_recv,
            device_id=at(back, jnp.where(slot < SLOTS, core, other)), device_id_type=MESH)

    def finish(slot):
        by_column = jnp.max(column_best[slot], axis=0, keepdims=True)

        @pl.when(slot < SLOTS)
        def _():
            outgoing[slot] = jnp.maximum(by_column, jnp.max(row_best[slot].T, axis=0, keepdims=True))

        @pl.when(slot >= SLOTS)
        def _():
            outgoing[slot] = by_column

        @pl.when(slot > 0)
        def _():
            answer(slot).start()

        @pl.when(slot == 0)
        def _():
            incoming[0] = outgoing[0]

    def arrived(which, slot, h):
        pltpu.make_async_copy(chunk_of(slot, h), chunk_of(slot, h), recv_sem.at[slot, h]).wait()
        if h == 0:
            pltpu.make_async_copy(labels.at[slot], labels.at[slot], label_recv.at[slot]).wait()
        give(which, slot, h)

    def taken(k):
        for h in range(chunks):
            pltpu.make_async_copy(chunk_of(SLOTS + k, h), chunk_of(SLOTS + k, h), take_sem.at[k, h]).wait()
        pltpu.make_async_copy(labels.at[SLOTS + k], labels.at[SLOTS + k], label_take.at[k]).wait()

    def sent(slot, h):
        relay(0, slot, h, 0).wait_send()

    def moves(n):
        for which in (0, 1):
            todo = STEPS[n][which][0]
            if todo:
                @pl.when(core == which)
                def _(which=which, todo=todo):
                    for op in todo:
                        if op[0] == "a":
                            arrived(which, *op[1:])
                        elif op[0] == "t":
                            taken(op[1])
                        else:
                            if len(op) > 5:
                                sent(*op[5:])
                            send(*op[1:5])

    def chosen(place, n):
        return jnp.where(core == 0, lookup(column(0, place), n), lookup(column(1, place), n))

    spread(0)
    tile((0,), 0, own=True)

    def step(n, carry):
        for g in range(0, len(STEPS), 6):
            @pl.when(lax.div(n, 6) == g // 6)
            def _(g=g):
                for k in range(g, min(g + 6, len(STEPS))):
                    @pl.when(n == k)
                    def _(k=k):
                        moves(k)
        for place in (1, 2):
            opened = chosen(place, n)

            @pl.when(opened != NONE)
            def _(opened=opened):
                spread(opened)
        ended = chosen(3, n)

        @pl.when(ended != NONE)
        def _():
            finish(ended)

        tile((chosen(4, n), chosen(5, n)), chosen(6, n))
        return carry

    lax.fori_loop(0, len(STEPS), step, 0)
    left = max(len(t) for t in TAIL)

    def last(n, carry):
        ends = [(list(t) + [NONE] * left)[:left] for t in TAIL]
        ended = jnp.where(core == 0, lookup(ends[0], n), lookup(ends[1], n))

        @pl.when(ended != NONE)
        def _():
            finish(ended)
        return carry

    lax.fori_loop(0, left, last, 0)

    rest = incoming.at[pl.ds(1, HELD - 1)]
    pltpu.make_async_copy(rest, rest, result_recv).wait()
    out_ref[...] = jnp.max(incoming[...], axis=0)

    for which in (0, 1):
        @pl.when(core == which)
        def _(which=which):
            for move in LAST_SENDS[which]:
                sent(*move)
    for k in range(EXTRA):
        for h in range(chunks):
            share(0, k, h).wait_send()
        share_label(0, k).wait_send()
    for slot in range(1, SLOTS):
        relay_label(0, slot, 0).wait_send()
    for slot in range(1, HELD):
        answer(slot).wait_send()


def body(embeddings, cluster_ids):
    rows, width = embeddings.shape
    chunks = 1 + max(h for sends in LAST_SENDS for _, h in sends)
    dma = pltpu.SemaphoreType.DMA
    best = pl.pallas_call(
        functools.partial(kernel, chunks),
        out_shape=jax.ShapeDtypeStruct((1, rows), jnp.float32),
        in_specs=[pl.BlockSpec(memory_space=pl.ANY), pl.BlockSpec(memory_space=pl.ANY)],
        out_specs=pl.BlockSpec(memory_space=pltpu.VMEM),
        scratch_shapes=[
            pltpu.VMEM((rows, width), jnp.float32),
            pltpu.VMEM((1, rows), jnp.int32),
            pltpu.VMEM((HELD, rows, width), jnp.bfloat16),
            pltpu.VMEM((HELD, 1, rows), jnp.float32),
            pltpu.VMEM((SLOTS, rows, 128), jnp.float32),
            pltpu.VMEM((SLOTS, rows, 128), jnp.float32),
            pltpu.VMEM((HELD, 8, rows), jnp.float32),
            pltpu.VMEM((HELD, 1, rows), jnp.float32),
            pltpu.VMEM((HELD, 1, rows), jnp.float32),
            dma((2,)), dma((SLOTS, chunks)), dma((SLOTS, chunks)), dma((EXTRA, chunks)), dma((EXTRA, chunks)),
            dma((SLOTS,)), dma((SLOTS,)), dma((EXTRA,)), dma((EXTRA,)), dma((HELD,)), dma,
        ],
        compiler_params=pltpu.CompilerParams(
            collective_id=0, has_side_effects=True, vmem_limit_bytes=VMEM_BYTES),
    )(embeddings, cluster_ids.reshape(1, rows))
    return best.reshape(rows)


def solution(mesh):
    return jax.shard_map(
        body,
        mesh=mesh,
        in_specs=(P(("grp", "mem"), None), P(("grp", "mem"), None)),
        out_specs=P(("grp", "mem")),
        check_vma=False,
    )
```

```python
import functools

import jax
import jax.numpy as jnp
from jax import lax
from jax.experimental import pallas as pl
from jax.experimental.pallas import tpu as pltpu
from jax.sharding import PartitionSpec as P

FILL = -4.0
MESH = pl.DeviceIdType.MESH
SIDE = 4
VMEM_BYTES = 64 * 1024 * 1024 - 512 * 1024
DIRS = ((1, 0, 0), (3, 0, 0), (0, 1, 0), (0, 3, 0), (0, 0, 1), (0, 0, 3))

OFFSETS = (
    ((0, 0, 0), (1, 0, 0), (2, 0, 0), (0, 1, 0), (0, 2, 0), (0, 3, 0),
     (3, 0, 1), (0, 0, 1), (2, 0, 2), (3, 0, 2), (0, 1, 3), (0, 2, 3)),
    ((0, 0, 0), (1, 0, 3), (2, 0, 3), (0, 0, 3), (0, 1, 3), (0, 2, 3),
     (0, 3, 3), (3, 0, 0), (2, 0, 1), (3, 0, 1), (0, 1, 2), (0, 2, 2)),
)

SHARED = ((0, 1, 6, 7, 10, 11), (1, 2, 4, 5, 6, 10))

FIRST_SENDS = (
    ((0, 1, 0, 0), (0, 3, 0, 2), (0, 5, 1, 3), (0, 7, 0, 4)),
    ((0, 7, 0, 1), (0, 3, 0, 5)),
)

LAST_SENDS = (
    ((2, 1), (4, 0), (4, 1), (8, 1), (9, 1), (11, 1)),
    ((2, 1), (5, 1), (8, 1), (9, 1), (10, 1), (11, 1)),
)

STEPS = (
    (((('s', 0, 1, 1, 0, 1, 0), ('s', 0, 3, 1, 2, 3, 0), ('s', 0, 5, 0, 3, 5, 1), ('s', 0, 7, 1, 4, 7, 0), ('a', 1, 0), ('a', 3, 0), ('a', 5, 1), ('a', 7, 0), ('s', 7, 6, 0, 1), ('s', 3, 10, 0, 5), ('a', 1, 1), ('a', 3, 1), ('a', 5, 0), ('a', 7, 1)), 1, None, None, None, 0, 1, 7),
     ((('s', 0, 7, 1, 1, 7, 0), ('s', 0, 3, 1, 5, 3, 0), ('a', 3, 0), ('a', 7, 0), ('s', 3, 1, 0, 0), ('s', 3, 4, 0, 2), ('s', 3, 6, 0, 3), ('s', 7, 9, 0, 4), ('a', 3, 1), ('a', 7, 1)), 3, 7, None, None, 3, 7, 0)),
    (((('t', 0),), None, None, None, None, 0, 1, 12),
     ((('s', 3, 1, 1, 0, 1, 0), ('s', 3, 4, 1, 2, 4, 0), ('s', 7, 9, 1, 4, 9, 0), ('a', 1, 0), ('a', 4, 0), ('a', 6, 0), ('a', 9, 0), ('s', 9, 8, 0, 1, 7, 1), ('s', 3, 6, 1, 3, 6, 0), ('s', 4, 10, 0, 5, 3, 1), ('a', 1, 1), ('a', 4, 1), ('a', 9, 1)), 1, None, None, None, 0, 1, 4)),
    (((), 3, None, None, None, 1, 3, 0),
     ((), None, None, None, None, 1, 3, 9)),
    (((), 5, None, None, None, 3, 5, 1),
     ((), 4, None, None, None, 1, 4, 7)),
    (((), None, None, None, None, 3, 5, 12),
     ((('t', 3),), None, None, None, None, 3, 1, 15)),
    (((('s', 7, 6, 1, 1, 6, 0), ('s', 5, 4, 1, 3, 5, 0), ('s', 3, 10, 1, 5, 10, 0)), 7, None, None, None, 5, 7, 3),
     ((('t', 0),), 9, None, None, None, 4, 9, 12)),
    (((('t', 3),), None, None, None, None, 1, 3, 15),
     ((('s', 1, 2, 0, 0, 1, 1), ('s', 9, 8, 1, 1, 8, 0), ('s', 6, 5, 0, 3, 6, 1), ('s', 4, 10, 1, 5, 10, 0)), None, None, None, None, 4, 9, 15)),
    (((('a', 6, 0), ('a', 10, 0)), None, None, None, None, 5, 7, 15),
     ((), None, None, None, None, 7, 4, 3)),
    (((('s', 1, 2, 0, 0, 1, 1), ('s', 3, 4, 0, 2, 3, 1), ('s', 6, 9, 0, 4, 7, 1), ('a', 4, 1), ('a', 6, 1), ('a', 10, 1)), None, None, None, None, 1, 3, 6),
     ((('a', 6, 1), ('a', 8, 0), ('a', 10, 0), ('s', 10, 11, 0, 2, 4, 1), ('t', 4)), None, None, None, None, 3, 4, 16)),
    (((), None, None, None, None, 1, 5, 10),
     ((), None, None, None, None, 0, 1, 6)),
    (((), 6, None, None, None, 6, 7, 10),
     ((), None, None, None, None, 7, 9, 6)),
    (((), None, None, None, None, 7, 6, 5),
     ((), 6, None, None, None, 9, 6, 4)),
    (((), None, None, None, None, 7, 6, 12),
     ((('t', 5),), None, None, None, None, 9, 6, 17)),
    (((('s', 6, 9, 1, 4, 9, 0),), 10, None, None, None, 10, 0, 12),
     ((('s', 6, 5, 1, 3, 5, 0), ('t', 2)), None, None, None, None, 4, 9, 14)),
    (((('t', 1),), None, None, 12, None, 3, 6, 13),
     ((('a', 2, 0), ('a', 5, 0), ('a', 8, 1), ('a', 10, 1)), None, None, None, None, 0, 1, 10)),
    (((('a', 2, 0), ('a', 4, 0), ('a', 9, 0)), None, None, None, None, 1, 6, 4),
     ((('s', 10, 11, 1, 2, 11, 0),), 10, None, None, None, 4, 10, 8)),
    (((), 4, None, None, None, 10, 4, 13),
     ((('a', 11, 0),), 8, None, None, None, 6, 8, 12)),
    (((), None, None, None, None, 10, 4, 15),
     ((), None, None, None, None, 6, 9, 10)),
    (((('s', 1, 2, 1, 0, 2, 0), ('s', 9, 8, 0, 1, 6, 1), ('s', 4, 11, 0, 5, 10, 1), ('a', 9, 1)), None, None, None, None, 0, 1, 9),
     ((), None, None, None, None, 6, 10, 16)),
    (((), None, None, None, None, 4, 5, 9),
     ((('s', 1, 2, 1, 0, 2, 0),), None, None, 6, None, 8, 0, 14)),
    (((('t', 2),), 9, None, 5, None, 7, 9, 14),
     ((), None, None, 14, None, 8, 10, 15)),
    (((('t', 4),), None, None, None, None, 0, 7, 16),
     ((('a', 5, 1),), None, None, 15, None, 1, 7, 5)),
    (((('s', 9, 8, 1, 1, 8, 0), ('s', 4, 11, 1, 5, 11, 0), ('a', 2, 1), ('a', 8, 0), ('a', 11, 0)), None, None, None, None, 0, 3, 2),
     ((), None, None, None, None, 8, 9, 5)),
    (((), None, None, None, None, 4, 6, 2),
     ((('a', 11, 1),), 5, None, 9, None, 10, 5, 12)),
    (((), 2, None, 6, None, 9, 2, 10),
     ((('t', 1),), None, None, None, None, 3, 4, 13)),
    (((), None, None, None, None, 9, 2, 15),
     ((), None, None, None, None, 5, 8, 13)),
    (((), None, None, 15, None, 9, 2, 16),
     ((), None, None, None, None, 0, 1, 11)),
    (((('t', 5),), None, None, None, None, 7, 9, 17),
     ((('a', 2, 1),), 11, None, 1, None, 5, 11, 16)),
    (((('a', 8, 1), ('a', 11, 1)), None, None, 9, None, 1, 2, 11),
     ((), None, None, None, None, 11, 0, 12)),
    (((), None, None, 1, None, 2, 3, 8),
     ((), None, None, 12, None, 11, 0, 13)),
    (((), 8, None, 3, None, 2, 8, 14),
     ((), 2, None, 13, None, 2, 0, 16)),
    (((), None, None, 2, 14, 4, 10, 8),
     ((), None, None, 16, None, 3, 4, 2)),
    (((), None, None, 4, 10, 7, 0, 11),
     ((), None, None, 3, 4, 5, 7, 2)),
    (((), None, None, 7, 11, 8, 0, 13),
     ((), None, None, 5, 7, 8, 2, 17)),
    (((), None, None, 13, None, 8, 0, 16),
     ((), None, None, 17, None, 10, 0, 2)),
    (((), None, None, 16, None, 8, 0, 17),
     ((), None, None, 10, 0, 11, 2, 8)),
)

TAIL = (
    (8, 0, 17),
    (11, 2, 8),
)


SLOTS = len(OFFSETS[0])
EXTRA = len(SHARED[0])
HELD = SLOTS + EXTRA
NONE = 31


def lookup(values, n, bits=5):
    each = 30 // bits
    words = [sum(v << (bits * k) for k, v in enumerate(values[s:s + each])) for s in range(0, len(values), each)]
    word = jnp.int32(words[0])
    for k, w in enumerate(words[1:], 1):
        word = jnp.where(n >= each * k, jnp.int32(w), word)
    return lax.rem(lax.shift_right_logical(word, bits * lax.rem(n, each)), 1 << bits)


def column(which, place):
    return [NONE if pair[which][place] is None else pair[which][place] for pair in STEPS]


def kernel(chunks, emb_ref, lab_ref, out_ref, emb, ids, buf, labels, label_rows, row_best, column_best, outgoing,
           incoming, load_sem, send_sem, recv_sem, give_sem, take_sem, label_send, label_recv, label_give,
           label_take, result_send, result_recv):
    rows, width = emb.shape
    part = rows // chunks
    load = pltpu.make_async_copy(emb_ref, emb, load_sem.at[0])
    load.start()
    load_ids = pltpu.make_async_copy(lab_ref, ids, load_sem.at[1])
    load_ids.start()
    gx = lax.axis_index("grp")
    mem = lax.axis_index("mem")
    core = lax.rem(mem, 2)
    other = 1 - core
    gy = lax.rem(mem // 2, SIDE)
    gz = mem // (2 * SIDE)

    def at(offset, on):
        x, y, z = (lax.rem(g + k, SIDE) for g, k in zip((gx, gy, gz), offset))
        return (x, (z * SIDE + y) * 2 + on)

    barrier = pltpu.get_barrier_semaphore()
    for direction in DIRS:
        pl.semaphore_signal(barrier, inc=1, device_id=at(direction, core), device_id_type=MESH)
    pl.semaphore_signal(barrier, inc=1, device_id=at((0, 0, 0), other), device_id_type=MESH)

    def chunk_of(slot, h):
        return buf.at[slot, pl.ds(h * part, part)]

    def relay(source, target, h, direction):
        return pltpu.make_async_remote_copy(
            src_ref=chunk_of(source, h), dst_ref=chunk_of(target, h),
            send_sem=send_sem.at[target, h], recv_sem=recv_sem.at[target, h],
            device_id=at(DIRS[direction], core), device_id_type=MESH)

    def relay_label(source, target, direction):
        return pltpu.make_async_remote_copy(
            src_ref=labels.at[source], dst_ref=labels.at[target],
            send_sem=label_send.at[target], recv_sem=label_recv.at[target],
            device_id=at(DIRS[direction], core), device_id_type=MESH)

    def send(source, target, h, direction):
        if h == 0:
            relay_label(source, target, direction).start()
        relay(source, target, h, direction).start()

    def share(slot, k, h):
        return pltpu.make_async_remote_copy(
            src_ref=chunk_of(slot, h), dst_ref=chunk_of(SLOTS + k, h),
            send_sem=give_sem.at[k, h], recv_sem=take_sem.at[k, h],
            device_id=at((0, 0, 0), other), device_id_type=MESH)

    def share_label(slot, k):
        return pltpu.make_async_remote_copy(
            src_ref=labels.at[slot], dst_ref=labels.at[SLOTS + k],
            send_sem=label_give.at[k], recv_sem=label_take.at[k],
            device_id=at((0, 0, 0), other), device_id_type=MESH)

    def give(which, slot, h):
        if slot in SHARED[1 - which]:
            k = SHARED[1 - which].index(slot)
            if h == 0:
                share_label(slot, k).start()
            share(slot, k, h).start()

    load_ids.wait()
    labels[0] = ids[...].astype(jnp.float32)
    load.wait()
    for h in range(chunks):
        e = emb[pl.ds(h * part, part)]
        squares = jnp.sum(e * e, axis=1, keepdims=True)
        buf[0, pl.ds(h * part, part)] = (e * lax.rsqrt(squares + 1e-06)).astype(jnp.bfloat16)
        if h == 0:
            pl.semaphore_wait(barrier, len(DIRS) + 1)
        for which in (0, 1):
            @pl.when(core == which)
            def _(which=which, h=h):
                for move in FIRST_SENDS[which]:
                    if move[2] == h:
                        send(*move)

    for which in (0, 1):
        @pl.when(core == which)
        def _(which=which):
            for h in range(chunks):
                give(which, 0, h)

    def clear(slot, carry):
        column_best[slot] = jnp.full(column_best.shape[1:], FILL, jnp.float32)

        @pl.when(slot < SLOTS)
        def _():
            row_best[slot] = jnp.full(row_best.shape[1:], FILL, jnp.float32)
        return carry

    lax.fori_loop(0, HELD, clear, 0)

    def spread(slot):
        label_rows[slot] = jnp.broadcast_to(labels[slot], (128, rows)).T

    def tile(left, right, own=False):
        sims = lax.dot_general(jnp.concatenate([buf[a] for a in left], axis=0), buf[right], (((1,), (1,)), ((), ())),
                               preferred_element_type=jnp.float32)
        names = labels[right]
        tops = [row_best[a] for a in left]
        for k in range(rows // 128):
            lanes = slice(k * 128, (k + 1) * 128)
            high = column_best[right, :, lanes]
            for n, a in enumerate(left):
                keep = label_rows[a] == names[:, lanes]
                if own:
                    keep = keep & (lax.broadcasted_iota(jnp.int32, (rows, 128), 0)
                                   != lax.broadcasted_iota(jnp.int32, (rows, 128), 1) + k * 128)
                scores = jnp.where(keep, sims[n * rows:(n + 1) * rows, lanes], FILL)
                tops[n] = jnp.maximum(tops[n], scores)
                high = jnp.maximum(high, jnp.max(scores.reshape(rows // 8, 8, 128), axis=0))
            column_best[right, :, lanes] = high
        for n, a in enumerate(left):
            row_best[a] = tops[n]

    def answer(slot):
        offsets = [OFFSETS[w] + tuple(OFFSETS[1 - w][k] for k in SHARED[w]) for w in (0, 1)]
        back = [SIDE - jnp.where(core == 0, *(lookup([o[k] for o in offsets[w]], slot, 2) for w in (0, 1)))
                for k in range(3)]
        return pltpu.make_async_remote_copy(
            src_ref=outgoing.at[slot], dst_ref=incoming.at[slot],
            send_sem=result_send.at[slot], recv_sem=result_recv,
            device_id=at(back, jnp.where(slot < SLOTS, core, other)), device_id_type=MESH)

    def finish(slot):
        by_column = jnp.max(column_best[slot], axis=0, keepdims=True)

        @pl.when(slot < SLOTS)
        def _():
            outgoing[slot] = jnp.maximum(by_column, jnp.max(row_best[slot].T, axis=0, keepdims=True))

        @pl.when(slot >= SLOTS)
        def _():
            outgoing[slot] = by_column

        @pl.when(slot > 0)
        def _():
            answer(slot).start()

        @pl.when(slot == 0)
        def _():
            incoming[0] = outgoing[0]

    def arrived(which, slot, h):
        pltpu.make_async_copy(chunk_of(slot, h), chunk_of(slot, h), recv_sem.at[slot, h]).wait()
        if h == 0:
            pltpu.make_async_copy(labels.at[slot], labels.at[slot], label_recv.at[slot]).wait()
        give(which, slot, h)

    def taken(k):
        for h in range(chunks):
            pltpu.make_async_copy(chunk_of(SLOTS + k, h), chunk_of(SLOTS + k, h), take_sem.at[k, h]).wait()
        pltpu.make_async_copy(labels.at[SLOTS + k], labels.at[SLOTS + k], label_take.at[k]).wait()

    def sent(slot, h):
        relay(0, slot, h, 0).wait_send()

    def moves(n):
        for which in (0, 1):
            todo = STEPS[n][which][0]
            if todo:
                @pl.when(core == which)
                def _(which=which, todo=todo):
                    for op in todo:
                        if op[0] == "a":
                            arrived(which, *op[1:])
                        elif op[0] == "t":
                            taken(op[1])
                        else:
                            if len(op) > 5:
                                sent(*op[5:])
                            send(*op[1:5])

    def chosen(place, n):
        return jnp.where(core == 0, lookup(column(0, place), n), lookup(column(1, place), n))

    spread(0)
    tile((0,), 0, own=True)

    def step(n, carry):
        for g in range(0, len(STEPS), 6):
            @pl.when(lax.div(n, 6) == g // 6)
            def _(g=g):
                for k in range(g, min(g + 6, len(STEPS))):
                    @pl.when(n == k)
                    def _(k=k):
                        moves(k)
        for place in (1, 2):
            opened = chosen(place, n)

            @pl.when(opened != NONE)
            def _(opened=opened):
                spread(opened)
        for place in (3, 4):
            ended = chosen(place, n)

            @pl.when(ended != NONE)
            def _(ended=ended):
                finish(ended)

        tile((chosen(5, n), chosen(6, n)), chosen(7, n))
        return carry

    lax.fori_loop(0, len(STEPS), step, 0)
    left = max(len(t) for t in TAIL)

    def last(n, carry):
        ends = [(list(t) + [NONE] * left)[:left] for t in TAIL]
        ended = jnp.where(core == 0, lookup(ends[0], n), lookup(ends[1], n))

        @pl.when(ended != NONE)
        def _():
            finish(ended)
        return carry

    lax.fori_loop(0, left, last, 0)

    rest = incoming.at[pl.ds(1, HELD - 1)]
    pltpu.make_async_copy(rest, rest, result_recv).wait()
    out_ref[...] = jnp.max(incoming[...], axis=0)

    for which in (0, 1):
        @pl.when(core == which)
        def _(which=which):
            for move in LAST_SENDS[which]:
                sent(*move)
    for k in range(EXTRA):
        for h in range(chunks):
            share(0, k, h).wait_send()
        share_label(0, k).wait_send()
    for slot in range(1, SLOTS):
        relay_label(0, slot, 0).wait_send()
    for slot in range(1, HELD):
        answer(slot).wait_send()


def body(embeddings, cluster_ids):
    rows, width = embeddings.shape
    chunks = 1 + max(h for sends in LAST_SENDS for _, h in sends)
    dma = pltpu.SemaphoreType.DMA
    best = pl.pallas_call(
        functools.partial(kernel, chunks),
        out_shape=jax.ShapeDtypeStruct((1, rows), jnp.float32),
        in_specs=[pl.BlockSpec(memory_space=pl.ANY), pl.BlockSpec(memory_space=pl.ANY)],
        out_specs=pl.BlockSpec(memory_space=pltpu.VMEM),
        scratch_shapes=[
            pltpu.VMEM((rows, width), jnp.float32),
            pltpu.VMEM((1, rows), jnp.int32),
            pltpu.VMEM((HELD, rows, width), jnp.bfloat16),
            pltpu.VMEM((HELD, 1, rows), jnp.float32),
            pltpu.VMEM((SLOTS, rows, 128), jnp.float32),
            pltpu.VMEM((SLOTS, rows, 128), jnp.float32),
            pltpu.VMEM((HELD, 8, rows), jnp.float32),
            pltpu.VMEM((HELD, 1, rows), jnp.float32),
            pltpu.VMEM((HELD, 1, rows), jnp.float32),
            dma((2,)), dma((SLOTS, chunks)), dma((SLOTS, chunks)), dma((EXTRA, chunks)), dma((EXTRA, chunks)),
            dma((SLOTS,)), dma((SLOTS,)), dma((EXTRA,)), dma((EXTRA,)), dma((HELD,)), dma,
        ],
        compiler_params=pltpu.CompilerParams(
            collective_id=0, has_side_effects=True, vmem_limit_bytes=VMEM_BYTES),
    )(embeddings, cluster_ids.reshape(1, rows))
    return best.reshape(rows)


def solution(mesh):
    return jax.shard_map(
        body,
        mesh=mesh,
        in_specs=(P(("grp", "mem"), None), P(("grp", "mem"), None)),
        out_specs=P(("grp", "mem")),
        check_vma=False,
    )
```

```python
import functools

import jax
import jax.numpy as jnp
from jax import lax
from jax.experimental import pallas as pl
from jax.experimental.pallas import tpu as pltpu
from jax.sharding import PartitionSpec as P

FILL = -4.0
MESH = pl.DeviceIdType.MESH
SIDE = 4
VMEM_BYTES = 64 * 1024 * 1024 - 512 * 1024
DIRS = ((1, 0, 0), (3, 0, 0), (0, 1, 0), (0, 3, 0), (0, 0, 1), (0, 0, 3))

OFFSETS = (
    ((0, 0, 0), (1, 0, 0), (2, 0, 0), (0, 1, 0), (3, 1, 0), (2, 2, 0),
     (3, 2, 0), (0, 0, 1), (0, 0, 2), (0, 3, 2), (0, 0, 3), (0, 3, 3)),
    ((0, 0, 0), (0, 3, 0), (1, 3, 0), (2, 3, 0), (3, 0, 0), (2, 1, 0),
     (3, 1, 0), (0, 3, 1), (0, 3, 2), (0, 2, 2), (0, 3, 3), (0, 2, 3)),
)

SHARED = ((0, 2, 4, 7, 9, 11), (1, 2, 4, 7, 8, 11))

FIRST_SENDS = (
    ((0, 1, 0, 0), (0, 3, 0, 2), (0, 7, 0, 4), (0, 10, 1, 5)),
    ((0, 4, 0, 1), (0, 1, 0, 3)),
)

LAST_SENDS = (
    ((1, 0), (1, 1), (2, 0), (2, 1), (3, 0), (3, 1), (4, 0), (4, 1), (5, 0), (5, 1), (6, 0), (6, 1), (7, 0), (7, 1), (8, 0), (8, 1), (9, 0), (9, 1), (10, 0), (10, 1), (11, 0), (11, 1)),
    ((1, 0), (1, 1), (2, 0), (2, 1), (3, 0), (3, 1), (4, 0), (4, 1), (5, 0), (5, 1), (6, 0), (6, 1), (7, 0), (7, 1), (8, 0), (8, 1), (9, 0), (9, 1), (10, 0), (10, 1), (11, 0), (11, 1)),
)

STEPS = (
    (((('s', 0, 1, 1, 0), ('s', 0, 3, 1, 2), ('s', 0, 10, 0, 5), ('s', 0, 7, 1, 4), ('a', 1, 0), ('a', 7, 0), ('a', 10, 1), ('a', 3, 0), ('s', 10, 11, 1, 3), ('s', 7, 8, 0, 4), ('s', 3, 4, 0, 1), ('a', 1, 1), ('t', 0)), 1, None, None, None, 0, 1, 12),
     ((('s', 0, 4, 1, 1), ('s', 0, 1, 1, 3), ('a', 4, 0), ('a', 1, 0), ('s', 1, 2, 0, 0), ('s', 1, 10, 0, 5), ('s', 4, 6, 0, 2), ('a', 1, 1), ('a', 4, 1)), 1, 4, None, None, 1, 4, 0)),
    (((('a', 3, 1), ('a', 7, 1), ('a', 10, 0)), 3, None, None, None, 1, 3, 0),
     ((('s', 1, 10, 1, 5), ('s', 1, 2, 1, 0), ('s', 1, 7, 0, 4), ('s', 4, 6, 1, 2), ('a', 2, 0), ('a', 6, 0), ('a', 10, 0), ('s', 6, 5, 0, 1), ('s', 10, 11, 0, 3), ('s', 1, 7, 1, 4), ('a', 10, 1)), None, None, None, None, 0, 4, 10)),
    (((), None, None, None, None, 0, 3, 7),
     ((('a', 2, 1), ('a', 7, 0), ('a', 6, 1), ('t', 3)), 10, None, None, None, 1, 10, 15)),
    (((), 7, None, None, None, 3, 7, 1),
     ((), None, None, None, None, 4, 10, 1)),
    (((), None, None, None, None, 3, 7, 12),
     ((), None, None, None, None, 4, 10, 2)),
    (((('s', 3, 4, 1, 1), ('s', 10, 11, 0, 3)), None, None, None, None, 1, 3, 10),
     ((), 2, None, None, None, 1, 2, 6)),
    (((('t', 2),), None, None, None, None, 1, 3, 14),
     ((('s', 10, 11, 1, 3), ('s', 6, 5, 1, 1), ('s', 7, 8, 0, 4), ('s', 2, 3, 0, 0)), 6, None, None, None, 2, 6, 15)),
    (((('a', 8, 0), ('a', 11, 1)), 10, None, None, None, 7, 10, 14),
     ((('t', 0),), None, None, None, None, 10, 6, 12)),
    (((('a', 4, 0), ('s', 4, 6, 0, 2), ('s', 10, 8, 1, 5), ('s', 1, 2, 0, 0), ('a', 4, 1)), None, None, None, None, 1, 10, 4),
     ((('a', 11, 0), ('a', 7, 1), ('a', 5, 0), ('s', 11, 9, 0, 5), ('t', 2)), None, None, None, None, 1, 2, 14)),
    (((('a', 11, 0),), 4, None, None, None, 10, 4, 7),
     ((), None, None, None, None, 0, 2, 7)),
    (((), None, None, None, None, 10, 4, 12),
     ((), None, None, None, None, 4, 10, 7)),
    (((), None, None, None, None, 1, 3, 11),
     ((('t', 5),), 7, None, None, None, 6, 7, 17)),
    (((), None, None, None, None, 4, 7, 11),
     ((), None, None, None, None, 10, 7, 6)),
    (((), 11, None, None, None, 11, 0, 12),
     ((('s', 7, 8, 1, 4),), None, None, None, None, 10, 7, 14)),
    (((('s', 4, 6, 1, 2), ('t', 1)), None, None, 12, None, 10, 11, 13),
     ((('a', 11, 1),), None, None, None, None, 0, 2, 11)),
    (((('a', 2, 0), ('a', 6, 0), ('a', 8, 1)), None, None, 10, None, 1, 4, 8),
     ((('s', 11, 9, 1, 5), ('a', 5, 1), ('a', 3, 0)), None, None, None, None, 6, 7, 11)),
    (((), 8, None, None, None, 11, 8, 14),
     ((('a', 8, 0),), 11, None, None, None, 7, 11, 12)),
    (((('t', 3),), None, None, None, None, 0, 3, 15),
     ((('a', 9, 0), ('t', 4)), 5, None, 7, None, 6, 5, 16)),
    (((('s', 1, 2, 1, 0), ('s', 6, 5, 0, 1), ('s', 8, 9, 0, 3), ('a', 6, 1)), None, None, None, None, 0, 1, 6),
     ((), None, None, None, None, 6, 5, 16)),
    (((), None, None, None, None, 7, 8, 6),
     ((('s', 2, 3, 1, 0),), None, None, 16, None, 10, 11, 5)),
    (((('t', 5),), None, None, None, None, 0, 3, 17),
     ((), None, None, None, None, 11, 5, 15)),
    (((('s', 6, 5, 1, 1), ('s', 8, 9, 1, 3), ('a', 9, 0), ('a', 5, 0), ('a', 2, 1)), None, None, None, None, 0, 4, 2),
     ((('a', 8, 1),), None, None, 15, None, 2, 4, 8)),
    (((), 6, 2, 4, None, 6, 2, 11),
     ((), None, None, None, None, 5, 6, 8)),
    (((), None, None, None, None, 6, 2, 14),
     ((('a', 9, 1),), 8, None, 6, None, 5, 8, 12)),
    (((), None, None, 14, None, 6, 2, 15),
     ((), None, None, None, None, 11, 8, 14)),
    (((), None, None, None, None, 6, 2, 17),
     ((('t', 1),), None, None, None, None, 1, 5, 13)),
    (((), None, None, None, None, 7, 8, 2),
     ((), None, None, None, None, 8, 10, 13)),
    (((('t', 4),), None, None, None, None, 3, 6, 16),
     ((('a', 3, 1),), None, None, None, None, 0, 2, 9)),
    (((('a', 5, 1), ('a', 9, 1)), None, None, 6, None, 2, 7, 5),
     ((), 9, None, 2, None, 9, 0, 12)),
    (((), 5, None, 7, None, 5, 0, 15),
     ((), None, None, 12, None, 9, 0, 13)),
    (((), None, None, 15, None, 5, 0, 16),
     ((), None, None, 13, None, 1, 4, 3)),
    (((), None, None, 16, None, 5, 0, 17),
     ((), 3, None, 1, 4, 5, 3, 17)),
    (((), None, None, 17, None, 8, 5, 13),
     ((), None, None, 17, None, 8, 10, 3)),
    (((), None, None, 13, None, 8, 11, 5),
     ((), None, None, 8, 10, 9, 3, 5)),
    (((), None, None, 8, 11, 1, 2, 9),
     ((), None, None, 5, None, 9, 3, 14)),
    (((), None, None, 5, 1, 3, 0, 9),
     ((), None, None, 9, 14, 11, 0, 3)),
)

TAIL = (
    (2, 3, 0, 9),
    (11, 0, 3),
)


SLOTS = len(OFFSETS[0])
EXTRA = len(SHARED[0])
HELD = SLOTS + EXTRA
NONE = 31


def lookup(values, n, bits=5):
    each = 30 // bits
    words = [sum(v << (bits * k) for k, v in enumerate(values[s:s + each])) for s in range(0, len(values), each)]
    word = jnp.int32(words[0])
    for k, w in enumerate(words[1:], 1):
        word = jnp.where(n >= each * k, jnp.int32(w), word)
    return lax.rem(lax.shift_right_logical(word, bits * lax.rem(n, each)), 1 << bits)


def column(which, place):
    return [NONE if pair[which][place] is None else pair[which][place] for pair in STEPS]


def kernel(chunks, emb_ref, lab_ref, out_ref, emb, ids, buf, labels, label_rows, row_best, column_best, outgoing,
           incoming, load_sem, send_sem, recv_sem, give_sem, take_sem, label_send, label_recv, label_give,
           label_take, result_send, result_recv):
    rows, width = emb.shape
    part = rows // chunks
    load = pltpu.make_async_copy(emb_ref, emb, load_sem.at[0])
    load.start()
    load_ids = pltpu.make_async_copy(lab_ref, ids, load_sem.at[1])
    load_ids.start()
    gx = lax.axis_index("grp")
    mem = lax.axis_index("mem")
    core = lax.rem(mem, 2)
    other = 1 - core
    gy = lax.rem(mem // 2, SIDE)
    gz = mem // (2 * SIDE)

    def at(offset, on):
        x, y, z = (lax.rem(g + k, SIDE) for g, k in zip((gx, gy, gz), offset))
        return (x, (z * SIDE + y) * 2 + on)

    barrier = pltpu.get_barrier_semaphore()
    for direction in DIRS:
        pl.semaphore_signal(barrier, inc=1, device_id=at(direction, core), device_id_type=MESH)
    pl.semaphore_signal(barrier, inc=1, device_id=at((0, 0, 0), other), device_id_type=MESH)

    def chunk_of(slot, h):
        return buf.at[slot, pl.ds(h * part, part)]

    def relay(source, target, h, direction):
        return pltpu.make_async_remote_copy(
            src_ref=chunk_of(source, h), dst_ref=chunk_of(target, h),
            send_sem=send_sem.at[target, h], recv_sem=recv_sem.at[target, h],
            device_id=at(DIRS[direction], core), device_id_type=MESH)

    def relay_label(source, target, direction):
        return pltpu.make_async_remote_copy(
            src_ref=labels.at[source], dst_ref=labels.at[target],
            send_sem=label_send.at[target], recv_sem=label_recv.at[target],
            device_id=at(DIRS[direction], core), device_id_type=MESH)

    def send(source, target, h, direction):
        if h == 0:
            relay_label(source, target, direction).start()
        relay(source, target, h, direction).start()

    def share(slot, k, h):
        return pltpu.make_async_remote_copy(
            src_ref=chunk_of(slot, h), dst_ref=chunk_of(SLOTS + k, h),
            send_sem=give_sem.at[k, h], recv_sem=take_sem.at[k, h],
            device_id=at((0, 0, 0), other), device_id_type=MESH)

    def share_label(slot, k):
        return pltpu.make_async_remote_copy(
            src_ref=labels.at[slot], dst_ref=labels.at[SLOTS + k],
            send_sem=label_give.at[k], recv_sem=label_take.at[k],
            device_id=at((0, 0, 0), other), device_id_type=MESH)

    def give(which, slot, h):
        if slot in SHARED[1 - which]:
            k = SHARED[1 - which].index(slot)
            if h == 0:
                share_label(slot, k).start()
            share(slot, k, h).start()

    load_ids.wait()
    labels[0] = ids[...].astype(jnp.float32)
    load.wait()
    for h in range(chunks):
        e = emb[pl.ds(h * part, part)]
        squares = jnp.sum(e * e, axis=1, keepdims=True)
        buf[0, pl.ds(h * part, part)] = (e * lax.rsqrt(squares + 1e-06)).astype(jnp.bfloat16)
        if h == 0:
            pl.semaphore_wait(barrier, len(DIRS) + 1)
        for which in (0, 1):
            @pl.when(core == which)
            def _(which=which, h=h):
                for move in FIRST_SENDS[which]:
                    if move[2] == h:
                        send(*move)

    for which in (0, 1):
        @pl.when(core == which)
        def _(which=which):
            for h in range(chunks):
                give(which, 0, h)

    def clear(slot, carry):
        column_best[slot] = jnp.full(column_best.shape[1:], FILL, jnp.float32)

        @pl.when(slot < SLOTS)
        def _():
            row_best[slot] = jnp.full(row_best.shape[1:], FILL, jnp.float32)
        return carry

    lax.fori_loop(0, HELD, clear, 0)

    def spread(slot):
        label_rows[slot] = jnp.broadcast_to(labels[slot], (128, rows)).T

    def tile(left, right, own=False):
        sims = lax.dot_general(jnp.concatenate([buf[a] for a in left], axis=0), buf[right], (((1,), (1,)), ((), ())),
                               preferred_element_type=jnp.float32)
        names = labels[right]
        tops = [row_best[a] for a in left]
        for k in range(rows // 128):
            lanes = slice(k * 128, (k + 1) * 128)
            high = column_best[right, :, lanes]
            for n, a in enumerate(left):
                keep = label_rows[a] == names[:, lanes]
                if own:
                    keep = keep & (lax.broadcasted_iota(jnp.int32, (rows, 128), 0)
                                   != lax.broadcasted_iota(jnp.int32, (rows, 128), 1) + k * 128)
                scores = jnp.where(keep, sims[n * rows:(n + 1) * rows, lanes], FILL)
                tops[n] = jnp.maximum(tops[n], scores)
                high = jnp.maximum(high, jnp.max(scores.reshape(rows // 8, 8, 128), axis=0))
            column_best[right, :, lanes] = high
        for n, a in enumerate(left):
            row_best[a] = tops[n]

    def answer(slot):
        offsets = [OFFSETS[w] + tuple(OFFSETS[1 - w][k] for k in SHARED[w]) for w in (0, 1)]
        back = [SIDE - jnp.where(core == 0, *(lookup([o[k] for o in offsets[w]], slot, 2) for w in (0, 1)))
                for k in range(3)]
        return pltpu.make_async_remote_copy(
            src_ref=outgoing.at[slot], dst_ref=incoming.at[slot],
            send_sem=result_send.at[slot], recv_sem=result_recv,
            device_id=at(back, jnp.where(slot < SLOTS, core, other)), device_id_type=MESH)

    def finish(slot):
        by_column = jnp.max(column_best[slot], axis=0, keepdims=True)

        @pl.when(slot < SLOTS)
        def _():
            outgoing[slot] = jnp.maximum(by_column, jnp.max(row_best[slot].T, axis=0, keepdims=True))

        @pl.when(slot >= SLOTS)
        def _():
            outgoing[slot] = by_column

        @pl.when(slot > 0)
        def _():
            answer(slot).start()

        @pl.when(slot == 0)
        def _():
            incoming[0] = outgoing[0]

    def arrived(which, slot, h):
        pltpu.make_async_copy(chunk_of(slot, h), chunk_of(slot, h), recv_sem.at[slot, h]).wait()
        if h == 0:
            pltpu.make_async_copy(labels.at[slot], labels.at[slot], label_recv.at[slot]).wait()
        give(which, slot, h)

    def taken(k):
        for h in range(chunks):
            pltpu.make_async_copy(chunk_of(SLOTS + k, h), chunk_of(SLOTS + k, h), take_sem.at[k, h]).wait()
        pltpu.make_async_copy(labels.at[SLOTS + k], labels.at[SLOTS + k], label_take.at[k]).wait()

    def sent(slot, h):
        relay(0, slot, h, 0).wait_send()

    def moves(n):
        for which in (0, 1):
            todo = STEPS[n][which][0]
            if todo:
                @pl.when(core == which)
                def _(which=which, todo=todo):
                    for op in todo:
                        if op[0] == "a":
                            arrived(which, *op[1:])
                        elif op[0] == "t":
                            taken(op[1])
                        else:
                            if len(op) > 5:
                                sent(*op[5:])
                            send(*op[1:5])

    def chosen(place, n):
        return jnp.where(core == 0, lookup(column(0, place), n), lookup(column(1, place), n))

    spread(0)
    tile((0,), 0, own=True)

    def step(n, carry):
        for g in range(0, len(STEPS), 6):
            @pl.when(lax.div(n, 6) == g // 6)
            def _(g=g):
                for k in range(g, min(g + 6, len(STEPS))):
                    @pl.when(n == k)
                    def _(k=k):
                        moves(k)
        for place in (1, 2):
            opened = chosen(place, n)

            @pl.when(opened != NONE)
            def _(opened=opened):
                spread(opened)
        for place in (3, 4):
            ended = chosen(place, n)

            @pl.when(ended != NONE)
            def _(ended=ended):
                finish(ended)

        tile((chosen(5, n), chosen(6, n)), chosen(7, n))
        return carry

    lax.fori_loop(0, len(STEPS), step, 0)
    left = max(len(t) for t in TAIL)

    def last(n, carry):
        ends = [(list(t) + [NONE] * left)[:left] for t in TAIL]
        ended = jnp.where(core == 0, lookup(ends[0], n), lookup(ends[1], n))

        @pl.when(ended != NONE)
        def _():
            finish(ended)
        return carry

    lax.fori_loop(0, left, last, 0)

    rest = incoming.at[pl.ds(1, HELD - 1)]
    pltpu.make_async_copy(rest, rest, result_recv).wait()
    out_ref[...] = jnp.max(incoming[...], axis=0).reshape(rows)

    for which in (0, 1):
        @pl.when(core == which)
        def _(which=which):
            for move in LAST_SENDS[which]:
                sent(*move)
    for k in range(EXTRA):
        for h in range(chunks):
            share(0, k, h).wait_send()
        share_label(0, k).wait_send()
    for slot in range(1, SLOTS):
        relay_label(0, slot, 0).wait_send()
    for slot in range(1, HELD):
        answer(slot).wait_send()


def body(embeddings, cluster_ids):
    rows, width = embeddings.shape
    chunks = 1 + max(h for sends in LAST_SENDS for _, h in sends)
    dma = pltpu.SemaphoreType.DMA
    return pl.pallas_call(
        functools.partial(kernel, chunks),
        out_shape=jax.ShapeDtypeStruct((rows,), jnp.float32),
        in_specs=[pl.BlockSpec(memory_space=pl.ANY), pl.BlockSpec(memory_space=pl.ANY)],
        out_specs=pl.BlockSpec(memory_space=pltpu.VMEM),
        scratch_shapes=[
            pltpu.VMEM((rows, width), jnp.float32),
            pltpu.VMEM((1, rows), jnp.int32),
            pltpu.VMEM((HELD, rows, width), jnp.bfloat16),
            pltpu.VMEM((HELD, 1, rows), jnp.float32),
            pltpu.VMEM((SLOTS, rows, 128), jnp.float32),
            pltpu.VMEM((SLOTS, rows, 128), jnp.float32),
            pltpu.VMEM((HELD, 8, rows), jnp.float32),
            pltpu.VMEM((HELD, 1, rows), jnp.float32),
            pltpu.VMEM((HELD, 1, rows), jnp.float32),
            dma((2,)), dma((SLOTS, chunks)), dma((SLOTS, chunks)), dma((EXTRA, chunks)), dma((EXTRA, chunks)),
            dma((SLOTS,)), dma((SLOTS,)), dma((EXTRA,)), dma((EXTRA,)), dma((HELD,)), dma,
        ],
        compiler_params=pltpu.CompilerParams(
            collective_id=0, has_side_effects=True, vmem_limit_bytes=VMEM_BYTES),
    )(embeddings, cluster_ids.reshape(1, rows))


def solution(mesh):
    return jax.shard_map(
        body,
        mesh=mesh,
        in_specs=(P(("grp", "mem"), None), P(("grp", "mem"), None)),
        out_specs=P(("grp", "mem")),
        check_vma=False,
    )
```

```python
import functools

import jax
import jax.numpy as jnp
from jax import lax
from jax.experimental import pallas as pl
from jax.experimental.pallas import tpu as pltpu
from jax.sharding import PartitionSpec as P

FILL = -4.0
MESH = pl.DeviceIdType.MESH
SIDE = 4
VMEM_BYTES = 64 * 1024 * 1024 - 512 * 1024
DIRS = ((1, 0, 0), (3, 0, 0), (0, 1, 0), (0, 3, 0), (0, 0, 1), (0, 0, 3))

OFFSETS = (
    ((0, 0, 0), (0, 1, 0), (1, 1, 0), (0, 2, 0), (1, 2, 0), (0, 3, 0),
     (3, 0, 0), (0, 0, 1), (0, 0, 2), (2, 0, 2), (2, 0, 3), (3, 0, 3)),
    ((0, 0, 0), (1, 1, 0), (2, 1, 0), (1, 2, 0), (2, 2, 0), (1, 3, 0),
     (1, 0, 0), (1, 0, 1), (1, 0, 2), (3, 0, 2), (3, 0, 3), (0, 0, 3)),
)

SHARED = ((2, 5, 7, 9, 10, 11), (0, 2, 4, 7, 8, 11))

FIRST_SENDS = (
    ((0, 6, 0, 1), (0, 1, 0, 2), (0, 5, 0, 3), (0, 7, 0, 4)),
    ((0, 6, 0, 0), (0, 11, 0, 5)),
)

LAST_SENDS = (
    ((1, 0), (1, 1), (2, 0), (2, 1), (3, 0), (3, 1), (4, 0), (4, 1), (5, 0), (5, 1), (6, 0), (6, 1), (7, 0), (7, 1), (8, 0), (8, 1), (9, 0), (9, 1), (10, 0), (10, 1), (11, 0), (11, 1)),
    ((1, 0), (1, 1), (2, 0), (2, 1), (3, 0), (3, 1), (4, 0), (4, 1), (5, 0), (5, 1), (6, 0), (6, 1), (7, 0), (7, 1), (8, 0), (8, 1), (9, 0), (9, 1), (10, 0), (10, 1), (11, 0), (11, 1)),
)

STEPS = (
    (((('s', 0, 6, 1, 1), ('s', 0, 1, 1, 2), ('s', 0, 5, 1, 3), ('s', 0, 7, 1, 4), ('a', 7, 0), ('a', 6, 0), ('a', 5, 0), ('a', 1, 0), ('s', 1, 2, 0, 0), ('s', 6, 11, 0, 5), ('s', 5, 3, 0, 3), ('a', 1, 1), ('a', 6, 1), ('a', 5, 1)), (1, 6, 5, None), (None, None), (1, 6, 0, 6, 5, 1)),
     ((('s', 0, 6, 1, 0), ('s', 0, 11, 1, 5), ('a', 11, 0), ('a', 6, 0), ('s', 11, 10, 0, 1), ('s', 6, 7, 0, 4), ('s', 6, 1, 0, 2), ('a', 6, 1), ('a', 11, 1), ('t', 0)), (6, 11, None, None), (None, None), (0, 6, 12, 6, 11, 0))),
    (((('a', 7, 1),), (7, None, None, None), (None, None), (0, 1, 7, 6, 7, 5)),
     ((('s', 6, 1, 1, 2), ('s', 6, 5, 1, 3), ('s', 11, 10, 1, 1), ('s', 6, 7, 1, 4), ('a', 7, 0), ('a', 1, 0), ('a', 10, 0), ('s', 1, 2, 0, 0), ('s', 1, 3, 0, 2), ('s', 6, 5, 0, 3), ('s', 10, 9, 0, 5), ('a', 7, 1)), (7, None, None, None), (None, None), (6, 7, 11, 11, 7, 12))),
    (((('s', 1, 2, 1, 0), ('s', 6, 11, 1, 5), ('t', 5)), (None, None, None, None), (None, None), (1, 5, 17, 6, 7, 17)),
     ((('a', 5, 1), ('a', 10, 1), ('a', 1, 1)), (None, None, None, None), (None, None), (6, 7, 10, 0, 6, 1))),
    (((('a', 11, 0), ('a', 2, 0), ('a', 3, 0), ('s', 7, 8, 0, 4), ('s', 11, 10, 0, 1), ('a', 11, 1)), (11, None, None, None), (None, None), (1, 5, 11, 6, 11, 7)),
     ((), (10, 1, None, None), (None, None), (7, 10, 1, 10, 1, 12))),
    (((('a', 2, 1),), (None, None, None, None), (None, None), (5, 6, 2, 7, 11, 2)),
     ((('s', 1, 2, 1, 0), ('s', 10, 9, 1, 5), ('s', 7, 8, 0, 4), ('t', 3), ('t', 1)), (None, None, None, None), (None, None), (10, 1, 15, 0, 6, 13))),
    (((('s', 2, 4, 0, 2), ('s', 11, 10, 1, 1), ('t', 2)), (2, None, None, None), (None, None), (1, 2, 14, 5, 6, 14)),
     ((('a', 2, 0), ('a', 5, 0), ('t', 5)), (5, None, None, None), (None, None), (0, 7, 5, 1, 5, 17))),
    (((('s', 5, 3, 1, 3), ('a', 8, 0), ('a', 10, 0), ('s', 7, 8, 1, 4), ('s', 10, 9, 0, 5), ('s', 2, 4, 1, 2), ('a', 4, 0), ('a', 3, 1), ('t', 1)), (3, None, None, None), (None, None), (1, 6, 13, 2, 3, 17)),
     ((('a', 3, 0), ('a', 9, 0)), (None, None, None, None), (None, None), (10, 5, 13, 10, 11, 5))),
    (((('a', 10, 1), ('t', 4)), (None, None, None, None), (None, None), (5, 3, 16, 7, 11, 3)),
     ((('s', 3, 4, 0, 0), ('s', 5, 3, 1, 3), ('a', 8, 0), ('a', 2, 1)), (None, None, None, None), (None, None), (11, 5, 1, 0, 5, 2))),
    (((), (None, None, None, None), (None, None), (11, 3, 14, 0, 2, 10)),
     ((('a', 9, 1),), (2, None, None, None), (None, None), (5, 2, 12, 5, 2, 15))),
    (((('s', 10, 9, 1, 5), ('t', 0)), (None, None, None, None), (None, None), (3, 5, 10, 5, 6, 12)),
     ((('s', 7, 8, 1, 4), ('s', 2, 4, 1, 2)), (None, None, None, None), (12, None), (5, 2, 15, 7, 10, 2))),
    (((('a', 4, 1), ('t', 3)), (4, None, None, None), (None, None), (1, 3, 15, 4, 0, 14)),
     ((('a', 3, 1),), (3, None, None, None), (5, None), (1, 2, 9, 2, 3, 17))),
    (((('a', 9, 0), ('a', 8, 1)), (None, None, None, None), (14, None), (4, 0, 16, 5, 4, 15)),
     ((('a', 4, 0),), (9, None, None, None), (None, None), (7, 9, 3, 9, 3, 13))),
    (((), (10, None, None, None), (16, 5), (10, 4, 7, 0, 1, 8)),
     ((), (None, None, None, None), (None, None), (9, 3, 15, 10, 11, 3))),
    (((), (8, None, None, None), (7, None), (2, 3, 8, 6, 8, 4)),
     ((('t', 4),), (None, None, None, None), (15, 10), (1, 3, 16, 6, 0, 16))),
    (((('a', 9, 1),), (None, None, None, None), (6, 4), (8, 0, 15, 10, 8, 12)),
     ((('a', 4, 1), ('a', 8, 1), ('t', 2)), (8, None, None, None), (16, None), (0, 7, 4, 0, 8, 14))),
    (((), (None, None, None, None), (15, None), (10, 8, 13, 10, 8, 17)),
     ((), (None, None, None, None), (7, 14), (1, 2, 8, 3, 6, 8))),
    (((), (None, None, None, None), (13, 10), (1, 2, 9, 3, 0, 9)),
     ((), (4, None, None, None), (1, 2), (4, 8, 9, 4, 8, 17))),
    (((), (9, None, None, None), (17, 1), (9, 0, 12, 11, 9, 8)),
     ((), (None, None, None, None), (3, 6), (8, 0, 13, 11, 0, 8))),
)

TAIL = (
    (2, 3, 0, 12, 11, 9, 8),
    (9, 4, 17, 13, 11, 0, 8),
)


SLOTS = len(OFFSETS[0])
EXTRA = len(SHARED[0])
HELD = SLOTS + EXTRA
NONE = 31


def words(values, bits=5):
    each = 30 // bits
    return [sum(v << (bits * k) for k, v in enumerate(values[s:s + each])) for s in range(0, len(values), each)]


def lookup(packed, n, bits=5):
    each = 30 // bits
    word = packed[0]
    for k, w in enumerate(packed[1:], 1):
        word = jnp.where(n >= each * k, w, word)
    return lax.rem(lax.shift_right_logical(word, bits * lax.rem(n, each)), 1 << bits)


def of_core(core, lists, bits=5):
    return [jnp.where(core == 0, jnp.int32(a), jnp.int32(b)) for a, b in zip(*(words(v, bits) for v in lists))]


def column(which, place, k):
    return [NONE if pair[which][place][k] is None else pair[which][place][k] for pair in STEPS]


def kernel(chunks, emb_ref, lab_ref, out_ref, emb, ids, buf, labels, label_rows, row_best, column_best, outgoing,
           incoming, load_sem, send_sem, recv_sem, give_sem, take_sem, label_send, label_recv, label_give,
           label_take, result_send, result_recv):
    rows, width = emb.shape
    part = rows // chunks
    load = pltpu.make_async_copy(emb_ref, emb, load_sem.at[0])
    load.start()
    load_ids = pltpu.make_async_copy(lab_ref, ids, load_sem.at[1])
    load_ids.start()
    gx = lax.axis_index("grp")
    mem = lax.axis_index("mem")
    core = lax.rem(mem, 2)
    other = 1 - core
    gy = lax.rem(mem // 2, SIDE)
    gz = mem // (2 * SIDE)

    def at(offset, on):
        x, y, z = (lax.rem(g + k, SIDE) for g, k in zip((gx, gy, gz), offset))
        return (x, (z * SIDE + y) * 2 + on)

    barrier = pltpu.get_barrier_semaphore()
    for direction in DIRS:
        pl.semaphore_signal(barrier, inc=1, device_id=at(direction, core), device_id_type=MESH)
    pl.semaphore_signal(barrier, inc=1, device_id=at((0, 0, 0), other), device_id_type=MESH)

    def chunk_of(slot, h):
        return buf.at[slot, pl.ds(h * part, part)]

    def relay(source, target, h, direction):
        return pltpu.make_async_remote_copy(
            src_ref=chunk_of(source, h), dst_ref=chunk_of(target, h),
            send_sem=send_sem.at[target, h], recv_sem=recv_sem.at[target, h],
            device_id=at(DIRS[direction], core), device_id_type=MESH)

    def relay_label(source, target, direction):
        return pltpu.make_async_remote_copy(
            src_ref=labels.at[source], dst_ref=labels.at[target],
            send_sem=label_send.at[target], recv_sem=label_recv.at[target],
            device_id=at(DIRS[direction], core), device_id_type=MESH)

    def send(source, target, h, direction):
        if h == 0:
            relay_label(source, target, direction).start()
        relay(source, target, h, direction).start()

    def share(slot, k, h):
        return pltpu.make_async_remote_copy(
            src_ref=chunk_of(slot, h), dst_ref=chunk_of(SLOTS + k, h),
            send_sem=give_sem.at[k, h], recv_sem=take_sem.at[k, h],
            device_id=at((0, 0, 0), other), device_id_type=MESH)

    def share_label(slot, k):
        return pltpu.make_async_remote_copy(
            src_ref=labels.at[slot], dst_ref=labels.at[SLOTS + k],
            send_sem=label_give.at[k], recv_sem=label_take.at[k],
            device_id=at((0, 0, 0), other), device_id_type=MESH)

    def give(which, slot, h):
        if slot in SHARED[1 - which]:
            k = SHARED[1 - which].index(slot)
            if h == 0:
                share_label(slot, k).start()
            share(slot, k, h).start()

    load_ids.wait()
    labels[0] = ids[...].astype(jnp.float32)
    load.wait()
    for h in range(chunks):
        e = emb[pl.ds(h * part, part)]
        squares = jnp.sum(e * e, axis=1, keepdims=True)
        buf[0, pl.ds(h * part, part)] = (e * lax.rsqrt(squares + 1e-06)).astype(jnp.bfloat16)
        if h == 0:
            pl.semaphore_wait(barrier, len(DIRS) + 1)
        for which in (0, 1):
            @pl.when(core == which)
            def _(which=which, h=h):
                for move in FIRST_SENDS[which]:
                    if move[2] == h:
                        send(*move)

    for which in (0, 1):
        @pl.when(core == which)
        def _(which=which):
            for h in range(chunks):
                give(which, 0, h)

    def clear(slot, carry):
        column_best[slot] = jnp.full(column_best.shape[1:], FILL, jnp.float32)

        @pl.when(slot < SLOTS)
        def _():
            row_best[slot] = jnp.full(row_best.shape[1:], FILL, jnp.float32)
        return carry

    lax.fori_loop(0, HELD, clear, 0)

    def spread(slot):
        label_rows[slot] = jnp.broadcast_to(labels[slot], (128, rows)).T

    def tile(left, right, own=False):
        sims = lax.dot_general(jnp.concatenate([buf[a] for a in left], axis=0), buf[right], (((1,), (1,)), ((), ())),
                               preferred_element_type=jnp.float32)
        names = labels[right]
        tops = [row_best[a] for a in left]
        for k in range(rows // 128):
            lanes = slice(k * 128, (k + 1) * 128)
            high = column_best[right, :, lanes]
            for n, a in enumerate(left):
                keep = label_rows[a] == names[:, lanes]
                if own:
                    keep = keep & (lax.broadcasted_iota(jnp.int32, (rows, 128), 0)
                                   != lax.broadcasted_iota(jnp.int32, (rows, 128), 1) + k * 128)
                scores = jnp.where(keep, sims[n * rows:(n + 1) * rows, lanes], FILL)
                tops[n] = jnp.maximum(tops[n], scores)
                high = jnp.maximum(high, jnp.max(scores.reshape(rows // 8, 8, 128), axis=0))
            column_best[right, :, lanes] = high
        for n, a in enumerate(left):
            row_best[a] = tops[n]

    def answer(slot):
        offsets = [OFFSETS[w] + tuple(OFFSETS[1 - w][k] for k in SHARED[w]) for w in (0, 1)]
        back = [SIDE - lookup(of_core(core, [[o[k] for o in held] for held in offsets], 2), slot, 2) for k in range(3)]
        return pltpu.make_async_remote_copy(
            src_ref=outgoing.at[slot], dst_ref=incoming.at[slot],
            send_sem=result_send.at[slot], recv_sem=result_recv,
            device_id=at(back, jnp.where(slot < SLOTS, core, other)), device_id_type=MESH)

    def finish(slot):
        by_column = jnp.max(column_best[slot], axis=0, keepdims=True)

        @pl.when(slot < SLOTS)
        def _():
            outgoing[slot] = jnp.maximum(by_column, jnp.max(row_best[slot].T, axis=0, keepdims=True))

        @pl.when(slot >= SLOTS)
        def _():
            outgoing[slot] = by_column

        @pl.when(slot > 0)
        def _():
            answer(slot).start()

        @pl.when(slot == 0)
        def _():
            incoming[0] = outgoing[0]

    def arrived(which, slot, h):
        pltpu.make_async_copy(chunk_of(slot, h), chunk_of(slot, h), recv_sem.at[slot, h]).wait()
        if h == 0:
            pltpu.make_async_copy(labels.at[slot], labels.at[slot], label_recv.at[slot]).wait()
        give(which, slot, h)

    def taken(k):
        for h in range(chunks):
            pltpu.make_async_copy(chunk_of(SLOTS + k, h), chunk_of(SLOTS + k, h), take_sem.at[k, h]).wait()
        pltpu.make_async_copy(labels.at[SLOTS + k], labels.at[SLOTS + k], label_take.at[k]).wait()

    def sent(slot, h):
        relay(0, slot, h, 0).wait_send()

    def moves(n):
        for which in (0, 1):
            todo = STEPS[n][which][0]
            if todo:
                @pl.when(core == which)
                def _(which=which, todo=todo):
                    for op in todo:
                        if op[0] == "a":
                            arrived(which, *op[1:])
                        elif op[0] == "t":
                            taken(op[1])
                        else:
                            if len(op) > 5:
                                sent(*op[5:])
                            send(*op[1:5])

    def table(place):
        return [of_core(core, [column(w, place, k) for w in (0, 1)]) for k in range(len(STEPS[0][0][place]))]

    to_open, to_finish, to_compare = table(1), table(2), table(3)
    spread(0)
    tile((0,), 0, own=True)

    def step(n, carry):
        for g in range(0, len(STEPS), 6):
            @pl.when(lax.div(n, 6) == g // 6)
            def _(g=g):
                for k in range(g, min(g + 6, len(STEPS))):
                    @pl.when(n == k)
                    def _(k=k):
                        moves(k)
        for listed, act in ((to_open, spread), (to_finish, finish)):
            for packed in listed:
                slot = lookup(packed, n)

                @pl.when(slot != NONE)
                def _(slot=slot, act=act):
                    act(slot)
        units = [lookup(packed, n) for packed in to_compare]
        for k in range(0, len(units), 3):
            tile(units[k:k + 2], units[k + 2])
        return carry

    lax.fori_loop(0, len(STEPS), step, 0)
    left = max(len(t) for t in TAIL)
    ends = of_core(core, [(list(t) + [NONE] * left)[:left] for t in TAIL])

    def last(n, carry):
        ended = lookup(ends, n)

        @pl.when(ended != NONE)
        def _():
            finish(ended)
        return carry

    lax.fori_loop(0, left, last, 0)

    rest = incoming.at[pl.ds(1, HELD - 1)]
    pltpu.make_async_copy(rest, rest, result_recv).wait()
    out_ref[...] = jnp.max(incoming[...], axis=0).reshape(rows)

    for which in (0, 1):
        @pl.when(core == which)
        def _(which=which):
            for move in LAST_SENDS[which]:
                sent(*move)
    for k in range(EXTRA):
        for h in range(chunks):
            share(0, k, h).wait_send()
        share_label(0, k).wait_send()
    for slot in range(1, SLOTS):
        relay_label(0, slot, 0).wait_send()
    for slot in range(1, HELD):
        answer(slot).wait_send()


def body(embeddings, cluster_ids):
    rows, width = embeddings.shape
    chunks = 1 + max(h for sends in LAST_SENDS for _, h in sends)
    dma = pltpu.SemaphoreType.DMA
    return pl.pallas_call(
        functools.partial(kernel, chunks),
        out_shape=jax.ShapeDtypeStruct((rows,), jnp.float32),
        in_specs=[pl.BlockSpec(memory_space=pl.ANY), pl.BlockSpec(memory_space=pl.ANY)],
        out_specs=pl.BlockSpec(memory_space=pltpu.VMEM),
        scratch_shapes=[
            pltpu.VMEM((rows, width), jnp.float32),
            pltpu.VMEM((1, rows), jnp.int32),
            pltpu.VMEM((HELD, rows, width), jnp.bfloat16),
            pltpu.VMEM((HELD, 1, rows), jnp.float32),
            pltpu.VMEM((SLOTS, rows, 128), jnp.float32),
            pltpu.VMEM((SLOTS, rows, 128), jnp.float32),
            pltpu.VMEM((HELD, 8, rows), jnp.float32),
            pltpu.VMEM((HELD, 1, rows), jnp.float32),
            pltpu.VMEM((HELD, 1, rows), jnp.float32),
            dma((2,)), dma((SLOTS, chunks)), dma((SLOTS, chunks)), dma((EXTRA, chunks)), dma((EXTRA, chunks)),
            dma((SLOTS,)), dma((SLOTS,)), dma((EXTRA,)), dma((EXTRA,)), dma((HELD,)), dma,
        ],
        compiler_params=pltpu.CompilerParams(
            collective_id=0, has_side_effects=True, vmem_limit_bytes=VMEM_BYTES),
    )(embeddings, cluster_ids.reshape(1, rows))


def solution(mesh):
    return jax.shard_map(
        body,
        mesh=mesh,
        in_specs=(P(("grp", "mem"), None), P(("grp", "mem"), None)),
        out_specs=P(("grp", "mem")),
        check_vma=False,
    )
```

```python
import functools

import jax
import jax.numpy as jnp
from jax import lax
from jax.experimental import pallas as pl
from jax.experimental.pallas import tpu as pltpu
from jax.sharding import PartitionSpec as P

FILL = -4.0
MESH = pl.DeviceIdType.MESH
SIDE = 4
VMEM_BYTES = 64 * 1024 * 1024 - 512 * 1024
DIRS = ((1, 0, 0), (3, 0, 0), (0, 1, 0), (0, 3, 0), (0, 0, 1), (0, 0, 3))

OFFSETS = (
    ((0, 0, 0), (3, 0, 0), (0, 1, 0), (0, 2, 0), (2, 2, 0), (2, 3, 0),
     (3, 3, 0), (0, 0, 1), (1, 0, 1), (0, 0, 2), (1, 0, 2), (0, 0, 3)),
    ((0, 0, 0), (1, 0, 0), (1, 1, 0), (1, 2, 0), (3, 2, 0), (3, 3, 0),
     (0, 3, 0), (1, 0, 1), (2, 0, 1), (1, 0, 2), (2, 0, 2), (1, 0, 3)),
)

SHARED = ((2, 4, 5, 6, 8, 11), (0, 2, 3, 6, 8, 10))

FIRST_SENDS = (
    ((0, 1, 0, 1), (0, 2, 0, 2), (0, 7, 1, 4), (0, 11, 0, 5)),
    ((0, 1, 0, 0), (0, 6, 0, 3)),
)

LAST_SENDS = (
    ((1, 0), (1, 1), (2, 0), (2, 1), (3, 0), (3, 1), (4, 0), (4, 1), (5, 0), (5, 1), (6, 0), (6, 1), (7, 0), (7, 1), (8, 0), (8, 1), (9, 0), (9, 1), (10, 0), (10, 1), (11, 0), (11, 1)),
    ((1, 0), (1, 1), (2, 0), (2, 1), (3, 0), (3, 1), (4, 0), (4, 1), (5, 0), (5, 1), (6, 0), (6, 1), (7, 0), (7, 1), (8, 0), (8, 1), (9, 0), (9, 1), (10, 0), (10, 1), (11, 0), (11, 1)),
)

STEPS = (
    (((('s', 0, 7, 0, 4), ('s', 0, 2, 1, 2), ('s', 0, 1, 1, 1), ('s', 0, 11, 1, 5), ('a', 11, 0), ('a', 2, 0), ('a', 7, 1), ('s', 11, 9, 0, 5), ('a', 1, 0), ('s', 1, 6, 0, 3), ('s', 7, 8, 1, 0), ('a', 2, 1), ('a', 7, 0), ('a', 1, 1)), (2, 7, None, None), (None, None), (2, 7, 0, 0, 7, 1)),
     ((('s', 0, 1, 1, 0), ('s', 0, 6, 1, 3), ('a', 6, 0), ('a', 1, 0), ('s', 6, 5, 0, 1), ('s', 1, 2, 0, 2), ('s', 1, 7, 0, 4), ('t', 0), ('a', 1, 1), ('a', 6, 1)), (1, 6, None, None), (None, None), (0, 1, 12, 1, 6, 0))),
    (((('a', 11, 1), ('s', 1, 6, 1, 3), ('s', 7, 8, 0, 0), ('a', 8, 1)), (1, None, None, None), (None, None), (7, 1, 2, 1, 2, 11)),
     ((('s', 1, 7, 1, 4), ('s', 1, 2, 1, 2), ('s', 1, 11, 0, 5), ('s', 6, 5, 1, 1), ('a', 7, 0), ('a', 5, 0), ('a', 2, 0), ('s', 1, 11, 1, 5), ('s', 5, 4, 0, 3), ('a', 5, 1), ('s', 7, 8, 0, 0)), (5, None, None, None), (None, None), (6, 5, 1, 6, 5, 12))),
    (((('a', 6, 0), ('a', 9, 0), ('s', 2, 3, 0, 2), ('s', 7, 9, 1, 4), ('s', 6, 5, 0, 1), ('a', 8, 0), ('t', 3)), (None, None, None, None), (None, None), (1, 7, 15, 1, 2, 8)),
     ((('t', 1), ('a', 7, 1), ('a', 2, 1)), (None, None, None, None), (None, None), (6, 5, 13, 0, 1, 7))),
    (((), (8, 11, None, None), (None, None), (7, 8, 11, 11, 8, 15)),
     ((), (None, None, None, None), (None, None), (5, 6, 7, 5, 6, 2))),
    (((('a', 6, 1), ('s', 6, 5, 1, 1)), (None, None, None, None), (None, None), (2, 7, 6, 8, 11, 6)),
     ((('s', 5, 4, 1, 3), ('a', 11, 0), ('s', 7, 8, 1, 0), ('s', 2, 3, 0, 2), ('s', 11, 9, 0, 5), ('t', 4)), (7, 2, None, None), (None, None), (7, 2, 12, 0, 1, 16))),
    (((('s', 8, 10, 1, 4), ('t', 2), ('t', 0)), (6, None, None, None), (None, None), (8, 11, 14, 1, 6, 12)),
     ((('a', 11, 1),), (None, None, None, None), (None, None), (0, 5, 11, 6, 7, 11))),
    (((('a', 3, 0), ('a', 5, 0), ('a', 9, 1)), (None, None, None, None), (None, None), (7, 8, 12, 2, 6, 9)),
     ((('a', 8, 0), ('a', 4, 0)), (11, None, None, None), (None, None), (7, 11, 2, 7, 11, 13))),
    (((('t', 5),), (9, None, None, None), (None, None), (11, 9, 12, 1, 7, 17)),
     ((('s', 8, 10, 0, 4), ('s', 11, 9, 1, 5), ('a', 4, 1), ('t', 3)), (4, None, None, None), (None, None), (7, 11, 15, 11, 4, 16))),
    (((('s', 9, 10, 0, 0), ('s', 2, 3, 1, 2), ('s', 5, 4, 0, 3), ('a', 5, 1)), (None, None, None, None), (None, None), (0, 2, 5, 8, 9, 5)),
     ((('a', 8, 1), ('a', 9, 0), ('a', 3, 0)), (8, None, None, None), (None, None), (4, 8, 13, 5, 11, 8))),
    (((), (5, None, None, None), (None, None), (9, 5, 15, 11, 0, 5)),
     ((('s', 2, 3, 1, 2), ('s', 8, 10, 1, 4)), (None, None, None, None), (None, None), (7, 8, 4, 11, 8, 12))),
    (((('s', 5, 4, 1, 3), ('t', 1), ('t', 4)), (None, None, None, None), (None, None), (7, 9, 13, 1, 5, 16)),
     ((('a', 9, 1), ('a', 10, 0)), (None, None, None, None), (11, 12), (2, 4, 9, 5, 6, 9))),
    (((('a', 3, 1),), (3, None, None, None), (None, None), (0, 6, 3, 3, 0, 15)),
     ((), (None, None, None, None), (None, None), (0, 2, 8, 4, 8, 13))),
    (((('a', 10, 1), ('a', 4, 0), ('a', 10, 0)), (None, None, None, None), (6, 15), (5, 3, 17, 7, 8, 3)),
     ((), (9, None, None, None), (2, None), (8, 9, 15, 9, 0, 13))),
    (((), (10, None, None, None), (5, 17), (11, 3, 13, 9, 10, 3)),
     ((('t', 2),), (None, None, None, None), (13, None), (1, 7, 14, 9, 0, 14))),
    (((('a', 4, 1),), (None, None, None, None), (None, None), (9, 10, 14, 10, 0, 12)),
     ((('a', 10, 1),), (None, None, None, None), (14, None), (0, 4, 10, 5, 0, 10))),
    (((), (None, None, None, None), (14, 12), (1, 2, 10, 11, 3, 16)),
     ((('a', 3, 1), ('t', 5)), (3, None, None, None), (5, None), (0, 3, 17, 1, 4, 3))),
    (((), (None, None, None, None), (1, 2), (10, 0, 13, 3, 7, 4)),
     ((), (10, None, None, None), (0, 17), (6, 7, 3, 10, 3, 15))),
    (((), (4, None, None, None), (11, 10), (4, 0, 16, 8, 9, 4)),
     ((), (None, None, None, None), (1, 4), (9, 3, 16, 8, 9, 3))),
)

TAIL = (
    (13, 3, 7, 0, 16, 8, 9, 4),
    (6, 7, 10, 15, 16, 8, 9, 3),
)

SLOTS = len(OFFSETS[0])
EXTRA = len(SHARED[0])
HELD = SLOTS + EXTRA
NONE = 31


def words(values, bits=5):
    each = 30 // bits
    return [sum(v << (bits * k) for k, v in enumerate(values[s:s + each])) for s in range(0, len(values), each)]


def lookup(packed, n, bits=5):
    each = 30 // bits
    word = packed[0]
    for k, w in enumerate(packed[1:], 1):
        word = jnp.where(n >= each * k, w, word)
    return lax.rem(lax.shift_right_logical(word, bits * lax.rem(n, each)), 1 << bits)


def of_core(core, lists, bits=5):
    return [jnp.where(core == 0, jnp.int32(a), jnp.int32(b)) for a, b in zip(*(words(v, bits) for v in lists))]


def column(which, place, k):
    return [NONE if pair[which][place][k] is None else pair[which][place][k] for pair in STEPS]


def kernel(chunks, emb_ref, lab_ref, out_ref, emb, ids, buf, labels, label_rows, row_best, column_best, outgoing,
           incoming, load_sem, send_sem, recv_sem, give_sem, take_sem, label_send, label_recv, label_give,
           label_take, result_send, result_recv):
    rows, width = emb.shape
    part = rows // chunks
    load = pltpu.make_async_copy(emb_ref, emb, load_sem.at[0])
    load.start()
    load_ids = pltpu.make_async_copy(lab_ref, ids, load_sem.at[1])
    load_ids.start()
    gx = lax.axis_index("grp")
    mem = lax.axis_index("mem")
    core = lax.rem(mem, 2)
    other = 1 - core
    gy = lax.rem(mem // 2, SIDE)
    gz = mem // (2 * SIDE)

    def at(offset, on):
        x, y, z = (lax.rem(g + k, SIDE) for g, k in zip((gx, gy, gz), offset))
        return (x, (z * SIDE + y) * 2 + on)

    barrier = pltpu.get_barrier_semaphore()
    for direction in DIRS:
        pl.semaphore_signal(barrier, inc=1, device_id=at(direction, core), device_id_type=MESH)
    pl.semaphore_signal(barrier, inc=1, device_id=at((0, 0, 0), other), device_id_type=MESH)

    def chunk_of(slot, h):
        return buf.at[slot, pl.ds(h * part, part)]

    def relay(source, target, h, direction):
        return pltpu.make_async_remote_copy(
            src_ref=chunk_of(source, h), dst_ref=chunk_of(target, h),
            send_sem=send_sem.at[target, h], recv_sem=recv_sem.at[target, h],
            device_id=at(DIRS[direction], core), device_id_type=MESH)

    def relay_label(source, target, direction):
        return pltpu.make_async_remote_copy(
            src_ref=labels.at[source], dst_ref=labels.at[target],
            send_sem=label_send.at[target], recv_sem=label_recv.at[target],
            device_id=at(DIRS[direction], core), device_id_type=MESH)

    def send(source, target, h, direction):
        if h == 0:
            relay_label(source, target, direction).start()
        relay(source, target, h, direction).start()

    def share(slot, k, h):
        return pltpu.make_async_remote_copy(
            src_ref=chunk_of(slot, h), dst_ref=chunk_of(SLOTS + k, h),
            send_sem=give_sem.at[k, h], recv_sem=take_sem.at[k, h],
            device_id=at((0, 0, 0), other), device_id_type=MESH)

    def share_label(slot, k):
        return pltpu.make_async_remote_copy(
            src_ref=labels.at[slot], dst_ref=labels.at[SLOTS + k],
            send_sem=label_give.at[k], recv_sem=label_take.at[k],
            device_id=at((0, 0, 0), other), device_id_type=MESH)

    def give(which, slot, h):
        if slot in SHARED[1 - which]:
            k = SHARED[1 - which].index(slot)
            if h == 0:
                share_label(slot, k).start()
            share(slot, k, h).start()

    load_ids.wait()
    labels[0] = ids[...].astype(jnp.float32)
    load.wait()
    for h in range(chunks):
        e = emb[pl.ds(h * part, part)]
        squares = jnp.sum(e * e, axis=1, keepdims=True)
        buf[0, pl.ds(h * part, part)] = (e * lax.rsqrt(squares + 1e-06)).astype(jnp.bfloat16)
        if h == 0:
            pl.semaphore_wait(barrier, len(DIRS) + 1)
        for which in (0, 1):
            @pl.when(core == which)
            def _(which=which, h=h):
                for move in FIRST_SENDS[which]:
                    if move[2] == h:
                        send(*move)

    for which in (0, 1):
        @pl.when(core == which)
        def _(which=which):
            for h in range(chunks):
                give(which, 0, h)

    def clear(slot, carry):
        column_best[slot] = jnp.full(column_best.shape[1:], FILL, jnp.float32)

        @pl.when(slot < SLOTS)
        def _():
            row_best[slot] = jnp.full(row_best.shape[1:], FILL, jnp.float32)
        return carry

    lax.fori_loop(0, HELD, clear, 0)

    def spread(slot):
        label_rows[slot] = jnp.broadcast_to(labels[slot], (128, rows)).T

    def tile(left, right, own=False):
        sims = lax.dot_general(jnp.concatenate([buf[a] for a in left], axis=0), buf[right], (((1,), (1,)), ((), ())),
                               preferred_element_type=jnp.float32)
        names = labels[right]
        tops = [row_best[a] for a in left]
        for k in range(rows // 128):
            lanes = slice(k * 128, (k + 1) * 128)
            high = column_best[right, :, lanes]
            for n, a in enumerate(left):
                keep = label_rows[a] == names[:, lanes]
                if own:
                    keep = keep & (lax.broadcasted_iota(jnp.int32, (rows, 128), 0)
                                   != lax.broadcasted_iota(jnp.int32, (rows, 128), 1) + k * 128)
                scores = jnp.where(keep, sims[n * rows:(n + 1) * rows, lanes], FILL)
                tops[n] = jnp.maximum(tops[n], scores)
                high = jnp.maximum(high, jnp.max(scores.reshape(rows // 8, 8, 128), axis=0))
            column_best[right, :, lanes] = high
        for n, a in enumerate(left):
            row_best[a] = tops[n]

    def answer(slot):
        offsets = [OFFSETS[w] + tuple(OFFSETS[1 - w][k] for k in SHARED[w]) for w in (0, 1)]
        back = [SIDE - lookup(of_core(core, [[o[k] for o in held] for held in offsets], 2), slot, 2) for k in range(3)]
        return pltpu.make_async_remote_copy(
            src_ref=outgoing.at[slot], dst_ref=incoming.at[slot],
            send_sem=result_send.at[slot], recv_sem=result_recv,
            device_id=at(back, jnp.where(slot < SLOTS, core, other)), device_id_type=MESH)

    def finish(slot):
        by_column = jnp.max(column_best[slot], axis=0, keepdims=True)

        @pl.when(slot < SLOTS)
        def _():
            outgoing[slot] = jnp.maximum(by_column, jnp.max(row_best[slot].T, axis=0, keepdims=True))

        @pl.when(slot >= SLOTS)
        def _():
            outgoing[slot] = by_column

        @pl.when(slot > 0)
        def _():
            answer(slot).start()

        @pl.when(slot == 0)
        def _():
            incoming[0] = outgoing[0]

    def arrived(which, slot, h):
        pltpu.make_async_copy(chunk_of(slot, h), chunk_of(slot, h), recv_sem.at[slot, h]).wait()
        if h == 0:
            pltpu.make_async_copy(labels.at[slot], labels.at[slot], label_recv.at[slot]).wait()
        give(which, slot, h)

    def taken(k):
        for h in range(chunks):
            pltpu.make_async_copy(chunk_of(SLOTS + k, h), chunk_of(SLOTS + k, h), take_sem.at[k, h]).wait()
        pltpu.make_async_copy(labels.at[SLOTS + k], labels.at[SLOTS + k], label_take.at[k]).wait()

    def sent(slot, h):
        relay(0, slot, h, 0).wait_send()

    def moves(n):
        for which in (0, 1):
            todo = STEPS[n][which][0]
            if todo:
                @pl.when(core == which)
                def _(which=which, todo=todo):
                    for op in todo:
                        if op[0] == "a":
                            arrived(which, *op[1:])
                        elif op[0] == "t":
                            taken(op[1])
                        else:
                            if len(op) > 5:
                                sent(*op[5:])
                            send(*op[1:5])

    def table(place):
        return [of_core(core, [column(w, place, k) for w in (0, 1)]) for k in range(len(STEPS[0][0][place]))]

    to_open, to_finish, to_compare = table(1), table(2), table(3)
    spread(0)
    tile((0,), 0, own=True)

    def step(n, carry):
        for g in range(0, len(STEPS), 6):
            @pl.when(lax.div(n, 6) == g // 6)
            def _(g=g):
                for k in range(g, min(g + 6, len(STEPS))):
                    @pl.when(n == k)
                    def _(k=k):
                        moves(k)
        for listed, act in ((to_open, spread), (to_finish, finish)):
            for packed in listed:
                slot = lookup(packed, n)

                @pl.when(slot != NONE)
                def _(slot=slot, act=act):
                    act(slot)
        units = [lookup(packed, n) for packed in to_compare]
        for k in range(0, len(units), 3):
            tile(units[k:k + 2], units[k + 2])
        return carry

    lax.fori_loop(0, len(STEPS), step, 0)
    left = max(len(t) for t in TAIL)
    ends = of_core(core, [(list(t) + [NONE] * left)[:left] for t in TAIL])

    def last(n, carry):
        ended = lookup(ends, n)

        @pl.when(ended != NONE)
        def _():
            finish(ended)
        return carry

    lax.fori_loop(0, left, last, 0)

    for which in (0, 1):
        @pl.when(core == which)
        def _(which=which):
            for move in LAST_SENDS[which]:
                sent(*move)
    for k in range(EXTRA):
        for h in range(chunks):
            share(0, k, h).wait_send()
        share_label(0, k).wait_send()
    for slot in range(1, SLOTS):
        relay_label(0, slot, 0).wait_send()
    for slot in range(1, HELD):
        answer(slot).wait_send()
    rest = incoming.at[pl.ds(1, HELD - 1)]
    pltpu.make_async_copy(rest, rest, result_recv).wait()
    out_ref[...] = jnp.max(incoming[...], axis=0).reshape(rows)


def body(embeddings, cluster_ids):
    rows, width = embeddings.shape
    chunks = 1 + max(h for sends in LAST_SENDS for _, h in sends)
    dma = pltpu.SemaphoreType.DMA
    return pl.pallas_call(
        functools.partial(kernel, chunks),
        out_shape=jax.ShapeDtypeStruct((rows,), jnp.float32),
        in_specs=[pl.BlockSpec(memory_space=pl.ANY), pl.BlockSpec(memory_space=pl.ANY)],
        out_specs=pl.BlockSpec(memory_space=pltpu.VMEM),
        scratch_shapes=[
            pltpu.VMEM((rows, width), jnp.float32),
            pltpu.VMEM((1, rows), jnp.int32),
            pltpu.VMEM((HELD, rows, width), jnp.bfloat16),
            pltpu.VMEM((HELD, 1, rows), jnp.float32),
            pltpu.VMEM((SLOTS, rows, 128), jnp.float32),
            pltpu.VMEM((SLOTS, rows, 128), jnp.float32),
            pltpu.VMEM((HELD, 8, rows), jnp.float32),
            pltpu.VMEM((HELD, 1, rows), jnp.float32),
            pltpu.VMEM((HELD, 1, rows), jnp.float32),
            dma((2,)), dma((SLOTS, chunks)), dma((SLOTS, chunks)), dma((EXTRA, chunks)), dma((EXTRA, chunks)),
            dma((SLOTS,)), dma((SLOTS,)), dma((EXTRA,)), dma((EXTRA,)), dma((HELD,)), dma,
        ],
        compiler_params=pltpu.CompilerParams(
            collective_id=0, has_side_effects=True, vmem_limit_bytes=VMEM_BYTES),
    )(embeddings, cluster_ids.reshape(1, rows))


def solution(mesh):
    return jax.shard_map(
        body,
        mesh=mesh,
        in_specs=(P(("grp", "mem"), None), P(("grp", "mem"), None)),
        out_specs=P(("grp", "mem")),
        check_vma=False,
    )
```

```python
import functools

import jax
import jax.numpy as jnp
from jax import lax
from jax.experimental import pallas as pl
from jax.experimental.pallas import tpu as pltpu
from jax.sharding import PartitionSpec as P

FILL = -4.0
MESH = pl.DeviceIdType.MESH
SIDE = 4
VMEM_BYTES = 64 * 1024 * 1024 - 512 * 1024
DIRS = ((1, 0, 0), (3, 0, 0), (0, 1, 0), (0, 3, 0), (0, 0, 1), (0, 0, 3))

OFFSETS = (
    ((0, 0, 0), (3, 0, 0), (0, 1, 0), (0, 2, 0), (2, 2, 0), (2, 3, 0),
     (3, 3, 0), (0, 0, 1), (1, 0, 1), (0, 0, 2), (1, 0, 2), (0, 0, 3)),
    ((0, 0, 0), (1, 0, 0), (1, 1, 0), (1, 2, 0), (3, 2, 0), (3, 3, 0),
     (0, 3, 0), (1, 0, 1), (2, 0, 1), (1, 0, 2), (2, 0, 2), (1, 0, 3)),
)

SHARED = ((2, 4, 5, 6, 8, 11), (0, 2, 3, 6, 8, 10))

FIRST_SENDS = (
    ((0, 1, 0, 1), (0, 2, 0, 2), (0, 7, 1, 4), (0, 11, 0, 5)),
    ((0, 1, 0, 0), (0, 6, 0, 3)),
)

LAST_SENDS = (
    ((1, 0), (1, 1), (2, 0), (2, 1), (3, 0), (3, 1), (4, 0), (4, 1), (5, 0), (5, 1), (6, 0), (6, 1), (7, 0), (7, 1), (8, 0), (8, 1), (9, 0), (9, 1), (10, 0), (10, 1), (11, 0), (11, 1)),
    ((1, 0), (1, 1), (2, 0), (2, 1), (3, 0), (3, 1), (4, 0), (4, 1), (5, 0), (5, 1), (6, 0), (6, 1), (7, 0), (7, 1), (8, 0), (8, 1), (9, 0), (9, 1), (10, 0), (10, 1), (11, 0), (11, 1)),
)

STEPS = (
    (((('s', 0, 7, 0, 4), ('s', 0, 2, 1, 2), ('s', 0, 1, 1, 1), ('s', 0, 11, 1, 5), ('a', 2, 0), ('a', 7, 1), ('a', 11, 0), ('s', 11, 9, 0, 5), ('a', 1, 0), ('s', 1, 6, 0, 3), ('s', 7, 8, 1, 0), ('a', 2, 1), ('a', 7, 0), ('a', 1, 1)), (2, 7, None, None), (None, None, None), (2, 7, 0, 0, 7, 1)),
     ((('s', 0, 6, 1, 3), ('s', 0, 1, 1, 0), ('a', 6, 0), ('a', 1, 0), ('s', 6, 5, 0, 1), ('s', 1, 2, 0, 2), ('s', 1, 7, 0, 4), ('t', 0), ('a', 1, 1), ('a', 6, 1)), (1, 6, None, None), (None, None, None), (0, 1, 12, 1, 6, 0))),
    (((('a', 11, 1), ('s', 7, 8, 0, 0), ('s', 1, 6, 1, 3), ('t', 3), ('a', 8, 1)), (1, None, None, None), (None, None, None), (7, 1, 2, 1, 2, 11)),
     ((('s', 1, 7, 1, 4), ('s', 1, 2, 1, 2), ('s', 1, 11, 0, 5), ('s', 6, 5, 1, 1), ('a', 7, 0), ('a', 5, 0), ('a', 2, 0), ('s', 5, 4, 0, 3), ('s', 1, 11, 1, 5), ('a', 5, 1), ('s', 7, 8, 0, 0)), (5, None, None, None), (None, None, None), (6, 5, 1, 6, 5, 12))),
    (((('a', 6, 0), ('s', 2, 3, 0, 2), ('s', 6, 5, 0, 1), ('s', 7, 9, 1, 4), ('a', 8, 0)), (None, None, None, None), (None, None, None), (1, 7, 15, 1, 2, 8)),
     ((('t', 1), ('a', 7, 1), ('a', 2, 1)), (None, None, None, None), (None, None, None), (6, 5, 13, 0, 1, 7))),
    (((), (8, 11, None, None), (None, None, None), (7, 8, 11, 11, 8, 15)),
     ((), (None, None, None, None), (None, None, None), (5, 6, 7, 5, 6, 2))),
    (((('a', 6, 1), ('s', 6, 5, 1, 1), ('s', 8, 10, 1, 4), ('t', 2)), (None, None, None, None), (None, None, None), (2, 7, 6, 8, 11, 6)),
     ((('s', 5, 4, 1, 3), ('a', 11, 0), ('s', 7, 8, 1, 0), ('s', 2, 3, 0, 2), ('s', 11, 9, 0, 5), ('t', 4)), (7, 2, None, None), (None, None, None), (7, 2, 12, 0, 1, 16))),
    (((('t', 0),), (6, None, None, None), (None, None, None), (8, 11, 14, 1, 6, 12)),
     ((('a', 11, 1),), (None, None, None, None), (None, None, None), (0, 5, 11, 6, 7, 11))),
    (((('a', 3, 0), ('a', 9, 0), ('a', 5, 0), ('a', 9, 1)), (None, None, None, None), (None, None, None), (7, 8, 12, 2, 6, 9)),
     ((('a', 8, 0), ('a', 4, 0)), (11, None, None, None), (None, None, None), (7, 11, 2, 7, 11, 13))),
    (((('t', 5),), (9, None, None, None), (None, None, None), (11, 9, 12, 1, 7, 17)),
     ((('s', 8, 10, 0, 4), ('s', 11, 9, 1, 5), ('a', 4, 1), ('t', 3)), (4, None, None, None), (None, None, None), (7, 11, 15, 11, 4, 16))),
    (((('s', 9, 10, 0, 0), ('s', 2, 3, 1, 2), ('s', 5, 4, 0, 3), ('a', 5, 1)), (None, None, None, None), (None, None, None), (0, 2, 5, 8, 9, 5)),
     ((('a', 8, 1), ('a', 9, 0), ('a', 3, 0)), (8, None, None, None), (None, None, None), (4, 8, 13, 5, 11, 8))),
    (((), (5, None, None, None), (None, None, None), (9, 5, 15, 11, 0, 5)),
     ((('s', 2, 3, 1, 2), ('s', 8, 10, 1, 4)), (None, None, None, None), (None, None, None), (7, 8, 4, 11, 8, 12))),
    (((('s', 5, 4, 1, 3), ('t', 1), ('t', 4)), (None, None, None, None), (None, None, None), (7, 9, 13, 1, 5, 16)),
     ((('a', 9, 1),), (None, None, None, None), (11, 12, None), (2, 4, 9, 5, 6, 9))),
    (((('a', 3, 1),), (3, None, None, None), (None, None, None), (0, 6, 3, 3, 0, 15)),
     ((('a', 10, 0),), (None, None, None, None), (None, None, None), (0, 2, 8, 4, 8, 13))),
    (((('a', 10, 1), ('a', 4, 0), ('a', 10, 0)), (10, None, None, None), (6, 15, None), (9, 10, 14, 10, 0, 12)),
     ((), (9, None, None, None), (2, None, None), (8, 9, 15, 9, 0, 13))),
    (((), (None, None, None, None), (14, 12, None), (5, 3, 17, 7, 8, 3)),
     ((('t', 2),), (None, None, None, None), (13, None, None), (1, 7, 14, 9, 0, 14))),
    (((), (None, None, None, None), (5, 17, None), (11, 3, 13, 9, 10, 3)),
     ((('a', 10, 1),), (None, None, None, None), (14, None, None), (0, 4, 10, 5, 0, 10))),
    (((('a', 4, 1),), (None, None, None, None), (None, None, None), (1, 2, 10, 11, 3, 16)),
     ((('a', 3, 1), ('t', 5)), (3, None, None, None), (5, None, None), (0, 3, 17, 1, 4, 3))),
    (((), (None, None, None, None), (1, 2, 11), (10, 0, 13, 3, 7, 4)),
     ((), (10, None, None, None), (0, 17, 1), (6, 7, 3, 10, 3, 15))),
    (((), (4, None, None, None), (10, 13, 3), (4, 0, 16, 8, 9, 4)),
     ((), (None, None, None, None), (4, 6, 7), (9, 3, 16, 8, 9, 3))),
)

TAIL = (
    (7, 0, 16, 8, 9, 4),
    (10, 15, 16, 8, 9, 3),
)

SLOTS = len(OFFSETS[0])
EXTRA = len(SHARED[0])
HELD = SLOTS + EXTRA
NONE = 31


def words(values, bits=5):
    each = 30 // bits
    return [sum(v * (1 << bits * k) for k, v in enumerate(values[s:s + each])) for s in range(0, len(values), each)]


def lookup(packed, n, bits=5):
    each = 30 // bits
    word = packed[0]
    for k, w in enumerate(packed[1:], 1):
        word = jnp.where(n >= each * k, w, word)
    return lax.rem(lax.shift_right_logical(word, bits * lax.rem(n, each)), 1 << bits)


def of_core(core, lists, bits=5):
    return [jnp.where(core == 0, jnp.asarray(a, jnp.int32), jnp.asarray(b, jnp.int32))
            for a, b in zip(*(words(v, bits) for v in lists))]


def column(which, place, k):
    return [NONE if pair[which][place][k] is None else pair[which][place][k] for pair in STEPS]


def kernel(chunks, emb_ref, lab_ref, out_ref, emb, ids, buf, labels, label_rows, row_best, column_best, outgoing,
           incoming, load_sem, send_sem, recv_sem, give_sem, take_sem, label_send, label_recv, label_give,
           label_take, result_send, result_recv):
    rows, width = emb.shape
    part = rows // chunks
    load = pltpu.make_async_copy(emb_ref, emb, load_sem.at[0])
    load.start()
    load_ids = pltpu.make_async_copy(lab_ref, ids, load_sem.at[1])
    load_ids.start()
    gx = lax.axis_index("grp")
    mem = lax.axis_index("mem")
    core = lax.rem(mem, 2)
    other = 1 - core
    gy = lax.rem(mem // 2, SIDE)
    gz = mem // (2 * SIDE)

    def at(offset, on):
        x, y, z = (lax.rem(g + k, SIDE) for g, k in zip((gx, gy, gz), offset))
        return (x, (z * SIDE + y) * 2 + on)

    barrier = pltpu.get_barrier_semaphore()
    for direction in DIRS:
        pl.semaphore_signal(barrier, inc=1, device_id=at(direction, core), device_id_type=MESH)
    pl.semaphore_signal(barrier, inc=1, device_id=at((0, 0, 0), other), device_id_type=MESH)

    def chunk_of(slot, h):
        return buf.at[slot, pl.ds(h * part, part)]

    def relay(source, target, h, direction):
        return pltpu.make_async_remote_copy(
            src_ref=chunk_of(source, h), dst_ref=chunk_of(target, h),
            send_sem=send_sem.at[target, h], recv_sem=recv_sem.at[target, h],
            device_id=at(DIRS[direction], core), device_id_type=MESH)

    def relay_label(source, target, direction):
        return pltpu.make_async_remote_copy(
            src_ref=labels.at[source], dst_ref=labels.at[target],
            send_sem=label_send.at[target], recv_sem=label_recv.at[target],
            device_id=at(DIRS[direction], core), device_id_type=MESH)

    def send(source, target, h, direction):
        if h == 0:
            relay_label(source, target, direction).start()
        relay(source, target, h, direction).start()

    def share(slot, k, h):
        return pltpu.make_async_remote_copy(
            src_ref=chunk_of(slot, h), dst_ref=chunk_of(SLOTS + k, h),
            send_sem=give_sem.at[k, h], recv_sem=take_sem.at[k, h],
            device_id=at((0, 0, 0), other), device_id_type=MESH)

    def share_label(slot, k):
        return pltpu.make_async_remote_copy(
            src_ref=labels.at[slot], dst_ref=labels.at[SLOTS + k],
            send_sem=label_give.at[k], recv_sem=label_take.at[k],
            device_id=at((0, 0, 0), other), device_id_type=MESH)

    def give(which, slot, h):
        if slot in SHARED[1 - which]:
            k = SHARED[1 - which].index(slot)
            if h == 0:
                share_label(slot, k).start()
            share(slot, k, h).start()

    homes = []
    for which in (0, 1):
        offsets = OFFSETS[which] + tuple(OFFSETS[1 - which][k] for k in SHARED[which])
        homes.append([at([SIDE - k for k in o], which if n < SLOTS else 1 - which) for n, o in enumerate(offsets)])
    home_x, home_mem = (of_core(core, [[h[k] for h in held] for held in homes]) for k in (0, 1))

    load_ids.wait()
    labels[0] = ids[...].astype(jnp.float32)
    load.wait()
    for h in range(chunks):
        e = emb[pl.ds(h * part, part)]
        squares = jnp.sum(e * e, axis=1, keepdims=True)
        buf[0, pl.ds(h * part, part)] = (e * lax.rsqrt(squares + 1e-06)).astype(jnp.bfloat16)
        if h == 0:
            pl.semaphore_wait(barrier, len(DIRS) + 1)
        for which in (0, 1):
            @pl.when(core == which)
            def _(which=which, h=h):
                for move in FIRST_SENDS[which]:
                    if move[2] == h:
                        send(*move)

    for which in (0, 1):
        @pl.when(core == which)
        def _(which=which):
            for h in range(chunks):
                give(which, 0, h)

    def clear(slot, carry):
        column_best[slot] = jnp.full(column_best.shape[1:], FILL, jnp.float32)

        @pl.when(slot < SLOTS)
        def _():
            row_best[slot] = jnp.full(row_best.shape[1:], FILL, jnp.float32)
        return carry

    lax.fori_loop(0, HELD, clear, 0)

    def spread(slot):
        label_rows[slot] = jnp.broadcast_to(labels[slot], (128, rows)).T

    def tile(left, right, own=False):
        sims = lax.dot_general(jnp.concatenate([buf[a] for a in left], axis=0), buf[right], (((1,), (1,)), ((), ())),
                               preferred_element_type=jnp.float32)
        names = labels[right]
        tops = [row_best[a] for a in left]
        for k in range(rows // 128):
            lanes = slice(k * 128, (k + 1) * 128)
            high = column_best[right, :, lanes]
            for n, a in enumerate(left):
                keep = label_rows[a] == names[:, lanes]
                if own:
                    keep = keep & (lax.broadcasted_iota(jnp.int32, (rows, 128), 0)
                                   != lax.broadcasted_iota(jnp.int32, (rows, 128), 1) + k * 128)
                scores = jnp.where(keep, sims[n * rows:(n + 1) * rows, lanes], FILL)
                tops[n] = jnp.maximum(tops[n], scores)
                high = jnp.maximum(high, jnp.max(scores.reshape(rows // 8, 8, 128), axis=0))
            column_best[right, :, lanes] = high
        for n, a in enumerate(left):
            row_best[a] = tops[n]

    def answer(slot):
        return pltpu.make_async_remote_copy(
            src_ref=outgoing.at[slot], dst_ref=incoming.at[slot],
            send_sem=result_send.at[slot], recv_sem=result_recv,
            device_id=(lookup(home_x, slot), lookup(home_mem, slot)), device_id_type=MESH)

    def finish(slot):
        by_column = jnp.max(column_best[slot], axis=0, keepdims=True)

        @pl.when(slot < SLOTS)
        def _():
            outgoing[slot] = jnp.maximum(by_column, jnp.max(row_best[slot].T, axis=0, keepdims=True))

        @pl.when(slot >= SLOTS)
        def _():
            outgoing[slot] = by_column

        @pl.when(slot > 0)
        def _():
            answer(slot).start()

    def arrived(which, slot, h):
        pltpu.make_async_copy(chunk_of(slot, h), chunk_of(slot, h), recv_sem.at[slot, h]).wait()
        if h == 0:
            pltpu.make_async_copy(labels.at[slot], labels.at[slot], label_recv.at[slot]).wait()
        give(which, slot, h)

    def taken(k):
        for h in range(chunks):
            pltpu.make_async_copy(chunk_of(SLOTS + k, h), chunk_of(SLOTS + k, h), take_sem.at[k, h]).wait()
        pltpu.make_async_copy(labels.at[SLOTS + k], labels.at[SLOTS + k], label_take.at[k]).wait()

    def sent(slot, h):
        relay(0, slot, h, 0).wait_send()

    def moves(n):
        for which in (0, 1):
            todo = STEPS[n][which][0]
            if todo:
                @pl.when(core == which)
                def _(which=which, todo=todo):
                    for op in todo:
                        if op[0] == "a":
                            arrived(which, *op[1:])
                        elif op[0] == "t":
                            taken(op[1])
                        else:
                            if len(op) > 5:
                                sent(*op[5:])
                            send(*op[1:5])

    def table(place):
        return [of_core(core, [column(w, place, k) for w in (0, 1)]) for k in range(len(STEPS[0][0][place]))]

    to_open, to_finish, to_compare = table(1), table(2), table(3)
    spread(0)
    tile((0,), 0, own=True)

    def step(n, carry):
        for g in range(0, len(STEPS), 6):
            @pl.when(lax.div(n, 6) == g // 6)
            def _(g=g):
                for k in range(g, min(g + 6, len(STEPS))):
                    @pl.when(n == k)
                    def _(k=k):
                        moves(k)
        for listed, act in ((to_open, spread), (to_finish, finish)):
            for packed in listed:
                slot = lookup(packed, n)

                @pl.when(slot != NONE)
                def _(slot=slot, act=act):
                    act(slot)
        units = [lookup(packed, n) for packed in to_compare]
        for k in range(0, len(units), 3):
            tile(units[k:k + 2], units[k + 2])
        return carry

    lax.fori_loop(0, len(STEPS), step, 0)
    left = max(len(t) for t in TAIL)
    ends = of_core(core, [(list(t) + [NONE] * left)[:left] for t in TAIL])
    ended = [lookup(ends, n) for n in range(left)]
    for slot in ended:
        held = jnp.where(slot == NONE, 0, slot)
        by_row = jnp.max(row_best[jnp.minimum(held, SLOTS - 1)].T, axis=0, keepdims=True)
        by_column = jnp.max(column_best[held], axis=0, keepdims=True)
        outgoing[held] = jnp.where(held < SLOTS, jnp.maximum(by_row, by_column), by_column)
    for slot in ended:
        @pl.when((slot != NONE) & (slot > 0))
        def _(slot=slot):
            answer(slot).start()
    incoming[0] = outgoing[0]

    for which in (0, 1):
        @pl.when(core == which)
        def _(which=which):
            for move in LAST_SENDS[which]:
                sent(*move)
    for k in range(EXTRA):
        for h in range(chunks):
            share(0, k, h).wait_send()
        share_label(0, k).wait_send()
    for slot in range(1, SLOTS):
        relay_label(0, slot, 0).wait_send()
    for slot in range(1, HELD):
        answer(slot).wait_send()
    rest = incoming.at[pl.ds(1, HELD - 1)]
    pltpu.make_async_copy(rest, rest, result_recv).wait()
    out_ref[...] = jnp.max(incoming[...], axis=0).reshape(rows)


def body(embeddings, cluster_ids):
    rows, width = embeddings.shape
    chunks = 1 + max(h for sends in LAST_SENDS for _, h in sends)
    dma = pltpu.SemaphoreType.DMA
    return pl.pallas_call(
        functools.partial(kernel, chunks),
        out_shape=jax.ShapeDtypeStruct((rows,), jnp.float32),
        in_specs=[pl.BlockSpec(memory_space=pl.ANY), pl.BlockSpec(memory_space=pl.ANY)],
        out_specs=pl.BlockSpec(memory_space=pltpu.VMEM),
        scratch_shapes=[
            pltpu.VMEM((rows, width), jnp.float32),
            pltpu.VMEM((1, rows), jnp.int32),
            pltpu.VMEM((HELD, rows, width), jnp.bfloat16),
            pltpu.VMEM((HELD, 1, rows), jnp.float32),
            pltpu.VMEM((SLOTS, rows, 128), jnp.float32),
            pltpu.VMEM((SLOTS, rows, 128), jnp.float32),
            pltpu.VMEM((HELD, 8, rows), jnp.float32),
            pltpu.VMEM((HELD, 1, rows), jnp.float32),
            pltpu.VMEM((HELD, 1, rows), jnp.float32),
            dma((2,)), dma((SLOTS, chunks)), dma((SLOTS, chunks)), dma((EXTRA, chunks)), dma((EXTRA, chunks)),
            dma((SLOTS,)), dma((SLOTS,)), dma((EXTRA,)), dma((EXTRA,)), dma((HELD,)), dma,
        ],
        compiler_params=pltpu.CompilerParams(
            collective_id=0, has_side_effects=True, vmem_limit_bytes=VMEM_BYTES),
    )(embeddings, cluster_ids.reshape(1, rows))


def solution(mesh):
    return jax.shard_map(
        body,
        mesh=mesh,
        in_specs=(P(("grp", "mem"), None), P(("grp", "mem"), None)),
        out_specs=P(("grp", "mem")),
        check_vma=False,
    )
```

```python
import functools

import jax
import jax.numpy as jnp
from jax import lax
from jax.experimental import pallas as pl
from jax.experimental.pallas import tpu as pltpu
from jax.sharding import PartitionSpec as P

FILL = -4.0
MESH = pl.DeviceIdType.MESH
SIDE = 4
VMEM_BYTES = 64 * 1024 * 1024 - 512 * 1024
DIRS = ((1, 0, 0), (3, 0, 0), (0, 1, 0), (0, 3, 0), (0, 0, 1), (0, 0, 3))

OFFSETS = (
    ((0, 0, 0), (0, 1, 0), (2, 1, 0), (3, 1, 0), (1, 3, 0), (2, 3, 0),
     (1, 0, 0), (0, 1, 1), (0, 1, 2), (0, 2, 2), (0, 1, 3), (0, 2, 3)),
    ((0, 0, 0), (2, 0, 0), (3, 0, 0), (1, 2, 0), (2, 2, 0), (0, 3, 0),
     (1, 3, 0), (0, 0, 1), (0, 0, 2), (0, 1, 2), (0, 0, 3), (0, 1, 3)),
)

SHARED = ((0, 2, 6, 7, 9, 11), (3, 5, 6, 7, 8, 11))

FIRST_SENDS = (
    ((0, 1, 0, 2), (0, 6, 0, 0)),
    ((0, 5, 0, 3), (0, 10, 0, 5), (0, 7, 1, 4), (0, 2, 0, 1)),
)

LAST_SENDS = (
    ((2, 3), (4, 3), (5, 3), (8, 3), (9, 2), (9, 3)),
    ((1, 3), (3, 3), (4, 3), (8, 2), (9, 2), (9, 3)),
)

STEPS = (
    (((('s', 0, 1, 1, 2, 1, 0), ('s', 0, 6, 1, 0, 6, 0), ('a', 1, 0), ('a', 6, 0), ('s', 1, 10, 0, 5), ('s', 1, 3, 0, 1), ('s', 6, 4, 0, 3), ('s', 1, 7, 0, 4), ('s', 0, 1, 2, 2, 1, 1), ('s', 0, 6, 2, 0, 6, 1), ('a', 1, 1), ('a', 6, 1), ('s', 1, 10, 1, 5, 10, 0), ('s', 1, 3, 1, 1, 3, 0), ('s', 6, 4, 1, 3, 4, 0), ('s', 1, 7, 1, 4, 7, 0), ('s', 0, 1, 3, 2, 1, 2), ('s', 0, 6, 3, 0, 6, 2), ('a', 3, 0), ('a', 4, 0), ('a', 7, 0), ('a', 10, 0), ('a', 1, 2), ('a', 6, 2), ('s', 1, 10, 2, 5, 10, 1), ('s', 1, 3, 2, 1, 3, 1), ('s', 6, 4, 2, 3, 4, 1), ('s', 1, 7, 2, 4, 7, 1), ('s', 4, 5, 0, 0, 6, 3), ('s', 10, 11, 0, 2, 1, 3), ('a', 3, 1), ('a', 4, 1), ('a', 7, 1), ('a', 10, 1), ('a', 1, 3), ('a', 6, 3), ('t', 0)), (1, 6, None, None), (None, None, None), (0, 1, 12, 1, 6, 0)),
     ((('s', 0, 5, 1, 3, 5, 0), ('s', 0, 10, 2, 5, 10, 0), ('s', 0, 7, 3, 4, 7, 1), ('s', 0, 2, 1, 1, 2, 0), ('a', 2, 0), ('a', 5, 0), ('a', 7, 1), ('a', 10, 0), ('s', 5, 6, 0, 0), ('s', 10, 11, 0, 2), ('s', 0, 5, 2, 3, 5, 1), ('s', 0, 7, 0, 4, 7, 3), ('s', 0, 10, 1, 5, 10, 2), ('s', 0, 2, 2, 1, 2, 1), ('a', 2, 1), ('a', 5, 1), ('a', 7, 3), ('a', 10, 2), ('s', 5, 6, 1, 0, 6, 0), ('s', 10, 11, 2, 2, 11, 0), ('s', 0, 5, 3, 3, 5, 2), ('s', 7, 8, 1, 4, 7, 0), ('s', 0, 2, 3, 1, 2, 2), ('s', 0, 10, 3, 5, 10, 1), ('a', 6, 0), ('a', 11, 0), ('a', 2, 2), ('a', 5, 2), ('a', 7, 0), ('a', 10, 1), ('s', 5, 6, 2, 0, 6, 1), ('s', 10, 11, 1, 2, 11, 2), ('s', 6, 3, 0, 3, 5, 3), ('s', 0, 7, 2, 4, 8, 1), ('s', 2, 1, 0, 1, 2, 3), ('s', 11, 9, 0, 5, 10, 3), ('a', 6, 1), ('a', 11, 2), ('a', 2, 3), ('a', 5, 3), ('a', 8, 1), ('a', 10, 3)), (5, 2, None, None), (None, None, None), (0, 5, 10, 2, 5, 0))),
    (((('s', 1, 10, 3, 5, 10, 2), ('s', 1, 3, 3, 1, 3, 2), ('s', 6, 4, 3, 3, 4, 2), ('s', 1, 7, 3, 4, 7, 2), ('s', 10, 11, 1, 2, 11, 0), ('s', 4, 5, 1, 0, 5, 0), ('a', 3, 2), ('a', 4, 2), ('a', 7, 2), ('a', 10, 2), ('a', 5, 0), ('a', 11, 0), ('s', 10, 8, 0, 5, 10, 3), ('s', 3, 2, 0, 1, 3, 3), ('s', 7, 8, 1, 4, 7, 3), ('s', 4, 5, 2, 0, 5, 1), ('s', 10, 11, 2, 2, 11, 1), ('a', 3, 3), ('a', 4, 3), ('a', 7, 3), ('a', 10, 3), ('t', 3)), (None, None, None, None), (None, None, None), (0, 1, 15, 0, 1, 7)),
     ((('s', 5, 6, 3, 0, 6, 2), ('s', 8, 9, 1, 2, 11, 1), ('t', 2)), (10, None, None, None), (None, None, None), (2, 5, 14, 5, 10, 2))),
    (((('a', 5, 1), ('a', 11, 1)), (3, 4, None, None), (None, None, None), (0, 3, 10, 3, 4, 7)),
     ((('s', 6, 3, 1, 3, 3, 0), ('s', 7, 8, 3, 4, 7, 2), ('s', 2, 1, 1, 1, 1, 0), ('s', 11, 9, 2, 5, 9, 0), ('a', 6, 2), ('a', 11, 1), ('a', 1, 0), ('a', 3, 0), ('a', 7, 2), ('a', 9, 0)), (7, None, None, None), (None, None, None), (2, 5, 7, 10, 7, 14))),
    (((('s', 10, 8, 2, 5, 8, 0), ('s', 3, 2, 1, 1, 2, 0), ('s', 7, 8, 3, 4, 8, 1)), (None, None, None, None), (None, None, None), (3, 4, 15, 4, 6, 3)),
     ((('s', 3, 4, 0, 0, 6, 3), ('s', 10, 11, 3, 2, 9, 1), ('s', 6, 3, 2, 3, 3, 1), ('s', 7, 8, 0, 4, 8, 3), ('s', 2, 1, 2, 1, 1, 1), ('a', 6, 3), ('a', 9, 1)), (6, None, None, None), (None, None, None), (2, 10, 6, 10, 6, 7))),
    (((('s', 10, 11, 3, 2, 11, 2), ('s', 4, 5, 3, 0, 5, 2)), (7, None, None, None), (None, None, None), (4, 7, 10, 4, 7, 12)),
     ((('t', 3), ('t', 0)), (None, None, None, None), (None, None, None), (2, 5, 15, 5, 6, 12))),
    (((('a', 8, 0), ('t', 1)), (10, None, None, None), (None, None, None), (4, 10, 13, 6, 3, 12)),
     ((('a', 3, 1), ('a', 1, 1), ('a', 8, 3), ('a', 9, 2), ('s', 3, 4, 1, 0, 4, 0), ('s', 8, 9, 3, 2, 11, 3), ('s', 6, 3, 3, 3, 3, 2), ('s', 7, 8, 2, 4, 8, 0), ('s', 2, 1, 3, 1, 1, 2), ('a', 4, 0), ('a', 11, 3)), (None, None, None, None), (None, None, None), (2, 5, 11, 6, 7, 11))),
    (((('a', 2, 0), ('a', 8, 1), ('a', 5, 2), ('a', 11, 2), ('s', 11, 9, 1, 5, 8, 2)), (None, None, None, None), (None, None, None), (6, 4, 1, 7, 10, 6)),
     ((('a', 3, 2),), (11, None, None, None), (None, None, None), (6, 11, 15, 10, 11, 12))),
    (((('s', 3, 2, 2, 1, 2, 1), ('s', 8, 9, 0, 2, 11, 3), ('a', 8, 2), ('a', 2, 1), ('a', 8, 3), ('t', 5)), (None, None, None, None), (None, None, None), (0, 1, 17, 0, 3, 8)),
     ((('a', 1, 2), ('a', 8, 0), ('s', 3, 4, 2, 0, 4, 1), ('a', 3, 3)), (None, None, None, None), (None, None, None), (0, 2, 3, 7, 11, 3))),
    (((('a', 5, 3), ('a', 11, 3), ('s', 11, 9, 3, 5, 9, 1), ('s', 8, 9, 2, 2, 9, 0), ('t', 2)), (8, None, None, None), (None, None, None), (4, 6, 8, 10, 8, 14)),
     ((('a', 4, 1), ('s', 3, 4, 3, 0, 4, 2), ('a', 9, 3), ('a', 8, 2)), (3, None, None, None), (7, None, None), (11, 3, 14, 2, 5, 9))),
    (((('s', 3, 2, 3, 1, 2, 2), ('a', 9, 1)), (5, None, None, None), (None, None, None), (0, 3, 11, 4, 5, 11)),
     ((('a', 1, 3), ('t', 4)), (None, None, None, None), (None, None, None), (2, 5, 9, 3, 5, 16))),
    (((('a', 9, 0),), (None, None, None, None), (None, None, None), (4, 5, 17, 7, 8, 5)),
     ((('a', 4, 2), ('t', 5), ('t', 1)), (9, None, None, None), (None, None, None), (3, 5, 17, 9, 10, 13))),
    (((('a', 2, 2),), (None, None, None, None), (None, None, None), (8, 5, 13, 10, 5, 15)),
     ((), (8, None, None, None), (5, None, None), (9, 8, 6, 9, 8, 12))),
    (((('a', 9, 3), ('a', 9, 2), ('t', 4)), (11, None, None, None), (10, None, None), (11, 0, 13, 0, 4, 16)),
     ((('a', 4, 3),), (None, None, None, None), (12, None, None), (9, 8, 14, 0, 6, 1))),
    (((('a', 2, 3),), (None, None, None, None), (13, 4, None), (0, 3, 9, 1, 6, 2)),
     ((), (1, None, None, None), (6, None, None), (1, 0, 14, 1, 0, 16))),
    (((), (2, None, None, None), (3, 1, 6), (2, 0, 15, 2, 0, 16)),
     ((), (None, None, None, None), (14, 16, None), (2, 1, 8, 3, 1, 15))),
    (((), (None, None, None, None), (15, 16, None), (2, 0, 17, 7, 8, 2)),
     ((), (None, None, None, None), (2, 3, 15), (8, 1, 13, 9, 10, 1))),
    (((), (9, None, None, None), (17, 7, 8), (9, 2, 5, 11, 0, 2)),
     ((), (4, None, None, None), (13, 9, None), (1, 4, 17, 8, 10, 4))),
    (((), (None, None, None, None), (9, 5, 0), (11, 2, 12, 11, 2, 14)),
     ((), (None, None, None, None), (17, 8, 10), (11, 0, 4, 11, 4, 1))),
)

TAIL = (
    (12, 11, 2, 14),
    (0, 11, 4, 1),
)

SLOTS = len(OFFSETS[0])
EXTRA = len(SHARED[0])
HELD = SLOTS + EXTRA
NONE = 31


def words(values, bits=5):
    each = 30 // bits
    return [sum(v * (1 << bits * k) for k, v in enumerate(values[s:s + each])) for s in range(0, len(values), each)]


def lookup(packed, n, bits=5):
    each = 30 // bits
    word = packed[0]
    for k, w in enumerate(packed[1:], 1):
        word = jnp.where(n >= each * k, w, word)
    return lax.rem(lax.shift_right_logical(word, bits * lax.rem(n, each)), 1 << bits)


def of_core(core, lists, bits=5):
    return [jnp.where(core == 0, jnp.asarray(a, jnp.int32), jnp.asarray(b, jnp.int32))
            for a, b in zip(*(words(v, bits) for v in lists))]


def column(which, place, k):
    return [NONE if pair[which][place][k] is None else pair[which][place][k] for pair in STEPS]


def kernel(chunks, emb_ref, lab_ref, out_ref, emb, ids, buf, labels, label_rows, row_best, column_best, outgoing,
           incoming, load_sem, send_sem, recv_sem, give_sem, take_sem, label_send, label_recv, label_give,
           label_take, result_send, result_recv):
    rows, width = emb.shape
    part = rows // chunks
    load = pltpu.make_async_copy(emb_ref, emb, load_sem.at[0])
    load.start()
    load_ids = pltpu.make_async_copy(lab_ref, ids, load_sem.at[1])
    load_ids.start()
    gx = lax.axis_index("grp")
    mem = lax.axis_index("mem")
    core = lax.rem(mem, 2)
    other = 1 - core
    gy = lax.rem(mem // 2, SIDE)
    gz = mem // (2 * SIDE)

    def at(offset, on):
        x, y, z = (lax.rem(g + k, SIDE) for g, k in zip((gx, gy, gz), offset))
        return (x, (z * SIDE + y) * 2 + on)

    barrier = pltpu.get_barrier_semaphore()
    for direction in DIRS:
        pl.semaphore_signal(barrier, inc=1, device_id=at(direction, core), device_id_type=MESH)
    pl.semaphore_signal(barrier, inc=1, device_id=at((0, 0, 0), other), device_id_type=MESH)

    def chunk_of(slot, h):
        return buf.at[slot, pl.ds(h * part, part)]

    def relay(source, target, h, direction):
        return pltpu.make_async_remote_copy(
            src_ref=chunk_of(source, h), dst_ref=chunk_of(target, h),
            send_sem=send_sem.at[target, h], recv_sem=recv_sem.at[target, h],
            device_id=at(DIRS[direction], core), device_id_type=MESH)

    def relay_label(source, target, direction):
        return pltpu.make_async_remote_copy(
            src_ref=labels.at[source], dst_ref=labels.at[target],
            send_sem=label_send.at[target], recv_sem=label_recv.at[target],
            device_id=at(DIRS[direction], core), device_id_type=MESH)

    def send(source, target, h, direction):
        if h == 0:
            relay_label(source, target, direction).start()
        relay(source, target, h, direction).start()

    def share(slot, k, h):
        return pltpu.make_async_remote_copy(
            src_ref=chunk_of(slot, h), dst_ref=chunk_of(SLOTS + k, h),
            send_sem=give_sem.at[k, h], recv_sem=take_sem.at[k, h],
            device_id=at((0, 0, 0), other), device_id_type=MESH)

    def share_label(slot, k):
        return pltpu.make_async_remote_copy(
            src_ref=labels.at[slot], dst_ref=labels.at[SLOTS + k],
            send_sem=label_give.at[k], recv_sem=label_take.at[k],
            device_id=at((0, 0, 0), other), device_id_type=MESH)

    def give(which, slot, h):
        if slot in SHARED[1 - which]:
            k = SHARED[1 - which].index(slot)
            if h == 0:
                share_label(slot, k).start()
            share(slot, k, h).start()

    homes = []
    for which in (0, 1):
        offsets = OFFSETS[which] + tuple(OFFSETS[1 - which][k] for k in SHARED[which])
        homes.append([at([SIDE - k for k in o], which if n < SLOTS else 1 - which) for n, o in enumerate(offsets)])
    home_x, home_mem = (of_core(core, [[h[k] for h in held] for held in homes]) for k in (0, 1))

    load_ids.wait()
    labels[0] = ids[...].astype(jnp.float32)
    load.wait()
    for h in range(chunks):
        e = emb[pl.ds(h * part, part)]
        squares = jnp.sum(e * e, axis=1, keepdims=True)
        buf[0, pl.ds(h * part, part)] = (e * lax.rsqrt(squares + 1e-06)).astype(jnp.bfloat16)
        if h == 0:
            pl.semaphore_wait(barrier, len(DIRS) + 1)
        for which in (0, 1):
            @pl.when(core == which)
            def _(which=which, h=h):
                for move in FIRST_SENDS[which]:
                    if move[2] == h:
                        send(*move)

    for which in (0, 1):
        @pl.when(core == which)
        def _(which=which):
            for h in range(chunks):
                give(which, 0, h)

    def clear(slot, carry):
        column_best[slot] = jnp.full(column_best.shape[1:], FILL, jnp.float32)

        @pl.when(slot < SLOTS)
        def _():
            row_best[slot] = jnp.full(row_best.shape[1:], FILL, jnp.float32)
        return carry

    lax.fori_loop(0, HELD, clear, 0)

    def spread(slot):
        label_rows[slot] = jnp.broadcast_to(labels[slot], (128, rows)).T

    def tile(left, right, own=False):
        sims = lax.dot_general(jnp.concatenate([buf[a] for a in left], axis=0), buf[right], (((1,), (1,)), ((), ())),
                               preferred_element_type=jnp.float32)
        names = labels[right]
        tops = [row_best[a] for a in left]
        for k in range(rows // 128):
            lanes = slice(k * 128, (k + 1) * 128)
            high = column_best[right, :, lanes]
            for n, a in enumerate(left):
                keep = label_rows[a] == names[:, lanes]
                if own:
                    keep = keep & (lax.broadcasted_iota(jnp.int32, (rows, 128), 0)
                                   != lax.broadcasted_iota(jnp.int32, (rows, 128), 1) + k * 128)
                scores = jnp.where(keep, sims[n * rows:(n + 1) * rows, lanes], FILL)
                tops[n] = jnp.maximum(tops[n], scores)
                high = jnp.maximum(high, jnp.max(scores.reshape(rows // 8, 8, 128), axis=0))
            column_best[right, :, lanes] = high
        for n, a in enumerate(left):
            row_best[a] = tops[n]

    def answer(slot):
        return pltpu.make_async_remote_copy(
            src_ref=outgoing.at[slot], dst_ref=incoming.at[slot],
            send_sem=result_send.at[slot], recv_sem=result_recv,
            device_id=(lookup(home_x, slot), lookup(home_mem, slot)), device_id_type=MESH)

    def finish(slot):
        by_column = jnp.max(column_best[slot], axis=0, keepdims=True)

        @pl.when(slot < SLOTS)
        def _():
            outgoing[slot] = jnp.maximum(by_column, jnp.max(row_best[slot].T, axis=0, keepdims=True))

        @pl.when(slot >= SLOTS)
        def _():
            outgoing[slot] = by_column

        @pl.when(slot > 0)
        def _():
            answer(slot).start()

    def arrived(which, slot, h):
        pltpu.make_async_copy(chunk_of(slot, h), chunk_of(slot, h), recv_sem.at[slot, h]).wait()
        if h == 0:
            pltpu.make_async_copy(labels.at[slot], labels.at[slot], label_recv.at[slot]).wait()
        give(which, slot, h)

    def taken(k):
        for h in range(chunks):
            pltpu.make_async_copy(chunk_of(SLOTS + k, h), chunk_of(SLOTS + k, h), take_sem.at[k, h]).wait()
        pltpu.make_async_copy(labels.at[SLOTS + k], labels.at[SLOTS + k], label_take.at[k]).wait()

    def sent(slot, h):
        relay(0, slot, h, 0).wait_send()

    def moves(n):
        for which in (0, 1):
            todo = STEPS[n][which][0]
            if todo:
                @pl.when(core == which)
                def _(which=which, todo=todo):
                    for op in todo:
                        if op[0] == "a":
                            arrived(which, *op[1:])
                        elif op[0] == "t":
                            taken(op[1])
                        else:
                            if len(op) > 5:
                                sent(*op[5:])
                            send(*op[1:5])

    def table(place):
        return [of_core(core, [column(w, place, k) for w in (0, 1)]) for k in range(len(STEPS[0][0][place]))]

    to_open, to_finish, to_compare = table(1), table(2), table(3)
    spread(0)
    tile((0,), 0, own=True)

    def step(n, carry):
        for g in range(0, len(STEPS), 6):
            @pl.when(lax.div(n, 6) == g // 6)
            def _(g=g):
                for k in range(g, min(g + 6, len(STEPS))):
                    @pl.when(n == k)
                    def _(k=k):
                        moves(k)
        for listed, act in ((to_open, spread), (to_finish, finish)):
            for packed in listed:
                slot = lookup(packed, n)

                @pl.when(slot != NONE)
                def _(slot=slot, act=act):
                    act(slot)
        units = [lookup(packed, n) for packed in to_compare]
        for k in range(0, len(units), 3):
            tile(units[k:k + 2], units[k + 2])
        return carry

    lax.fori_loop(0, len(STEPS), step, 0)
    left = max(len(t) for t in TAIL)
    ends = of_core(core, [(list(t) + [NONE] * left)[:left] for t in TAIL])
    ended = [lookup(ends, n) for n in range(left)]
    for slot in ended:
        held = jnp.where(slot == NONE, 0, slot)
        by_row = jnp.max(row_best[jnp.minimum(held, SLOTS - 1)].T, axis=0, keepdims=True)
        by_column = jnp.max(column_best[held], axis=0, keepdims=True)
        outgoing[held] = jnp.where(held < SLOTS, jnp.maximum(by_row, by_column), by_column)
    for slot in ended:
        @pl.when((slot != NONE) & (slot > 0))
        def _(slot=slot):
            answer(slot).start()
    incoming[0] = outgoing[0]

    for which in (0, 1):
        @pl.when(core == which)
        def _(which=which):
            for move in LAST_SENDS[which]:
                sent(*move)
    for k in range(EXTRA):
        for h in range(chunks):
            share(0, k, h).wait_send()
        share_label(0, k).wait_send()
    for slot in range(1, SLOTS):
        relay_label(0, slot, 0).wait_send()
    for slot in range(1, HELD):
        answer(slot).wait_send()
    rest = incoming.at[pl.ds(1, HELD - 1)]
    pltpu.make_async_copy(rest, rest, result_recv).wait()
    out_ref[...] = jnp.max(incoming[...], axis=0).reshape(rows)


def body(embeddings, cluster_ids):
    rows, width = embeddings.shape
    chunks = 1 + max(h for sends in LAST_SENDS for _, h in sends)
    dma = pltpu.SemaphoreType.DMA
    return pl.pallas_call(
        functools.partial(kernel, chunks),
        out_shape=jax.ShapeDtypeStruct((rows,), jnp.float32),
        in_specs=[pl.BlockSpec(memory_space=pl.ANY), pl.BlockSpec(memory_space=pl.ANY)],
        out_specs=pl.BlockSpec(memory_space=pltpu.VMEM),
        scratch_shapes=[
            pltpu.VMEM((rows, width), jnp.float32),
            pltpu.VMEM((1, rows), jnp.int32),
            pltpu.VMEM((HELD, rows, width), jnp.bfloat16),
            pltpu.VMEM((HELD, 1, rows), jnp.float32),
            pltpu.VMEM((SLOTS, rows, 128), jnp.float32),
            pltpu.VMEM((SLOTS, rows, 128), jnp.float32),
            pltpu.VMEM((HELD, 8, rows), jnp.float32),
            pltpu.VMEM((HELD, 1, rows), jnp.float32),
            pltpu.VMEM((HELD, 1, rows), jnp.float32),
            dma((2,)), dma((SLOTS, chunks)), dma((SLOTS, chunks)), dma((EXTRA, chunks)), dma((EXTRA, chunks)),
            dma((SLOTS,)), dma((SLOTS,)), dma((EXTRA,)), dma((EXTRA,)), dma((HELD,)), dma,
        ],
        compiler_params=pltpu.CompilerParams(
            collective_id=0, has_side_effects=True, vmem_limit_bytes=VMEM_BYTES),
    )(embeddings, cluster_ids.reshape(1, rows))


def solution(mesh):
    return jax.shard_map(
        body,
        mesh=mesh,
        in_specs=(P(("grp", "mem"), None), P(("grp", "mem"), None)),
        out_specs=P(("grp", "mem")),
        check_vma=False,
    )
```

```python
import functools

import jax
import jax.numpy as jnp
from jax import lax
from jax.experimental import pallas as pl
from jax.experimental.pallas import tpu as pltpu
from jax.sharding import PartitionSpec as P

FILL = -4.0
MESH = pl.DeviceIdType.MESH
SIDE = 4
VMEM_BYTES = 64 * 1024 * 1024 - 512 * 1024
DIRS = ((1, 0, 0), (3, 0, 0), (0, 1, 0), (0, 3, 0), (0, 0, 1), (0, 0, 3))

OFFSETS = (
    ((0, 0, 0), (0, 0, 1), (1, 0, 1), (1, 0, 2), (2, 0, 2), (0, 1, 3),
     (0, 2, 3), (2, 0, 0), (3, 0, 0), (0, 1, 0), (0, 2, 0), (0, 3, 0)),
    ((0, 0, 0), (1, 0, 0), (1, 0, 1), (2, 0, 1), (0, 1, 2), (0, 2, 2),
     (0, 0, 3), (2, 0, 3), (3, 0, 3), (0, 1, 3), (0, 2, 3), (0, 3, 3)),
)

SHARED = ((1, 2, 3, 4, 8, 11), (0, 2, 5, 6, 7, 8))

FIRST_SENDS = (
    ((0, 1, 0, 4), (0, 9, 0, 2), (0, 8, 0, 1), (0, 11, 0, 3)),
    ((0, 6, 0, 5), (0, 1, 0, 0)),
)

LAST_SENDS = (
    ((1, 1), (2, 1), (3, 1), (4, 0), (4, 1), (6, 0), (6, 1), (7, 1), (10, 0), (10, 1)),
    ((1, 1), (2, 0), (2, 1), (3, 0), (3, 1), (5, 0), (5, 1), (6, 1), (7, 0), (7, 1), (8, 1), (10, 1)),
)

STEPS = (
    (((('s', 0, 8, 1, 1, 8, 0), ('s', 0, 9, 1, 2), ('s', 0, 11, 1, 3, 11, 0), ('s', 0, 1, 1, 4, 9, 0), ('a', 1, 0), ('a', 8, 0), ('a', 11, 0), ('a', 9, 0), ('s', 9, 5, 0, 5, 1, 0), ('s', 1, 2, 0, 0), ('s', 8, 7, 0, 1, 8, 1), ('s', 11, 10, 0, 3, 9, 1), ('a', 1, 1), ('t', 0), ('a', 11, 1), ('a', 9, 1), ('a', 8, 1), ('s', 1, 2, 1, 0), ('s', 9, 5, 1, 5, 5, 0), ('s', 9, 10, 1, 2, 2, 0), ('a', 2, 0), ('s', 8, 7, 1, 1, 7, 0), ('s', 2, 3, 0, 4, 11, 1)), (8, 9, 11, None), (None, None, None), (8, 9, 1, 9, 11, 12)),
     ((('t', 0), ('s', 0, 6, 1, 5, 6, 0), ('s', 0, 1, 1, 0), ('a', 6, 0), ('a', 1, 0), ('s', 6, 11, 0, 3), ('s', 6, 9, 0, 2), ('s', 6, 8, 0, 1), ('s', 1, 2, 0, 4), ('a', 1, 1), ('a', 6, 1)), (1, 6, None, None), (None, None, None), (0, 1, 12, 1, 6, 0))),
    (((('a', 7, 0), ('a', 5, 0), ('s', 5, 6, 0, 2), ('a', 10, 0)), (1, None, None, None), (None, None, None), (1, 8, 11, 1, 8, 12)),
     ((('s', 1, 2, 1, 4), ('s', 6, 8, 1, 1, 1, 0), ('s', 6, 9, 1, 2, 9, 0), ('s', 6, 11, 1, 3, 11, 0), ('a', 8, 0), ('a', 2, 0), ('a', 9, 0), ('s', 2, 3, 0, 0), ('a', 11, 0), ('s', 9, 4, 0, 5), ('s', 11, 10, 0, 3, 11, 1), ('a', 2, 1), ('a', 9, 1)), (2, None, None, None), (None, None, None), (1, 2, 6, 6, 2, 12))),
    (((('t', 1),), (None, None, None, None), (None, None, None), (0, 8, 9, 1, 8, 0)),
     ((('s', 2, 3, 1, 0, 8, 0), ('s', 8, 7, 0, 1), ('s', 9, 4, 1, 5), ('a', 11, 1)), (None, None, None, None), (None, None, None), (0, 1, 9, 2, 6, 9))),
    (((('a', 10, 1),), (None, None, None, None), (None, None, None), (9, 11, 13, 1, 8, 10)),
     ((('a', 8, 1), ('t', 5)), (9, 11, None, None), (None, None, None), (2, 9, 11, 9, 11, 12))),
    (((('a', 2, 1), ('s', 2, 3, 1, 4, 3, 0), ('a', 5, 1)), (2, 10, None, None), (None, None, None), (1, 2, 5, 10, 11, 2)),
     ((), (None, None, None, None), (None, None, None), (9, 11, 8, 0, 1, 11))),
    (((('a', 3, 0), ('t', 5), ('s', 5, 6, 1, 2), ('s', 3, 4, 0, 0, 5, 1)), (None, None, None, None), (None, None, None), (11, 2, 9, 1, 2, 17)),
     ((('a', 4, 0), ('a', 3, 0)), (None, None, None, None), (None, None, None), (1, 2, 8, 2, 9, 17))),
    (((('a', 7, 1),), (5, None, None, None), (None, None, None), (5, 9, 17, 2, 5, 8)),
     ((('t', 2), ('s', 11, 10, 1, 3, 4, 0), ('t', 1)), (None, None, None, None), (None, None, None), (0, 6, 14, 6, 9, 13))),
    (((('a', 6, 0), ('t', 4)), (None, None, None, None), (None, None, None), (10, 5, 13, 0, 2, 7)),
     ((('a', 10, 0), ('s', 10, 5, 0, 5, 9, 1), ('s', 8, 7, 1, 1, 10, 0), ('a', 3, 1), ('a', 4, 1)), (8, 3, 4, None), (None, None, None), (8, 3, 14, 8, 4, 12))),
    (((), (None, None, None, None), (None, None, None), (0, 2, 7, 5, 9, 7)),
     ((('s', 4, 5, 1, 2, 4, 1),), (None, None, None, None), (12, None, None), (8, 11, 4, 11, 4, 17))),
    (((('a', 3, 1), ('s', 3, 4, 1, 0)), (None, None, None, None), (None, None, None), (10, 11, 16, 2, 9, 16)),
     ((('t', 4),), (None, None, None, None), (None, None, None), (11, 4, 17, 4, 6, 16))),
    (((('a', 6, 1),), (3, 7, None, None), (2, None, None), (3, 0, 12, 7, 3, 10)),
     ((), (None, None, None, None), (11, None, None), (4, 9, 3, 0, 2, 4))),
    (((), (6, None, None, None), (None, None, None), (7, 6, 13, 8, 0, 6)),
     ((('a', 10, 1), ('a', 7, 0)), (10, None, None, None), (None, None, None), (4, 10, 13, 10, 0, 17))),
    (((('t', 3), ('t', 2), ('a', 4, 0)), (None, None, None, None), (13, None, None), (7, 3, 17, 8, 11, 3)),
     ((), (None, None, None, None), (17, None, None), (3, 8, 10, 10, 0, 16))),
    (((), (None, None, None, None), (17, 8, None), (9, 10, 14, 0, 5, 3)),
     ((), (None, None, None, None), (8, None, None), (9, 3, 16, 1, 2, 10))),
    (((('a', 4, 1),), (None, None, None, None), (None, None, None), (1, 3, 15, 1, 7, 6)),
     ((('a', 5, 0), ('t', 3), ('a', 7, 1), ('a', 5, 1)), (None, None, None, None), (16, None, None), (4, 6, 7, 9, 10, 7))),
    (((), (None, None, None, None), (3, 1, None), (10, 7, 12, 5, 7, 4)),
     ((), (7, 5, None, None), (4, 6, 9), (7, 5, 13, 0, 2, 5))),
    (((), (4, None, None, None), (12, 5, 7), (9, 10, 4, 11, 4, 15)),
     ((), (None, None, None, None), (13, 2, None), (3, 0, 5, 10, 7, 14))),
    (((), (None, None, None, None), (9, 10, 4), (11, 6, 14, 6, 0, 16)),
     ((), (None, None, None, None), (5, 10, 14), (0, 7, 15, 1, 3, 7))),
)

TAIL = (
    (15, 11, 14, 6, 0, 16),
    (0, 15, 1, 3, 7),
)

SLOTS = len(OFFSETS[0])
EXTRA = len(SHARED[0])
HELD = SLOTS + EXTRA
NONE = 31


def words(values, bits=5):
    each = 30 // bits
    return [sum(v * (1 << bits * k) for k, v in enumerate(values[s:s + each])) for s in range(0, len(values), each)]


def lookup(packed, n, bits=5):
    each = 30 // bits
    word = packed[0]
    for k, w in enumerate(packed[1:], 1):
        word = jnp.where(n >= each * k, w, word)
    return lax.rem(lax.shift_right_logical(word, bits * lax.rem(n, each)), 1 << bits)


def of_core(core, lists, bits=5):
    return [jnp.where(core == 0, jnp.asarray(a, jnp.int32), jnp.asarray(b, jnp.int32))
            for a, b in zip(*(words(v, bits) for v in lists))]


def column(which, place, k):
    return [NONE if pair[which][place][k] is None else pair[which][place][k] for pair in STEPS]


def kernel(chunks, emb_ref, lab_ref, out_ref, emb, ids, buf, labels, label_rows, row_best, column_best, outgoing,
           incoming, load_sem, send_sem, recv_sem, give_sem, take_sem, label_send, label_recv, label_give,
           label_take, result_send, result_recv):
    rows, width = emb.shape
    part = rows // chunks
    load = pltpu.make_async_copy(emb_ref, emb, load_sem.at[0])
    load.start()
    load_ids = pltpu.make_async_copy(lab_ref, ids, load_sem.at[1])
    load_ids.start()
    gx = lax.axis_index("grp")
    mem = lax.axis_index("mem")
    core = lax.rem(mem, 2)
    other = 1 - core
    gy = lax.rem(mem // 2, SIDE)
    gz = mem // (2 * SIDE)

    def at(offset, on):
        x, y, z = (lax.rem(g + k, SIDE) for g, k in zip((gx, gy, gz), offset))
        return (x, (z * SIDE + y) * 2 + on)

    near = [at(direction, core) for direction in DIRS]
    barrier = pltpu.get_barrier_semaphore()
    for device in near:
        pl.semaphore_signal(barrier, inc=1, device_id=device, device_id_type=MESH)
    pl.semaphore_signal(barrier, inc=1, device_id=(gx, mem + 1 - 2 * core), device_id_type=MESH)

    def chunk_of(slot, h):
        return buf.at[slot, pl.ds(h * part, part)]

    def relay(source, target, h, direction):
        return pltpu.make_async_remote_copy(
            src_ref=chunk_of(source, h), dst_ref=chunk_of(target, h),
            send_sem=send_sem.at[target, h], recv_sem=recv_sem.at[target, h],
            device_id=near[direction], device_id_type=MESH)

    def relay_label(source, target, direction):
        return pltpu.make_async_remote_copy(
            src_ref=labels.at[source], dst_ref=labels.at[target],
            send_sem=label_send.at[target], recv_sem=label_recv.at[target],
            device_id=near[direction], device_id_type=MESH)

    def send(source, target, h, direction):
        if h == 0:
            relay_label(source, target, direction).start()
        relay(source, target, h, direction).start()

    def share(slot, k, h):
        return pltpu.make_async_remote_copy(
            src_ref=chunk_of(slot, h), dst_ref=chunk_of(SLOTS + k, h),
            send_sem=give_sem.at[k, h], recv_sem=take_sem.at[k, h],
            device_id=(gx, mem + 1 - 2 * core), device_id_type=MESH)

    def share_label(slot, k):
        return pltpu.make_async_remote_copy(
            src_ref=labels.at[slot], dst_ref=labels.at[SLOTS + k],
            send_sem=label_give.at[k], recv_sem=label_take.at[k],
            device_id=(gx, mem + 1 - 2 * core), device_id_type=MESH)

    def give(which, slot, h):
        if slot in SHARED[1 - which]:
            k = SHARED[1 - which].index(slot)
            if h == 0:
                share_label(slot, k).start()
            share(slot, k, h).start()

    homes = []
    for which in (0, 1):
        offsets = OFFSETS[which] + tuple(OFFSETS[1 - which][k] for k in SHARED[which])
        homes.append([at([SIDE - k for k in o], which if n < SLOTS else 1 - which) for n, o in enumerate(offsets)])
    home_x, home_mem = (of_core(core, [[h[k] for h in held] for held in homes]) for k in (0, 1))

    load_ids.wait()
    labels[0] = ids[...].astype(jnp.float32)
    load.wait()
    for h in range(chunks):
        e = emb[pl.ds(h * part, part)]
        squares = jnp.sum(e * e, axis=1, keepdims=True)
        buf[0, pl.ds(h * part, part)] = (e * lax.rsqrt(squares + 1e-06)).astype(jnp.bfloat16)
        if h == 0:
            pl.semaphore_wait(barrier, len(DIRS) + 1)
        for which in (0, 1):
            @pl.when(core == which)
            def _(which=which, h=h):
                for move in FIRST_SENDS[which]:
                    if move[2] == h:
                        send(*move)

    for which in (0, 1):
        @pl.when(core == which)
        def _(which=which):
            for h in range(chunks):
                give(which, 0, h)

    def clear(slot, carry):
        column_best[slot] = jnp.full(column_best.shape[1:], FILL, jnp.float32)

        @pl.when(slot < SLOTS)
        def _():
            row_best[slot] = jnp.full(row_best.shape[1:], FILL, jnp.float32)
        return carry

    lax.fori_loop(0, HELD, clear, 0)

    def spread(slot):
        label_rows[slot] = jnp.broadcast_to(labels[slot], (128, rows)).T

    def tile(left, right, own=False):
        sims = lax.dot_general(jnp.concatenate([buf[a] for a in left], axis=0), buf[right], (((1,), (1,)), ((), ())),
                               preferred_element_type=jnp.float32)
        names = labels[right]
        tops = [row_best[a] for a in left]
        for k in range(rows // 128):
            lanes = slice(k * 128, (k + 1) * 128)
            high = column_best[right, :, lanes]
            for n, a in enumerate(left):
                keep = label_rows[a] == names[:, lanes]
                if own:
                    keep = keep & (lax.broadcasted_iota(jnp.int32, (rows, 128), 0)
                                   != lax.broadcasted_iota(jnp.int32, (rows, 128), 1) + k * 128)
                scores = jnp.where(keep, sims[n * rows:(n + 1) * rows, lanes], FILL)
                tops[n] = jnp.maximum(tops[n], scores)
                high = jnp.maximum(high, jnp.max(scores.reshape(rows // 8, 8, 128), axis=0))
            column_best[right, :, lanes] = high
        for n, a in enumerate(left):
            row_best[a] = tops[n]

    def answer(slot):
        return pltpu.make_async_remote_copy(
            src_ref=outgoing.at[slot], dst_ref=incoming.at[slot],
            send_sem=result_send.at[slot], recv_sem=result_recv,
            device_id=(lookup(home_x, slot), lookup(home_mem, slot)), device_id_type=MESH)

    def finish(slot):
        by_column = jnp.max(column_best[slot], axis=0, keepdims=True)

        @pl.when(slot < SLOTS)
        def _():
            outgoing[slot] = jnp.maximum(by_column, jnp.max(row_best[slot].T, axis=0, keepdims=True))

        @pl.when(slot >= SLOTS)
        def _():
            outgoing[slot] = by_column

        @pl.when(slot > 0)
        def _():
            answer(slot).start()

    def arrived(which, slot, h):
        pltpu.make_async_copy(chunk_of(slot, h), chunk_of(slot, h), recv_sem.at[slot, h]).wait()
        if h == 0:
            pltpu.make_async_copy(labels.at[slot], labels.at[slot], label_recv.at[slot]).wait()
        give(which, slot, h)

    def taken(k):
        for h in range(chunks):
            pltpu.make_async_copy(chunk_of(SLOTS + k, h), chunk_of(SLOTS + k, h), take_sem.at[k, h]).wait()
        pltpu.make_async_copy(labels.at[SLOTS + k], labels.at[SLOTS + k], label_take.at[k]).wait()

    def sent(slot, h):
        relay(0, slot, h, 0).wait_send()

    def moves(n):
        for which in (0, 1):
            todo = STEPS[n][which][0]
            if todo:
                @pl.when(core == which)
                def _(which=which, todo=todo):
                    for op in todo:
                        if op[0] == "a":
                            arrived(which, *op[1:])
                        elif op[0] == "t":
                            taken(op[1])
                        else:
                            if len(op) > 5:
                                sent(*op[5:])
                            send(*op[1:5])

    def table(place):
        return [of_core(core, [column(w, place, k) for w in (0, 1)]) for k in range(len(STEPS[0][0][place]))]

    to_open, to_finish, to_compare = table(1), table(2), table(3)
    spread(0)
    tile((0,), 0, own=True)

    def step(n, carry):
        for g in range(0, len(STEPS), 6):
            @pl.when(lax.div(n, 6) == g // 6)
            def _(g=g):
                for k in range(g, min(g + 6, len(STEPS))):
                    @pl.when(n == k)
                    def _(k=k):
                        moves(k)
        for listed, act in ((to_open, spread), (to_finish, finish)):
            for packed in listed:
                slot = lookup(packed, n)

                @pl.when(slot != NONE)
                def _(slot=slot, act=act):
                    act(slot)
        units = [lookup(packed, n) for packed in to_compare]
        for k in range(0, len(units), 3):
            tile(units[k:k + 2], units[k + 2])
        return carry

    lax.fori_loop(0, len(STEPS), step, 0)
    left = max(len(t) for t in TAIL)
    ends = of_core(core, [(list(t) + [NONE] * left)[:left] for t in TAIL])
    ended = [lookup(ends, n) for n in range(left)]
    for slot in ended:
        held = jnp.where(slot == NONE, 0, slot)
        by_row = jnp.max(row_best[jnp.minimum(held, SLOTS - 1)].T, axis=0, keepdims=True)
        by_column = jnp.max(column_best[held], axis=0, keepdims=True)
        outgoing[held] = jnp.where(held < SLOTS, jnp.maximum(by_row, by_column), by_column)
    for slot in ended:
        @pl.when((slot != NONE) & (slot > 0))
        def _(slot=slot):
            answer(slot).start()
    incoming[0] = outgoing[0]

    for which in (0, 1):
        @pl.when(core == which)
        def _(which=which):
            for move in LAST_SENDS[which]:
                sent(*move)
    for k in range(EXTRA):
        for h in range(chunks):
            share(0, k, h).wait_send()
        share_label(0, k).wait_send()
    for slot in range(1, SLOTS):
        relay_label(0, slot, 0).wait_send()
    for slot in range(1, HELD):
        answer(slot).wait_send()
    rest = incoming.at[pl.ds(1, HELD - 1)]
    pltpu.make_async_copy(rest, rest, result_recv).wait()
    out_ref[...] = jnp.max(incoming[...], axis=0).reshape(rows)


def body(embeddings, cluster_ids):
    rows, width = embeddings.shape
    chunks = 1 + max(h for sends in LAST_SENDS for _, h in sends)
    dma = pltpu.SemaphoreType.DMA
    return pl.pallas_call(
        functools.partial(kernel, chunks),
        out_shape=jax.ShapeDtypeStruct((rows,), jnp.float32),
        in_specs=[pl.BlockSpec(memory_space=pl.ANY), pl.BlockSpec(memory_space=pl.ANY)],
        out_specs=pl.BlockSpec(memory_space=pltpu.VMEM),
        scratch_shapes=[
            pltpu.VMEM((rows, width), jnp.float32),
            pltpu.VMEM((1, rows), jnp.int32),
            pltpu.VMEM((HELD, rows, width), jnp.bfloat16),
            pltpu.VMEM((HELD, 1, rows), jnp.float32),
            pltpu.VMEM((SLOTS, rows, 128), jnp.float32),
            pltpu.VMEM((SLOTS, rows, 128), jnp.float32),
            pltpu.VMEM((HELD, 8, rows), jnp.float32),
            pltpu.VMEM((HELD, 1, rows), jnp.float32),
            pltpu.VMEM((HELD, 1, rows), jnp.float32),
            dma((2,)), dma((SLOTS, chunks)), dma((SLOTS, chunks)), dma((EXTRA, chunks)), dma((EXTRA, chunks)),
            dma((SLOTS,)), dma((SLOTS,)), dma((EXTRA,)), dma((EXTRA,)), dma((HELD,)), dma,
        ],
        compiler_params=pltpu.CompilerParams(
            collective_id=0, has_side_effects=True, vmem_limit_bytes=VMEM_BYTES),
    )(embeddings, cluster_ids.reshape(1, rows))


def solution(mesh):
    return jax.shard_map(
        body,
        mesh=mesh,
        in_specs=(P(("grp", "mem"), None), P(("grp", "mem"), None)),
        out_specs=P(("grp", "mem")),
        check_vma=False,
    )
```

```python
import functools

import jax
import jax.numpy as jnp
from jax import lax
from jax.experimental import pallas as pl
from jax.experimental.pallas import tpu as pltpu
from jax.sharding import PartitionSpec as P

FILL = -4.0
MESH = pl.DeviceIdType.MESH
SIDE = 4
VMEM_BYTES = 64 * 1024 * 1024 - 512 * 1024
DIRS = ((1, 0, 0), (3, 0, 0), (0, 1, 0), (0, 3, 0), (0, 0, 1), (0, 0, 3))

OFFSETS = (
    ((0, 0, 0), (0, 0, 1), (1, 0, 1), (1, 0, 2), (2, 0, 2), (0, 1, 3),
     (0, 2, 3), (2, 0, 0), (3, 0, 0), (0, 1, 0), (0, 2, 0), (0, 3, 0)),
    ((0, 0, 0), (1, 0, 0), (1, 0, 1), (2, 0, 1), (0, 1, 2), (0, 2, 2),
     (0, 0, 3), (2, 0, 3), (3, 0, 3), (0, 1, 3), (0, 2, 3), (0, 3, 3)),
)

SHARED = ((1, 2, 3, 4, 8, 11), (0, 2, 5, 6, 7, 8))

FIRST_SENDS = (
    ((0, 1, 0, 4), (0, 9, 0, 2), (0, 8, 0, 1), (0, 11, 0, 3)),
    ((0, 6, 0, 5), (0, 1, 0, 0)),
)

LAST_SENDS = (
    ((1, 1), (2, 1), (3, 1), (4, 0), (4, 1), (6, 0), (6, 1), (7, 1), (10, 0), (10, 1)),
    ((1, 1), (2, 0), (2, 1), (3, 0), (3, 1), (5, 0), (5, 1), (6, 1), (7, 0), (7, 1), (8, 1), (10, 1)),
)

STEPS = (
    (((('s', 0, 8, 1, 1, 8, 0), ('s', 0, 9, 1, 2), ('s', 0, 11, 1, 3, 11, 0), ('s', 0, 1, 1, 4, 9, 0), ('a', 1, 0), ('a', 8, 0), ('a', 11, 0), ('a', 9, 0), ('s', 9, 5, 0, 5, 1, 0), ('s', 1, 2, 0, 0), ('s', 8, 7, 0, 1, 8, 1), ('s', 11, 10, 0, 3, 9, 1), ('a', 1, 1), ('t', 0), ('a', 11, 1), ('a', 9, 1), ('a', 8, 1), ('s', 1, 2, 1, 0), ('s', 9, 5, 1, 5, 5, 0), ('s', 9, 10, 1, 2, 2, 0), ('a', 2, 0), ('s', 8, 7, 1, 1, 7, 0), ('s', 2, 3, 0, 4, 11, 1)), (8, 9, 11, None), (None, None, None), (8, 9, 1, 9, 11, 12)),
     ((('t', 0), ('s', 0, 6, 1, 5, 6, 0), ('s', 0, 1, 1, 0), ('a', 6, 0), ('a', 1, 0), ('s', 6, 11, 0, 3), ('s', 6, 9, 0, 2), ('s', 6, 8, 0, 1), ('s', 1, 2, 0, 4), ('a', 1, 1), ('a', 6, 1)), (1, 6, None, None), (None, None, None), (0, 1, 12, 1, 6, 0))),
    (((('a', 7, 0), ('a', 5, 0), ('s', 5, 6, 0, 2), ('a', 10, 0)), (1, None, None, None), (None, None, None), (1, 8, 11, 1, 8, 12)),
     ((('s', 1, 2, 1, 4), ('s', 6, 8, 1, 1, 1, 0), ('s', 6, 9, 1, 2, 9, 0), ('s', 6, 11, 1, 3, 11, 0), ('a', 8, 0), ('a', 2, 0), ('a', 9, 0), ('s', 2, 3, 0, 0), ('a', 11, 0), ('s', 9, 4, 0, 5), ('s', 11, 10, 0, 3, 11, 1), ('a', 2, 1), ('a', 9, 1)), (2, None, None, None), (None, None, None), (1, 2, 6, 6, 2, 12))),
    (((('t', 1),), (None, None, None, None), (None, None, None), (0, 8, 9, 1, 8, 0)),
     ((('s', 2, 3, 1, 0, 8, 0), ('s', 8, 7, 0, 1), ('s', 9, 4, 1, 5), ('a', 11, 1)), (None, None, None, None), (None, None, None), (0, 1, 9, 2, 6, 9))),
    (((('a', 10, 1),), (None, None, None, None), (None, None, None), (9, 11, 13, 1, 8, 10)),
     ((('a', 8, 1), ('t', 5)), (9, 11, None, None), (None, None, None), (2, 9, 11, 9, 11, 12))),
    (((('a', 2, 1), ('s', 2, 3, 1, 4, 3, 0), ('a', 5, 1)), (2, 10, None, None), (None, None, None), (1, 2, 5, 10, 11, 2)),
     ((), (None, None, None, None), (None, None, None), (9, 11, 8, 0, 1, 11))),
    (((('a', 3, 0), ('t', 5), ('s', 5, 6, 1, 2), ('s', 3, 4, 0, 0, 5, 1)), (None, None, None, None), (None, None, None), (11, 2, 9, 1, 2, 17)),
     ((('a', 4, 0), ('a', 3, 0)), (None, None, None, None), (None, None, None), (1, 2, 8, 2, 9, 17))),
    (((('a', 7, 1),), (5, None, None, None), (None, None, None), (5, 9, 17, 2, 5, 8)),
     ((('t', 2), ('s', 11, 10, 1, 3, 4, 0), ('t', 1)), (None, None, None, None), (None, None, None), (0, 6, 14, 6, 9, 13))),
    (((('a', 6, 0), ('t', 4)), (None, None, None, None), (None, None, None), (10, 5, 13, 0, 2, 7)),
     ((('a', 10, 0), ('s', 10, 5, 0, 5, 9, 1), ('s', 8, 7, 1, 1, 10, 0), ('a', 3, 1), ('a', 4, 1)), (8, 3, 4, None), (None, None, None), (8, 3, 14, 8, 4, 12))),
    (((), (None, None, None, None), (None, None, None), (0, 2, 7, 5, 9, 7)),
     ((('s', 4, 5, 1, 2, 4, 1),), (None, None, None, None), (12, None, None), (8, 11, 4, 11, 4, 17))),
    (((('a', 3, 1), ('s', 3, 4, 1, 0)), (None, None, None, None), (None, None, None), (10, 11, 16, 2, 9, 16)),
     ((('t', 4),), (None, None, None, None), (None, None, None), (11, 4, 17, 4, 6, 16))),
    (((('a', 6, 1),), (3, 7, None, None), (2, None, None), (3, 0, 12, 7, 3, 10)),
     ((), (None, None, None, None), (11, None, None), (4, 9, 3, 0, 2, 4))),
    (((), (6, None, None, None), (None, None, None), (7, 6, 13, 8, 0, 6)),
     ((('a', 10, 1), ('a', 7, 0)), (10, None, None, None), (None, None, None), (4, 10, 13, 10, 0, 17))),
    (((('t', 3), ('t', 2), ('a', 4, 0)), (None, None, None, None), (13, None, None), (7, 3, 17, 8, 11, 3)),
     ((), (None, None, None, None), (17, None, None), (3, 8, 10, 10, 0, 16))),
    (((), (None, None, None, None), (17, 8, None), (9, 10, 14, 0, 5, 3)),
     ((), (None, None, None, None), (8, None, None), (9, 3, 16, 1, 2, 10))),
    (((('a', 4, 1),), (None, None, None, None), (None, None, None), (1, 3, 15, 1, 7, 6)),
     ((('a', 5, 0), ('t', 3), ('a', 7, 1), ('a', 5, 1)), (None, None, None, None), (16, None, None), (4, 6, 7, 9, 10, 7))),
    (((), (None, None, None, None), (3, 1, None), (10, 7, 12, 5, 7, 4)),
     ((), (7, 5, None, None), (4, 6, 9), (7, 5, 13, 0, 2, 5))),
    (((), (4, None, None, None), (12, 5, 7), (9, 10, 4, 11, 4, 15)),
     ((), (None, None, None, None), (13, 2, None), (3, 0, 5, 10, 7, 14))),
    (((), (None, None, None, None), (9, 10, 4), (11, 6, 14, 6, 0, 16)),
     ((), (None, None, None, None), (5, 10, 14), (0, 7, 15, 1, 3, 7))),
)

TAIL = (
    (15, 11, 14, 6, 0, 16),
    (0, 15, 1, 3, 7),
)

SLOTS = len(OFFSETS[0])
EXTRA = len(SHARED[0])
HELD = SLOTS + EXTRA
NONE = 31
GROUP = 64


def words(values, bits=5):
    each = 30 // bits
    return [sum(v * (1 << bits * k) for k, v in enumerate(values[s:s + each])) for s in range(0, len(values), each)]


def lookup(packed, n, bits=5):
    each = 30 // bits
    word = packed[0]
    for k, w in enumerate(packed[1:], 1):
        word = jnp.where(n >= each * k, w, word)
    return lax.rem(lax.shift_right_logical(word, bits * lax.rem(n, each)), 1 << bits)


def of_core(core, lists, bits=5):
    return [jnp.where(core == 0, jnp.asarray(a, jnp.int32), jnp.asarray(b, jnp.int32))
            for a, b in zip(*(words(v, bits) for v in lists))]


def column(which, place, k):
    return [NONE if pair[which][place][k] is None else pair[which][place][k] for pair in STEPS]


def kernel(chunks, emb_ref, lab_ref, out_ref, emb, ids, buf, labels, label_rows, row_best, column_best, outgoing,
           incoming, load_sem, send_sem, recv_sem, give_sem, take_sem, label_send, label_recv, label_give,
           label_take, result_send, result_recv):
    rows, width = emb.shape
    part = rows // chunks
    load = pltpu.make_async_copy(emb_ref, emb, load_sem.at[0])
    load.start()
    load_ids = pltpu.make_async_copy(lab_ref, ids, load_sem.at[1])
    load_ids.start()
    gx = lax.axis_index("grp")
    mem = lax.axis_index("mem")
    core = lax.rem(mem, 2)
    other = 1 - core
    gy = lax.rem(mem // 2, SIDE)
    gz = mem // (2 * SIDE)

    def at(offset, on):
        x, y, z = (lax.rem(g + k, SIDE) for g, k in zip((gx, gy, gz), offset))
        return (x, (z * SIDE + y) * 2 + on)

    near = [at(direction, core) for direction in DIRS]
    barrier = pltpu.get_barrier_semaphore()
    for device in near:
        pl.semaphore_signal(barrier, inc=1, device_id=device, device_id_type=MESH)
    pl.semaphore_signal(barrier, inc=1, device_id=(gx, mem + 1 - 2 * core), device_id_type=MESH)

    def chunk_of(slot, h):
        return buf.at[slot, pl.ds(h * part, part)]

    def relay(source, target, h, direction):
        return pltpu.make_async_remote_copy(
            src_ref=chunk_of(source, h), dst_ref=chunk_of(target, h),
            send_sem=send_sem.at[target, h], recv_sem=recv_sem.at[target, h],
            device_id=near[direction], device_id_type=MESH)

    def relay_label(source, target, direction):
        return pltpu.make_async_remote_copy(
            src_ref=labels.at[source], dst_ref=labels.at[target],
            send_sem=label_send.at[target], recv_sem=label_recv.at[target],
            device_id=near[direction], device_id_type=MESH)

    def send(source, target, h, direction):
        if h == 0:
            relay_label(source, target, direction).start()
        relay(source, target, h, direction).start()

    def share(slot, k, h):
        return pltpu.make_async_remote_copy(
            src_ref=chunk_of(slot, h), dst_ref=chunk_of(SLOTS + k, h),
            send_sem=give_sem.at[k, h], recv_sem=take_sem.at[k, h],
            device_id=(gx, mem + 1 - 2 * core), device_id_type=MESH)

    def share_label(slot, k):
        return pltpu.make_async_remote_copy(
            src_ref=labels.at[slot], dst_ref=labels.at[SLOTS + k],
            send_sem=label_give.at[k], recv_sem=label_take.at[k],
            device_id=(gx, mem + 1 - 2 * core), device_id_type=MESH)

    def give(which, slot, h):
        if slot in SHARED[1 - which]:
            k = SHARED[1 - which].index(slot)
            if h == 0:
                share_label(slot, k).start()
            share(slot, k, h).start()

    homes = []
    for which in (0, 1):
        offsets = OFFSETS[which] + tuple(OFFSETS[1 - which][k] for k in SHARED[which])
        homes.append([at([SIDE - k for k in o], which if n < SLOTS else 1 - which) for n, o in enumerate(offsets)])
    home_x, home_mem = (of_core(core, [[h[k] for h in held] for held in homes]) for k in (0, 1))

    load_ids.wait()
    labels[0] = ids[...].astype(jnp.float32)
    load.wait()
    for h in range(chunks):
        e = emb[pl.ds(h * part, part)]
        squares = jnp.sum(e * e, axis=1, keepdims=True)
        buf[0, pl.ds(h * part, part)] = (e * lax.rsqrt(squares + 1e-06)).astype(jnp.bfloat16)
        if h == 0:
            pl.semaphore_wait(barrier, len(DIRS) + 1)
        for which in (0, 1):
            @pl.when(core == which)
            def _(which=which, h=h):
                for move in FIRST_SENDS[which]:
                    if move[2] == h:
                        send(*move)

    for which in (0, 1):
        @pl.when(core == which)
        def _(which=which):
            for h in range(chunks):
                give(which, 0, h)

    def clear(slot, carry):
        column_best[slot] = jnp.full(column_best.shape[1:], FILL, jnp.float32)

        @pl.when(slot < SLOTS)
        def _():
            row_best[slot] = jnp.full(row_best.shape[1:], FILL, jnp.float32)
        return carry

    lax.fori_loop(0, HELD, clear, 0)

    def spread(slot):
        label_rows[slot] = jnp.broadcast_to(labels[slot], (128, rows)).T

    def tile(left, right, own=False):
        sims = lax.dot_general(jnp.concatenate([buf[a] for a in left], axis=0), buf[right], (((1,), (1,)), ((), ())),
                               preferred_element_type=jnp.float32)
        names = labels[right]
        lanes = [slice(k, k + 128) for k in range(0, rows, 128)]
        high = [column_best[right, :, k] for k in lanes]
        for n, a in enumerate(left):
            for r in range(0, rows, GROUP):
                mine = label_rows[a, pl.ds(r, GROUP)]
                top = row_best[a, pl.ds(r, GROUP)]
                for m, k in enumerate(lanes):
                    keep = mine == names[:, k]
                    if own:
                        keep = keep & (lax.broadcasted_iota(jnp.int32, (GROUP, 128), 0) + r
                                       != lax.broadcasted_iota(jnp.int32, (GROUP, 128), 1) + m * 128)
                    scores = jnp.where(keep, sims[n * rows + r:n * rows + r + GROUP, k], FILL)
                    top = jnp.maximum(top, scores)
                    high[m] = jnp.maximum(high[m], jnp.max(scores.reshape(GROUP // 8, 8, 128), axis=0))
                row_best[a, pl.ds(r, GROUP)] = top
        for m, k in enumerate(lanes):
            column_best[right, :, k] = high[m]

    def answer(slot):
        return pltpu.make_async_remote_copy(
            src_ref=outgoing.at[slot], dst_ref=incoming.at[slot],
            send_sem=result_send.at[slot], recv_sem=result_recv,
            device_id=(lookup(home_x, slot), lookup(home_mem, slot)), device_id_type=MESH)

    def finish(slot):
        by_column = jnp.max(column_best[slot], axis=0, keepdims=True)

        @pl.when(slot < SLOTS)
        def _():
            outgoing[slot] = jnp.maximum(by_column, jnp.max(row_best[slot].T, axis=0, keepdims=True))

        @pl.when(slot >= SLOTS)
        def _():
            outgoing[slot] = by_column

        @pl.when(slot > 0)
        def _():
            answer(slot).start()

    def arrived(which, slot, h):
        pltpu.make_async_copy(chunk_of(slot, h), chunk_of(slot, h), recv_sem.at[slot, h]).wait()
        if h == 0:
            pltpu.make_async_copy(labels.at[slot], labels.at[slot], label_recv.at[slot]).wait()
        give(which, slot, h)

    def taken(k):
        for h in range(chunks):
            pltpu.make_async_copy(chunk_of(SLOTS + k, h), chunk_of(SLOTS + k, h), take_sem.at[k, h]).wait()
        pltpu.make_async_copy(labels.at[SLOTS + k], labels.at[SLOTS + k], label_take.at[k]).wait()

    def sent(slot, h):
        relay(0, slot, h, 0).wait_send()

    def moves(n):
        for which in (0, 1):
            todo = STEPS[n][which][0]
            if todo:
                @pl.when(core == which)
                def _(which=which, todo=todo):
                    for op in todo:
                        if op[0] == "a":
                            arrived(which, *op[1:])
                        elif op[0] == "t":
                            taken(op[1])
                        else:
                            if len(op) > 5:
                                sent(*op[5:])
                            send(*op[1:5])

    def table(place):
        return [of_core(core, [column(w, place, k) for w in (0, 1)]) for k in range(len(STEPS[0][0][place]))]

    to_open, to_finish, to_compare = table(1), table(2), table(3)
    spread(0)
    tile((0,), 0, own=True)

    def step(n, carry):
        for g in range(0, len(STEPS), 6):
            @pl.when(lax.div(n, 6) == g // 6)
            def _(g=g):
                for k in range(g, min(g + 6, len(STEPS))):
                    @pl.when(n == k)
                    def _(k=k):
                        moves(k)
        for listed, act in ((to_open, spread), (to_finish, finish)):
            for packed in listed:
                slot = lookup(packed, n)

                @pl.when(slot != NONE)
                def _(slot=slot, act=act):
                    act(slot)
        units = [lookup(packed, n) for packed in to_compare]
        for k in range(0, len(units), 3):
            tile(units[k:k + 2], units[k + 2])
        return carry

    lax.fori_loop(0, len(STEPS), step, 0)
    left = max(len(t) for t in TAIL)
    ends = of_core(core, [(list(t) + [NONE] * left)[:left] for t in TAIL])
    ended = [lookup(ends, n) for n in range(left)]
    for slot in ended:
        held = jnp.where(slot == NONE, 0, slot)
        by_row = jnp.max(row_best[jnp.minimum(held, SLOTS - 1)].T, axis=0, keepdims=True)
        by_column = jnp.max(column_best[held], axis=0, keepdims=True)
        outgoing[held] = jnp.where(held < SLOTS, jnp.maximum(by_row, by_column), by_column)
    for slot in ended:
        @pl.when((slot != NONE) & (slot > 0))
        def _(slot=slot):
            answer(slot).start()
    incoming[0] = outgoing[0]

    for which in (0, 1):
        @pl.when(core == which)
        def _(which=which):
            for move in LAST_SENDS[which]:
                sent(*move)
    for k in range(EXTRA):
        for h in range(chunks):
            share(0, k, h).wait_send()
        share_label(0, k).wait_send()
    for slot in range(1, SLOTS):
        relay_label(0, slot, 0).wait_send()
    for slot in range(1, HELD):
        answer(slot).wait_send()
    rest = incoming.at[pl.ds(1, HELD - 1)]
    pltpu.make_async_copy(rest, rest, result_recv).wait()
    out_ref[...] = jnp.max(incoming[...], axis=0).reshape(rows)


def body(embeddings, cluster_ids):
    rows, width = embeddings.shape
    chunks = 1 + max(h for sends in LAST_SENDS for _, h in sends)
    dma = pltpu.SemaphoreType.DMA
    return pl.pallas_call(
        functools.partial(kernel, chunks),
        out_shape=jax.ShapeDtypeStruct((rows,), jnp.float32),
        in_specs=[pl.BlockSpec(memory_space=pl.ANY), pl.BlockSpec(memory_space=pl.ANY)],
        out_specs=pl.BlockSpec(memory_space=pltpu.VMEM),
        scratch_shapes=[
            pltpu.VMEM((rows, width), jnp.float32),
            pltpu.VMEM((1, rows), jnp.int32),
            pltpu.VMEM((HELD, rows, width), jnp.bfloat16),
            pltpu.VMEM((HELD, 1, rows), jnp.float32),
            pltpu.VMEM((SLOTS, rows, 128), jnp.float32),
            pltpu.VMEM((SLOTS, rows, 128), jnp.float32),
            pltpu.VMEM((HELD, 8, rows), jnp.float32),
            pltpu.VMEM((HELD, 1, rows), jnp.float32),
            pltpu.VMEM((HELD, 1, rows), jnp.float32),
            dma((2,)), dma((SLOTS, chunks)), dma((SLOTS, chunks)), dma((EXTRA, chunks)), dma((EXTRA, chunks)),
            dma((SLOTS,)), dma((SLOTS,)), dma((EXTRA,)), dma((EXTRA,)), dma((HELD,)), dma,
        ],
        compiler_params=pltpu.CompilerParams(
            collective_id=0, has_side_effects=True, vmem_limit_bytes=VMEM_BYTES),
    )(embeddings, cluster_ids.reshape(1, rows))


def solution(mesh):
    return jax.shard_map(
        body,
        mesh=mesh,
        in_specs=(P(("grp", "mem"), None), P(("grp", "mem"), None)),
        out_specs=P(("grp", "mem")),
        check_vma=False,
    )
```

```python
import functools

import jax
import jax.numpy as jnp
from jax import lax
from jax.experimental import pallas as pl
from jax.experimental.pallas import tpu as pltpu
from jax.sharding import PartitionSpec as P

FILL = -4.0
MESH = pl.DeviceIdType.MESH
SIDE = 4
VMEM_BYTES = 64 * 1024 * 1024 - 512 * 1024
DIRS = ((1, 0, 0), (3, 0, 0), (0, 1, 0), (0, 3, 0), (0, 0, 1), (0, 0, 3))

OFFSETS = (
    ((0, 0, 0), (0, 3, 3), (0, 2, 3), (0, 3, 0), (1, 0, 0), (2, 0, 0),
     (0, 1, 0), (0, 2, 0), (0, 0, 1), (3, 0, 1), (2, 0, 2), (3, 0, 2)),
    ((0, 0, 0), (0, 3, 2), (0, 2, 2), (0, 3, 3), (0, 0, 3), (1, 0, 3),
     (2, 0, 3), (0, 1, 3), (0, 2, 3), (3, 0, 0), (2, 0, 1), (3, 0, 1)),
)

SHARED = ((1, 5, 7, 9, 10, 11), (0, 1, 2, 4, 5, 9))

FIRST_SENDS = (
    ((0, 8, 0, 4), (0, 3, 0, 3), (0, 4, 0, 0), (0, 6, 0, 2)),
    ((0, 4, 0, 5), (0, 9, 0, 1)),
)

LAST_SENDS = (
    ((1, 1), (2, 1), (5, 1), (6, 1), (7, 0), (9, 1), (10, 0), (10, 1), (11, 0), (11, 1)),
    ((2, 0), (2, 1), (3, 0), (3, 1), (6, 1), (8, 1), (9, 0), (9, 1), (10, 1), (11, 1)),
)

STEPS = (
    (((('s', 0, 8, 1, 4, 8, 0), ('s', 0, 3, 1, 3, 3, 0), ('s', 0, 4, 1, 0, 4, 0), ('s', 0, 6, 1, 2, 6, 0), ('a', 6, 0), ('a', 4, 0), ('a', 8, 0), ('a', 3, 0), ('s', 8, 9, 0, 1), ('s', 3, 1, 0, 5), ('s', 4, 5, 0, 0, 4, 1), ('s', 6, 7, 0, 2), ('a', 4, 1), ('a', 3, 1), ('a', 6, 1), ('a', 8, 1)), (3, 4, None, None), (None, None, None), (0, 3, 8, 3, 4, 0)),
     ((('s', 0, 4, 1, 5, 4, 0), ('s', 0, 9, 1, 1), ('t', 0), ('a', 4, 0), ('s', 4, 7, 0, 2), ('s', 4, 3, 0, 3), ('a', 9, 0), ('s', 4, 5, 0, 0), ('s', 9, 11, 0, 4), ('a', 4, 1), ('a', 9, 1)), (4, 9, None, None), (None, None, None), (0, 4, 12, 4, 9, 0))),
    (((('s', 8, 9, 1, 1, 9, 0), ('s', 3, 7, 1, 3, 3, 1), ('s', 3, 1, 1, 5, 1, 0), ('a', 9, 0), ('t', 3)), (6, None, None, None), (None, None, None), (3, 4, 15, 4, 6, 3)),
     ((('s', 9, 11, 1, 4, 11, 0), ('s', 4, 5, 1, 0, 5, 0), ('s', 4, 7, 1, 2, 7, 0), ('s', 4, 3, 1, 3), ('a', 3, 0), ('a', 11, 0), ('s', 3, 1, 0, 5, 4, 1), ('s', 11, 10, 0, 1), ('a', 5, 0), ('a', 7, 0), ('s', 7, 8, 0, 2, 7, 1), ('s', 5, 6, 0, 0, 5, 1), ('a', 11, 1)), (11, None, None, None), (None, None, None), (9, 11, 4, 9, 11, 12))),
    (((('s', 9, 11, 0, 4, 8, 1), ('a', 1, 0)), (8, None, None, None), (None, None, None), (6, 8, 4, 6, 8, 15)),
     ((('a', 3, 1), ('s', 3, 1, 1, 5, 1, 0), ('s', 11, 10, 1, 1, 10, 0)), (None, None, None, None), (None, None, None), (0, 4, 3, 9, 11, 3))),
    (((('s', 4, 5, 1, 0, 5, 0), ('s', 1, 2, 0, 3, 7, 1), ('a', 5, 0), ('a', 7, 0), ('a', 7, 1), ('t', 5)), (7, None, None, None), (None, None, None), (3, 6, 17, 6, 7, 8)),
     ((('a', 5, 1), ('a', 7, 1), ('t', 3)), (3, None, None, None), (None, None, None), (11, 3, 15, 0, 3, 7))),
    (((('a', 1, 1), ('a', 9, 1), ('s', 9, 11, 1, 4), ('a', 11, 0), ('s', 11, 10, 0, 1)), (None, None, None, None), (None, None, None), (3, 4, 9, 6, 7, 9)),
     ((('a', 1, 0), ('a', 10, 0)), (7, None, None, None), (None, None, None), (3, 7, 12, 9, 11, 7))),
    (((), (1, None, None, None), (None, None, None), (7, 1, 4, 7, 1, 17)),
     ((), (None, None, None, None), (None, None, None), (3, 7, 5, 9, 11, 5))),
    (((('s', 1, 2, 1, 3, 2, 0), ('t', 1), ('t', 2)), (9, None, None, None), (None, None, None), (8, 9, 14, 3, 6, 13)),
     ((('s', 7, 8, 1, 2, 8, 0), ('t', 1), ('t', 5)), (5, None, None, None), (None, None, None), (0, 4, 13, 3, 5, 17))),
    (((('a', 5, 1),), (None, None, None, None), (None, None, None), (8, 9, 1, 1, 3, 14)),
     ((('a', 8, 0), ('s', 8, 2, 0, 5, 1, 1), ('a', 1, 1)), (1, None, None, None), (None, None, None), (0, 5, 1, 5, 1, 12))),
    (((), (None, None, None, None), (None, None, None), (7, 8, 13, 0, 1, 5)),
     ((('s', 5, 6, 1, 0, 6, 0), ('s', 1, 2, 1, 3), ('a', 6, 0)), (None, None, None, None), (12, None, None), (7, 1, 15, 7, 11, 1))),
    (((('a', 11, 1), ('a', 2, 0)), (None, None, None, None), (None, None, None), (0, 1, 5, 3, 7, 5)),
     ((('t', 4), ('a', 10, 1)), (None, None, None, None), (None, None, None), (7, 11, 1, 1, 3, 16))),
    (((('s', 11, 10, 1, 1),), (5, 11, None, None), (None, None, None), (4, 6, 11, 5, 11, 14)),
     ((), (10, None, None, None), (7, None, None), (1, 3, 10, 4, 10, 16))),
    (((), (None, None, None, None), (14, None, None), (7, 5, 15, 0, 1, 11)),
     ((('a', 8, 1),), (8, None, None, None), (None, None, None), (5, 10, 13, 1, 8, 17))),
    (((('a', 10, 0), ('a', 2, 1), ('t', 0)), (None, None, None, None), (None, None, None), (11, 0, 15, 6, 8, 12)),
     ((('a', 2, 0),), (None, None, None, None), (None, None, None), (5, 9, 8, 8, 0, 15))),
    (((('t', 4),), (2, None, None, None), (15, None, None), (3, 6, 16, 2, 0, 13)),
     ((('a', 6, 1),), (None, None, None, None), (5, 15, None), (8, 0, 16, 10, 11, 8))),
    (((), (None, None, None, None), (6, 13, None), (9, 2, 5, 4, 8, 2)),
     ((('a', 2, 1), ('t', 2)), (6, None, None, None), (16, None, None), (0, 6, 14, 1, 3, 6))),
    (((('a', 10, 1),), (None, None, None, None), (9, 4, 8), (7, 2, 16, 5, 2, 17)),
     ((), (None, None, None, None), (14, 1, 3), (4, 8, 6, 8, 6, 13))),
    (((), (10, None, None, None), (16, 2, 17), (11, 10, 7, 11, 10, 12)),
     ((), (None, None, None, None), (4, 8, 13), (9, 10, 6, 0, 10, 2))),
    (((), (None, None, None, None), (7, 11, 12), (1, 3, 10, 5, 0, 10)),
     ((), (2, None, None, None), (9, 10, None), (6, 2, 17, 11, 0, 2))),
)

TAIL = (
    (1, 3, 5, 0, 10),
    (6, 17, 11, 0, 2),
)

SLOTS = len(OFFSETS[0])
EXTRA = len(SHARED[0])
HELD = SLOTS + EXTRA
NONE = 31
GROUP = 64


def words(values, bits=5):
    each = 30 // bits
    return [sum(v * (1 << bits * k) for k, v in enumerate(values[s:s + each])) for s in range(0, len(values), each)]


def lookup(packed, n, bits=5):
    each = 30 // bits
    word = packed[0]
    for k, w in enumerate(packed[1:], 1):
        word = jnp.where(n >= each * k, w, word)
    return lax.rem(lax.shift_right_logical(word, bits * lax.rem(n, each)), 1 << bits)


def of_core(core, lists, bits=5):
    return [jnp.where(core == 0, jnp.asarray(a, jnp.int32), jnp.asarray(b, jnp.int32))
            for a, b in zip(*(words(v, bits) for v in lists))]


def column(which, place, k):
    return [NONE if pair[which][place][k] is None else pair[which][place][k] for pair in STEPS]


def kernel(chunks, emb_ref, lab_ref, out_ref, emb, ids, buf, labels, label_rows, row_best, column_best, outgoing,
           incoming, load_sem, send_sem, recv_sem, give_sem, take_sem, label_send, label_recv, label_give,
           label_take, result_send, result_recv):
    rows, width = emb.shape
    part = rows // chunks
    load = pltpu.make_async_copy(emb_ref, emb, load_sem.at[0])
    load.start()
    load_ids = pltpu.make_async_copy(lab_ref, ids, load_sem.at[1])
    load_ids.start()
    gx = lax.axis_index("grp")
    mem = lax.axis_index("mem")
    core = lax.rem(mem, 2)
    other = 1 - core
    gy = lax.rem(mem // 2, SIDE)
    gz = mem // (2 * SIDE)

    def at(offset, on):
        x, y, z = (lax.rem(g + k, SIDE) for g, k in zip((gx, gy, gz), offset))
        return (x, (z * SIDE + y) * 2 + on)

    near = [at(direction, core) for direction in DIRS]
    barrier = pltpu.get_barrier_semaphore()
    for device in near:
        pl.semaphore_signal(barrier, inc=1, device_id=device, device_id_type=MESH)
    pl.semaphore_signal(barrier, inc=1, device_id=(gx, mem + 1 - 2 * core), device_id_type=MESH)

    def chunk_of(slot, h):
        return buf.at[slot, pl.ds(h * part, part)]

    def relay(source, target, h, direction):
        return pltpu.make_async_remote_copy(
            src_ref=chunk_of(source, h), dst_ref=chunk_of(target, h),
            send_sem=send_sem.at[target, h], recv_sem=recv_sem.at[target, h],
            device_id=near[direction], device_id_type=MESH)

    def relay_label(source, target, direction):
        return pltpu.make_async_remote_copy(
            src_ref=labels.at[source], dst_ref=labels.at[target],
            send_sem=label_send.at[target], recv_sem=label_recv.at[target],
            device_id=near[direction], device_id_type=MESH)

    def send(source, target, h, direction):
        if h == 0:
            relay_label(source, target, direction).start()
        relay(source, target, h, direction).start()

    def share(slot, k, h):
        return pltpu.make_async_remote_copy(
            src_ref=chunk_of(slot, h), dst_ref=chunk_of(SLOTS + k, h),
            send_sem=give_sem.at[k, h], recv_sem=take_sem.at[k, h],
            device_id=(gx, mem + 1 - 2 * core), device_id_type=MESH)

    def share_label(slot, k):
        return pltpu.make_async_remote_copy(
            src_ref=labels.at[slot], dst_ref=labels.at[SLOTS + k],
            send_sem=label_give.at[k], recv_sem=label_take.at[k],
            device_id=(gx, mem + 1 - 2 * core), device_id_type=MESH)

    def give(which, slot, h):
        if slot in SHARED[1 - which]:
            k = SHARED[1 - which].index(slot)
            if h == 0:
                share_label(slot, k).start()
            share(slot, k, h).start()

    homes = []
    for which in (0, 1):
        offsets = OFFSETS[which] + tuple(OFFSETS[1 - which][k] for k in SHARED[which])
        homes.append([at([SIDE - k for k in o], which if n < SLOTS else 1 - which) for n, o in enumerate(offsets)])
    home_x, home_mem = (of_core(core, [[h[k] for h in held] for held in homes]) for k in (0, 1))

    load_ids.wait()
    labels[0] = ids[...].astype(jnp.float32)
    load.wait()
    for h in range(chunks):
        e = emb[pl.ds(h * part, part)]
        squares = jnp.sum(e * e, axis=1, keepdims=True)
        buf[0, pl.ds(h * part, part)] = (e * lax.rsqrt(squares + 1e-06)).astype(jnp.bfloat16)
        if h == 0:
            pl.semaphore_wait(barrier, len(DIRS) + 1)
        for which in (0, 1):
            @pl.when(core == which)
            def _(which=which, h=h):
                for move in FIRST_SENDS[which]:
                    if move[2] == h:
                        send(*move)

    for which in (0, 1):
        @pl.when(core == which)
        def _(which=which):
            for h in range(chunks):
                give(which, 0, h)

    def clear(slot, carry):
        column_best[slot] = jnp.full(column_best.shape[1:], FILL, jnp.float32)

        @pl.when(slot < SLOTS)
        def _():
            row_best[slot] = jnp.full(row_best.shape[1:], FILL, jnp.float32)
        return carry

    lax.fori_loop(0, HELD, clear, 0)

    def spread(slot):
        label_rows[slot] = jnp.broadcast_to(labels[slot], (128, rows)).T

    def tile(left, right, own=False):
        sims = lax.dot_general(jnp.concatenate([buf[a] for a in left], axis=0), buf[right], (((1,), (1,)), ((), ())),
                               preferred_element_type=jnp.float32)
        names = labels[right]
        lanes = [slice(k, k + 128) for k in range(0, rows, 128)]
        high = [column_best[right, :, k] for k in lanes]
        for n, a in enumerate(left):
            for r in range(0, rows, GROUP):
                mine = label_rows[a, pl.ds(r, GROUP)]
                top = row_best[a, pl.ds(r, GROUP)]
                for m, k in enumerate(lanes):
                    keep = mine == names[:, k]
                    if own:
                        keep = keep & (lax.broadcasted_iota(jnp.int32, (GROUP, 128), 0) + r
                                       != lax.broadcasted_iota(jnp.int32, (GROUP, 128), 1) + m * 128)
                    scores = jnp.where(keep, sims[n * rows + r:n * rows + r + GROUP, k], FILL)
                    top = jnp.maximum(top, scores)
                    high[m] = jnp.maximum(high[m], jnp.max(scores.reshape(GROUP // 8, 8, 128), axis=0))
                row_best[a, pl.ds(r, GROUP)] = top
        for m, k in enumerate(lanes):
            column_best[right, :, k] = high[m]

    def answer(slot):
        return pltpu.make_async_remote_copy(
            src_ref=outgoing.at[slot], dst_ref=incoming.at[slot],
            send_sem=result_send.at[slot], recv_sem=result_recv,
            device_id=(lookup(home_x, slot), lookup(home_mem, slot)), device_id_type=MESH)

    def finish(slot):
        by_column = jnp.max(column_best[slot], axis=0, keepdims=True)

        @pl.when(slot < SLOTS)
        def _():
            outgoing[slot] = jnp.maximum(by_column, jnp.max(row_best[slot].T, axis=0, keepdims=True))

        @pl.when(slot >= SLOTS)
        def _():
            outgoing[slot] = by_column

        @pl.when(slot > 0)
        def _():
            answer(slot).start()

    def arrived(which, slot, h):
        pltpu.make_async_copy(chunk_of(slot, h), chunk_of(slot, h), recv_sem.at[slot, h]).wait()
        if h == 0:
            pltpu.make_async_copy(labels.at[slot], labels.at[slot], label_recv.at[slot]).wait()
        give(which, slot, h)

    def taken(k):
        for h in range(chunks):
            pltpu.make_async_copy(chunk_of(SLOTS + k, h), chunk_of(SLOTS + k, h), take_sem.at[k, h]).wait()
        pltpu.make_async_copy(labels.at[SLOTS + k], labels.at[SLOTS + k], label_take.at[k]).wait()

    def sent(slot, h):
        relay(0, slot, h, 0).wait_send()

    def moves(n):
        for which in (0, 1):
            todo = STEPS[n][which][0]
            if todo:
                @pl.when(core == which)
                def _(which=which, todo=todo):
                    for op in todo:
                        if op[0] == "a":
                            arrived(which, *op[1:])
                        elif op[0] == "t":
                            taken(op[1])
                        else:
                            if len(op) > 5:
                                sent(*op[5:])
                            send(*op[1:5])

    def table(place):
        return [of_core(core, [column(w, place, k) for w in (0, 1)]) for k in range(len(STEPS[0][0][place]))]

    to_open, to_finish, to_compare = table(1), table(2), table(3)
    spread(0)
    tile((0,), 0, own=True)

    def step(n, carry):
        for g in range(0, len(STEPS), 6):
            @pl.when(lax.div(n, 6) == g // 6)
            def _(g=g):
                for k in range(g, min(g + 6, len(STEPS))):
                    @pl.when(n == k)
                    def _(k=k):
                        moves(k)
        for listed, act in ((to_open, spread), (to_finish, finish)):
            for packed in listed:
                slot = lookup(packed, n)

                @pl.when(slot != NONE)
                def _(slot=slot, act=act):
                    act(slot)
        units = [lookup(packed, n) for packed in to_compare]
        for k in range(0, len(units), 3):
            tile(units[k:k + 2], units[k + 2])
        return carry

    lax.fori_loop(0, len(STEPS), step, 0)
    left = max(len(t) for t in TAIL)
    ends = of_core(core, [(list(t) + [NONE] * left)[:left] for t in TAIL])
    ended = [lookup(ends, n) for n in range(left)]
    for slot in ended:
        held = jnp.where(slot == NONE, 0, slot)
        by_row = jnp.max(row_best[jnp.minimum(held, SLOTS - 1)].T, axis=0, keepdims=True)
        by_column = jnp.max(column_best[held], axis=0, keepdims=True)
        outgoing[held] = jnp.where(held < SLOTS, jnp.maximum(by_row, by_column), by_column)
    for slot in ended:
        @pl.when((slot != NONE) & (slot > 0))
        def _(slot=slot):
            answer(slot).start()
    incoming[0] = outgoing[0]

    for which in (0, 1):
        @pl.when(core == which)
        def _(which=which):
            for move in LAST_SENDS[which]:
                sent(*move)
    for k in range(EXTRA):
        for h in range(chunks):
            share(0, k, h).wait_send()
        share_label(0, k).wait_send()
    for slot in range(1, SLOTS):
        relay_label(0, slot, 0).wait_send()
    for slot in range(1, HELD):
        answer(slot).wait_send()
    rest = incoming.at[pl.ds(1, HELD - 1)]
    pltpu.make_async_copy(rest, rest, result_recv).wait()
    out_ref[...] = jnp.max(incoming[...], axis=0).reshape(rows)


def body(embeddings, cluster_ids):
    rows, width = embeddings.shape
    chunks = 1 + max(h for sends in LAST_SENDS for _, h in sends)
    dma = pltpu.SemaphoreType.DMA
    return pl.pallas_call(
        functools.partial(kernel, chunks),
        out_shape=jax.ShapeDtypeStruct((rows,), jnp.float32),
        in_specs=[pl.BlockSpec(memory_space=pl.ANY), pl.BlockSpec(memory_space=pl.ANY)],
        out_specs=pl.BlockSpec(memory_space=pltpu.VMEM),
        scratch_shapes=[
            pltpu.VMEM((rows, width), jnp.float32),
            pltpu.VMEM((1, rows), jnp.int32),
            pltpu.VMEM((HELD, rows, width), jnp.bfloat16),
            pltpu.VMEM((HELD, 1, rows), jnp.float32),
            pltpu.VMEM((SLOTS, rows, 128), jnp.float32),
            pltpu.VMEM((SLOTS, rows, 128), jnp.float32),
            pltpu.VMEM((HELD, 8, rows), jnp.float32),
            pltpu.VMEM((HELD, 1, rows), jnp.float32),
            pltpu.VMEM((HELD, 1, rows), jnp.float32),
            dma((2,)), dma((SLOTS, chunks)), dma((SLOTS, chunks)), dma((EXTRA, chunks)), dma((EXTRA, chunks)),
            dma((SLOTS,)), dma((SLOTS,)), dma((EXTRA,)), dma((EXTRA,)), dma((HELD,)), dma,
        ],
        compiler_params=pltpu.CompilerParams(
            collective_id=0, has_side_effects=True, vmem_limit_bytes=VMEM_BYTES),
    )(embeddings, cluster_ids.reshape(1, rows))


def solution(mesh):
    return jax.shard_map(
        body,
        mesh=mesh,
        in_specs=(P(("grp", "mem"), None), P(("grp", "mem"), None)),
        out_specs=P(("grp", "mem")),
        check_vma=False,
    )
```

```python
import functools

import jax
import jax.numpy as jnp
from jax import lax
from jax.experimental import pallas as pl
from jax.experimental.pallas import tpu as pltpu
from jax.sharding import PartitionSpec as P

FILL = -4.0
MESH = pl.DeviceIdType.MESH
SIDE = 4
VMEM_BYTES = 64 * 1024 * 1024 - 512 * 1024
DIRS = ((1, 0, 0), (3, 0, 0), (0, 1, 0), (0, 3, 0), (0, 0, 1), (0, 0, 3))

OFFSETS = (
    ((0, 0, 0), (3, 0, 0), (3, 1, 0), (2, 1, 0), (0, 2, 0), (2, 2, 0),
     (0, 3, 0), (0, 0, 1), (0, 0, 2), (1, 0, 2), (0, 0, 3), (1, 0, 3)),
    ((0, 0, 0), (1, 0, 0), (0, 1, 0), (3, 1, 0), (1, 2, 0), (3, 2, 0),
     (1, 3, 0), (1, 0, 1), (1, 0, 2), (2, 0, 2), (1, 0, 3), (2, 0, 3)),
)

SHARED = ((2, 3, 5, 6, 7, 11), (0, 2, 4, 6, 9, 11))

FIRST_SENDS = (
    ((0, 1, 0, 1), (0, 10, 0, 5), (0, 6, 0, 3), (0, 7, 0, 4)),
    ((0, 1, 0, 0), (0, 2, 0, 2)),
)

LAST_SENDS = (
    ((1, 1), (2, 1), (3, 0), (3, 1), (4, 0), (5, 0), (5, 1), (6, 0), (6, 1), (7, 1), (8, 0), (8, 1), (9, 0), (9, 1), (10, 1)),
    ((3, 0), (3, 1), (4, 0), (4, 1), (5, 0), (5, 1), (6, 1), (7, 0), (7, 1), (8, 0), (8, 1), (9, 0), (9, 1), (10, 1), (11, 0), (11, 1)),
)

STEPS = (
    (((('s', 0, 7, 1, 4, 1, 0), ('s', 0, 1, 1, 1), ('s', 0, 10, 1, 5), ('a', 10, 0), ('a', 6, 0), ('a', 1, 0), ('s', 10, 11, 0, 0, 10, 0), ('s', 0, 6, 1, 3), ('s', 1, 2, 0, 2), ('a', 1, 1), ('a', 7, 1), ('s', 1, 2, 1, 2, 11, 0), ('a', 10, 1), ('s', 10, 11, 1, 0, 7, 0), ('s', 6, 4, 0, 3), ('a', 6, 1), ('s', 10, 8, 0, 5, 2, 0), ('a', 2, 0), ('a', 7, 0), ('s', 7, 8, 1, 4), ('s', 2, 3, 0, 1), ('a', 2, 1), ('t', 0), ('a', 11, 0), ('s', 6, 4, 1, 3, 11, 1), ('s', 11, 9, 0, 5), ('s', 2, 3, 1, 1), ('t', 1)), (10, 2, 6, 7), (None, None, None), (10, 2, 7, 6, 7, 1)),
     ((('t', 0), ('s', 0, 2, 1, 2, 2, 0), ('s', 0, 1, 1, 0), ('a', 2, 0), ('a', 1, 0), ('s', 1, 7, 0, 4, 1, 0), ('s', 1, 6, 0, 3), ('s', 2, 3, 0, 1), ('s', 1, 10, 0, 5), ('a', 1, 1), ('a', 2, 1), ('s', 2, 3, 1, 1, 2, 1), ('s', 1, 10, 1, 5), ('s', 1, 7, 1, 4), ('a', 10, 0), ('a', 3, 0), ('s', 1, 6, 1, 3), ('s', 10, 11, 0, 0, 6, 0), ('s', 3, 5, 0, 2, 1, 1), ('a', 6, 0), ('t', 3), ('a', 7, 0), ('a', 3, 1), ('a', 7, 1), ('a', 10, 1)), (3, 10, 1, 2), (None, None, None), (3, 10, 15, 1, 2, 0))),
    (((('a', 11, 1), ('a', 4, 0)), (1, None, None, None), (None, None, None), (1, 6, 12, 1, 6, 11)),
     ((('s', 7, 8, 0, 4), ('s', 10, 11, 1, 0, 10, 0), ('s', 3, 5, 1, 2), ('a', 11, 0), ('a', 6, 1), ('t', 1)), (7, None, None, None), (None, None, None), (7, 10, 6, 2, 3, 6))),
    (((('a', 8, 0), ('a', 8, 1)), (8, None, None, None), (None, None, None), (7, 10, 13, 6, 8, 2)),
     ((('a', 5, 0),), (None, None, None, None), (None, None, None), (0, 1, 12, 0, 2, 7))),
    (((), (None, None, None, None), (None, None, None), (0, 6, 7, 7, 10, 12)),
     ((('s', 7, 8, 1, 4), ('s', 6, 4, 0, 3)), (6, None, None, None), (None, None, None), (1, 6, 13, 0, 1, 10))),
    (((('t', 3), ('a', 3, 0), ('s', 3, 5, 0, 2, 4, 1), ('s', 8, 9, 1, 0), ('a', 9, 0), ('a', 3, 1), ('a', 4, 1)), (11, None, None, None), (None, None, None), (8, 11, 13, 0, 2, 4)),
     ((('t', 5), ('a', 11, 1)), (11, None, None, None), (None, None, None), (10, 11, 13, 2, 3, 12))),
    (((), (None, None, None, None), (None, None, None), (1, 6, 10, 7, 8, 15)),
     ((('a', 5, 1), ('s', 6, 4, 1, 3)), (None, None, None, None), (None, None, None), (6, 11, 12, 2, 3, 1))),
    (((), (None, None, None, None), (None, None, None), (10, 11, 15, 1, 6, 0)),
     ((('a', 8, 0),), (None, None, None, None), (None, None, None), (0, 3, 11, 3, 10, 7))),
    (((), (3, 4, None, None), (None, None, None), (3, 0, 12, 4, 3, 11)),
     ((('s', 8, 9, 0, 0), ('t', 2)), (None, None, None, None), (None, None, None), (6, 7, 11, 1, 10, 14))),
    (((('t', 4), ('t', 5), ('s', 3, 5, 1, 2)), (None, None, None, None), (None, None, None), (1, 3, 17, 1, 6, 8)),
     ((('a', 8, 1), ('s', 11, 9, 1, 5)), (None, None, None, None), (None, None, None), (2, 3, 8, 10, 11, 5))),
    (((('t', 2),), (None, None, None, None), (None, None, None), (0, 6, 3, 8, 4, 12)),
     ((), (5, None, None, None), (None, None, None), (5, 6, 8, 10, 7, 12))),
    (((('a', 9, 1),), (9, None, None, None), (12, None, None), (7, 8, 14, 10, 9, 14)),
     ((), (None, None, None, None), (6, 12, None), (7, 11, 15, 0, 1, 17))),
    (((('a', 5, 0),), (None, None, None, None), (14, None, None), (6, 0, 9, 4, 3, 16)),
     ((('a', 4, 0),), (8, None, None, None), (7, None, None), (5, 8, 17, 8, 0, 14))),
    (((), (None, None, None, None), (6, None, None), (7, 8, 3, 7, 8, 4)),
     ((('a', 4, 1),), (4, None, None, None), (None, None, None), (10, 11, 4, 8, 4, 13))),
    (((), (None, None, None, None), (3, None, None), (4, 9, 13, 1, 2, 16)),
     ((('t', 4),), (None, None, None, None), (None, None, None), (1, 2, 4, 0, 4, 16))),
    (((('a', 5, 1),), (None, None, None, None), (13, None, None), (9, 0, 15, 4, 7, 5)),
     ((('a', 9, 1), ('a', 9, 0)), (None, None, None, None), (1, 16, None), (0, 3, 9, 2, 3, 10))),
    (((), (5, None, None, None), (15, None, None), (7, 5, 17, 1, 4, 9)),
     ((), (None, None, None, None), (2, 3, 10), (11, 5, 14, 4, 0, 17))),
    (((), (None, None, None, None), (7, 17, 1), (0, 2, 4, 8, 11, 5)),
     ((), (9, None, None, None), (11, 14, 17), (9, 0, 13, 8, 0, 15))),
    (((), (None, None, None, None), (9, 0, 4), (10, 11, 16, 10, 11, 2)),
     ((), (None, None, None, None), (13, 15, None), (5, 8, 4, 5, 0, 9))),
)

TAIL = (
    (8, 5, 16, 10, 11, 2),
    (8, 4, 5, 0, 9),
)

SLOTS = len(OFFSETS[0])
EXTRA = len(SHARED[0])
HELD = SLOTS + EXTRA
NONE = 31
GROUP = 64


def words(values, bits=5):
    each = 30 // bits
    return [sum(v * (1 << bits * k) for k, v in enumerate(values[s:s + each])) for s in range(0, len(values), each)]


def lookup(packed, n, bits=5):
    each = 30 // bits
    word = packed[0]
    for k, w in enumerate(packed[1:], 1):
        word = jnp.where(n >= each * k, w, word)
    return lax.rem(lax.shift_right_logical(word, bits * lax.rem(n, each)), 1 << bits)


def of_core(core, lists, bits=5):
    return [jnp.where(core == 0, jnp.asarray(a, jnp.int32), jnp.asarray(b, jnp.int32))
            for a, b in zip(*(words(v, bits) for v in lists))]


def column(which, place, k):
    return [NONE if pair[which][place][k] is None else pair[which][place][k] for pair in STEPS]


def kernel(chunks, emb_ref, lab_ref, out_ref, emb, ids, buf, labels, label_rows, row_best, column_best, outgoing,
           incoming, load_sem, send_sem, recv_sem, give_sem, take_sem, label_send, label_recv, label_give,
           label_take, result_send, result_recv):
    rows, width = emb.shape
    part = rows // chunks
    load = pltpu.make_async_copy(emb_ref, emb, load_sem.at[0])
    load.start()
    load_ids = pltpu.make_async_copy(lab_ref, ids, load_sem.at[1])
    load_ids.start()
    gx = lax.axis_index("grp")
    mem = lax.axis_index("mem")
    core = lax.rem(mem, 2)
    other = 1 - core
    gy = lax.rem(mem // 2, SIDE)
    gz = mem // (2 * SIDE)

    def at(offset, on):
        x, y, z = (lax.rem(g + k, SIDE) for g, k in zip((gx, gy, gz), offset))
        return (x, (z * SIDE + y) * 2 + on)

    near = [at(direction, core) for direction in DIRS]
    barrier = pltpu.get_barrier_semaphore()
    for device in near:
        pl.semaphore_signal(barrier, inc=1, device_id=device, device_id_type=MESH)
    pl.semaphore_signal(barrier, inc=1, device_id=(gx, mem + 1 - 2 * core), device_id_type=MESH)

    def chunk_of(slot, h):
        return buf.at[slot, pl.ds(h * part, part)]

    def relay(source, target, h, direction):
        return pltpu.make_async_remote_copy(
            src_ref=chunk_of(source, h), dst_ref=chunk_of(target, h),
            send_sem=send_sem.at[target, h], recv_sem=recv_sem.at[target, h],
            device_id=near[direction], device_id_type=MESH)

    def relay_label(source, target, direction):
        return pltpu.make_async_remote_copy(
            src_ref=labels.at[source], dst_ref=labels.at[target],
            send_sem=label_send.at[target], recv_sem=label_recv.at[target],
            device_id=near[direction], device_id_type=MESH)

    def send(source, target, h, direction):
        if h == 0:
            relay_label(source, target, direction).start()
        relay(source, target, h, direction).start()

    def share(slot, k, h):
        return pltpu.make_async_remote_copy(
            src_ref=chunk_of(slot, h), dst_ref=chunk_of(SLOTS + k, h),
            send_sem=give_sem.at[k, h], recv_sem=take_sem.at[k, h],
            device_id=(gx, mem + 1 - 2 * core), device_id_type=MESH)

    def share_label(slot, k):
        return pltpu.make_async_remote_copy(
            src_ref=labels.at[slot], dst_ref=labels.at[SLOTS + k],
            send_sem=label_give.at[k], recv_sem=label_take.at[k],
            device_id=(gx, mem + 1 - 2 * core), device_id_type=MESH)

    def give(which, slot, h):
        if slot in SHARED[1 - which]:
            k = SHARED[1 - which].index(slot)
            if h == 0:
                share_label(slot, k).start()
            share(slot, k, h).start()

    homes = []
    for which in (0, 1):
        offsets = OFFSETS[which] + tuple(OFFSETS[1 - which][k] for k in SHARED[which])
        homes.append([at([SIDE - k for k in o], which if n < SLOTS else 1 - which) for n, o in enumerate(offsets)])
    home_x, home_mem = (of_core(core, [[h[k] for h in held] for held in homes]) for k in (0, 1))

    load_ids.wait()
    labels[0] = ids[...].astype(jnp.float32)
    load.wait()
    for h in range(chunks):
        e = emb[pl.ds(h * part, part)]
        squares = jnp.sum(e * e, axis=1, keepdims=True)
        buf[0, pl.ds(h * part, part)] = (e * lax.rsqrt(squares + 1e-06)).astype(jnp.bfloat16)
        if h == 0:
            pl.semaphore_wait(barrier, len(DIRS) + 1)
        for which in (0, 1):
            @pl.when(core == which)
            def _(which=which, h=h):
                for move in FIRST_SENDS[which]:
                    if move[2] == h:
                        send(*move)

    for which in (0, 1):
        @pl.when(core == which)
        def _(which=which):
            for h in range(chunks):
                give(which, 0, h)

    def clear(slot, carry):
        column_best[slot] = jnp.full(column_best.shape[1:], FILL, jnp.float32)

        @pl.when(slot < SLOTS)
        def _():
            row_best[slot] = jnp.full(row_best.shape[1:], FILL, jnp.float32)
        return carry

    lax.fori_loop(0, HELD, clear, 0)

    def spread(slot):
        label_rows[slot] = jnp.broadcast_to(labels[slot], (128, rows)).T

    def tile(left, right, own=False):
        sims = lax.dot_general(jnp.concatenate([buf[a] for a in left], axis=0), buf[right], (((1,), (1,)), ((), ())),
                               preferred_element_type=jnp.float32)
        names = labels[right]
        lanes = [slice(k, k + 128) for k in range(0, rows, 128)]
        high = [column_best[right, :, k] for k in lanes]
        for n, a in enumerate(left):
            for r in range(0, rows, GROUP):
                mine = label_rows[a, pl.ds(r, GROUP)]
                top = row_best[a, pl.ds(r, GROUP)]
                for m, k in enumerate(lanes):
                    keep = mine == names[:, k]
                    if own:
                        keep = keep & (lax.broadcasted_iota(jnp.int32, (GROUP, 128), 0) + r
                                       != lax.broadcasted_iota(jnp.int32, (GROUP, 128), 1) + m * 128)
                    scores = jnp.where(keep, sims[n * rows + r:n * rows + r + GROUP, k], FILL)
                    top = jnp.maximum(top, scores)
                    high[m] = jnp.maximum(high[m], jnp.max(scores.reshape(GROUP // 8, 8, 128), axis=0))
                row_best[a, pl.ds(r, GROUP)] = top
        for m, k in enumerate(lanes):
            column_best[right, :, k] = high[m]

    def answer(slot):
        return pltpu.make_async_remote_copy(
            src_ref=outgoing.at[slot], dst_ref=incoming.at[slot],
            send_sem=result_send.at[slot], recv_sem=result_recv,
            device_id=(lookup(home_x, slot), lookup(home_mem, slot)), device_id_type=MESH)

    def finish(slot):
        by_column = jnp.max(column_best[slot], axis=0, keepdims=True)

        @pl.when(slot < SLOTS)
        def _():
            outgoing[slot] = jnp.maximum(by_column, jnp.max(row_best[slot].T, axis=0, keepdims=True))

        @pl.when(slot >= SLOTS)
        def _():
            outgoing[slot] = by_column

        @pl.when(slot > 0)
        def _():
            answer(slot).start()

    def arrived(which, slot, h):
        pltpu.make_async_copy(chunk_of(slot, h), chunk_of(slot, h), recv_sem.at[slot, h]).wait()
        if h == 0:
            pltpu.make_async_copy(labels.at[slot], labels.at[slot], label_recv.at[slot]).wait()
        give(which, slot, h)

    def taken(k):
        for h in range(chunks):
            pltpu.make_async_copy(chunk_of(SLOTS + k, h), chunk_of(SLOTS + k, h), take_sem.at[k, h]).wait()
        pltpu.make_async_copy(labels.at[SLOTS + k], labels.at[SLOTS + k], label_take.at[k]).wait()

    def sent(slot, h):
        relay(0, slot, h, 0).wait_send()

    def moves(n):
        for which in (0, 1):
            todo = STEPS[n][which][0]
            if todo:
                @pl.when(core == which)
                def _(which=which, todo=todo):
                    for op in todo:
                        if op[0] == "a":
                            arrived(which, *op[1:])
                        elif op[0] == "t":
                            taken(op[1])
                        else:
                            if len(op) > 5:
                                sent(*op[5:])
                            send(*op[1:5])

    def table(place):
        return [of_core(core, [column(w, place, k) for w in (0, 1)]) for k in range(len(STEPS[0][0][place]))]

    to_open, to_finish, to_compare = table(1), table(2), table(3)
    spread(0)
    tile((0,), 0, own=True)

    def step(n, carry):
        for g in range(0, len(STEPS), 6):
            @pl.when(lax.div(n, 6) == g // 6)
            def _(g=g):
                for k in range(g, min(g + 6, len(STEPS))):
                    @pl.when(n == k)
                    def _(k=k):
                        moves(k)
        for listed, act in ((to_open, spread), (to_finish, finish)):
            for packed in listed:
                slot = lookup(packed, n)

                @pl.when(slot != NONE)
                def _(slot=slot, act=act):
                    act(slot)
        units = [lookup(packed, n) for packed in to_compare]
        for k in range(0, len(units), 3):
            tile(units[k:k + 2], units[k + 2])
        return carry

    lax.fori_loop(0, len(STEPS), step, 0)
    left = max(len(t) for t in TAIL)
    ends = of_core(core, [(list(t) + [NONE] * left)[:left] for t in TAIL])
    ended = [lookup(ends, n) for n in range(left)]
    for slot in ended:
        held = jnp.where(slot == NONE, 0, slot)
        by_row = jnp.max(row_best[jnp.minimum(held, SLOTS - 1)].T, axis=0, keepdims=True)
        by_column = jnp.max(column_best[held], axis=0, keepdims=True)
        outgoing[held] = jnp.where(held < SLOTS, jnp.maximum(by_row, by_column), by_column)
    for slot in ended:
        @pl.when((slot != NONE) & (slot > 0))
        def _(slot=slot):
            answer(slot).start()
    incoming[0] = outgoing[0]

    for which in (0, 1):
        @pl.when(core == which)
        def _(which=which):
            for move in LAST_SENDS[which]:
                sent(*move)
    for k in range(EXTRA):
        for h in range(chunks):
            share(0, k, h).wait_send()
        share_label(0, k).wait_send()
    for slot in range(1, SLOTS):
        relay_label(0, slot, 0).wait_send()
    for slot in range(1, HELD):
        answer(slot).wait_send()
    rest = incoming.at[pl.ds(1, HELD - 1)]
    pltpu.make_async_copy(rest, rest, result_recv).wait()
    out_ref[...] = jnp.max(incoming[...], axis=0).reshape(rows)


def body(embeddings, cluster_ids):
    rows, width = embeddings.shape
    chunks = 1 + max(h for sends in LAST_SENDS for _, h in sends)
    dma = pltpu.SemaphoreType.DMA
    return pl.pallas_call(
        functools.partial(kernel, chunks),
        out_shape=jax.ShapeDtypeStruct((rows,), jnp.float32),
        in_specs=[pl.BlockSpec(memory_space=pl.ANY), pl.BlockSpec(memory_space=pl.ANY)],
        out_specs=pl.BlockSpec(memory_space=pltpu.VMEM),
        scratch_shapes=[
            pltpu.VMEM((rows, width), jnp.float32),
            pltpu.VMEM((1, rows), jnp.int32),
            pltpu.VMEM((HELD, rows, width), jnp.bfloat16),
            pltpu.VMEM((HELD, 1, rows), jnp.float32),
            pltpu.VMEM((SLOTS, rows, 128), jnp.float32),
            pltpu.VMEM((SLOTS, rows, 128), jnp.float32),
            pltpu.VMEM((HELD, 8, rows), jnp.float32),
            pltpu.VMEM((HELD, 1, rows), jnp.float32),
            pltpu.VMEM((HELD, 1, rows), jnp.float32),
            dma((2,)), dma((SLOTS, chunks)), dma((SLOTS, chunks)), dma((EXTRA, chunks)), dma((EXTRA, chunks)),
            dma((SLOTS,)), dma((SLOTS,)), dma((EXTRA,)), dma((EXTRA,)), dma((HELD,)), dma,
        ],
        compiler_params=pltpu.CompilerParams(
            collective_id=0, has_side_effects=True, vmem_limit_bytes=VMEM_BYTES),
    )(embeddings, cluster_ids.reshape(1, rows))


def solution(mesh):
    return jax.shard_map(
        body,
        mesh=mesh,
        in_specs=(P(("grp", "mem"), None), P(("grp", "mem"), None)),
        out_specs=P(("grp", "mem")),
        check_vma=False,
    )
```

```python
import functools

import jax
import jax.numpy as jnp
from jax import lax
from jax.experimental import pallas as pl
from jax.experimental.pallas import tpu as pltpu
from jax.sharding import PartitionSpec as P

FILL = -4.0
MESH = pl.DeviceIdType.MESH
SIDE = 4
VMEM_BYTES = 64 * 1024 * 1024 - 512 * 1024
DIRS = ((1, 0, 0), (3, 0, 0), (0, 1, 0), (0, 3, 0), (0, 0, 1), (0, 0, 3))

OFFSETS = (
    ((0, 0, 0), (1, 0, 0), (2, 0, 0), (0, 1, 0), (0, 2, 0), (0, 3, 0),
     (0, 0, 1), (3, 0, 1), (2, 0, 2), (3, 0, 2), (0, 2, 3), (0, 3, 3)),
    ((0, 0, 0), (0, 0, 3), (1, 0, 3), (2, 0, 3), (0, 1, 3), (0, 2, 3),
     (0, 3, 3), (3, 0, 0), (2, 0, 1), (3, 0, 1), (0, 2, 2), (0, 3, 2)),
)

SHARED = ((2, 4, 7, 8, 9, 11), (0, 1, 2, 7, 10, 11))

FIRST_SENDS = (
    ((0, 6, 0, 4), (0, 5, 0, 3), (0, 1, 0, 0), (0, 3, 0, 2)),
    ((0, 1, 0, 5), (0, 7, 0, 1)),
)

LAST_SENDS = (
    ((1, 0), (2, 0), (3, 0), (4, 0), (5, 0), (5, 1), (6, 1), (7, 0), (7, 1), (8, 0), (8, 1), (9, 1), (10, 0), (10, 1), (11, 0), (11, 1)),
    ((2, 0), (3, 1), (4, 0), (5, 0), (5, 1), (6, 1), (8, 0), (9, 1), (10, 0), (10, 1), (11, 0)),
)

STEPS = (
    (((('s', 0, 6, 1, 4, 6, 0), ('s', 0, 5, 1, 3), ('s', 0, 3, 1, 2), ('s', 0, 1, 1, 0), ('a', 1, 0), ('a', 6, 0), ('a', 5, 0), ('a', 3, 0), ('s', 6, 7, 0, 1), ('s', 5, 11, 0, 5), ('s', 1, 2, 0, 0, 1, 1), ('s', 3, 4, 0, 2), ('a', 5, 1), ('a', 3, 1), ('s', 5, 4, 1, 3), ('a', 1, 1), ('s', 5, 11, 1, 5), ('a', 6, 1)), (1, 3, None, None), (None, None, None), (0, 1, 6, 1, 3, 0)),
     ((('s', 0, 1, 1, 5, 1, 0), ('s', 0, 7, 1, 1, 7, 0), ('a', 1, 0), ('a', 7, 0), ('s', 1, 6, 0, 3), ('s', 1, 2, 0, 0), ('t', 0), ('s', 7, 9, 0, 4), ('s', 1, 4, 0, 2), ('a', 1, 1), ('a', 7, 1), ('s', 1, 6, 1, 3, 7, 1)), (1, 7, None, None), (None, None, None), (0, 1, 12, 1, 7, 0))),
    (((('t', 2), ('s', 6, 7, 1, 1, 3, 1)), (5, None, None, None), (None, None, None), (1, 3, 14, 3, 5, 1)),
     ((('s', 1, 4, 1, 2), ('s', 7, 9, 1, 4, 9, 0), ('a', 6, 0), ('s', 1, 2, 1, 0), ('a', 2, 0), ('a', 9, 0), ('s', 9, 8, 0, 1, 6, 0), ('s', 6, 11, 0, 5, 1, 1), ('a', 4, 0), ('s', 4, 5, 0, 2, 4, 1), ('a', 9, 1)), (9, None, None, None), (None, None, None), (7, 9, 1, 7, 9, 12))),
    (((('a', 7, 0), ('s', 7, 9, 0, 4), ('a', 11, 0)), (6, None, None, None), (None, None, None), (5, 6, 3, 5, 6, 14)),
     ((('s', 2, 3, 0, 0), ('a', 4, 1), ('s', 9, 8, 1, 1), ('t', 1), ('a', 6, 1), ('s', 6, 11, 1, 5)), (6, None, None, None), (None, None, None), (0, 1, 6, 0, 6, 4))),
    (((('s', 1, 2, 1, 0), ('s', 11, 10, 0, 3, 4, 1), ('a', 2, 0), ('a', 4, 1), ('a', 4, 0), ('t', 4)), (4, None, None, None), (None, None, None), (3, 5, 16, 5, 4, 6)),
     ((), (None, None, None, None), (None, None, None), (9, 6, 13, 7, 9, 6))),
    (((('t', 1), ('a', 7, 1), ('a', 11, 1), ('s', 7, 9, 1, 4), ('a', 9, 0)), (None, None, None, None), (None, None, None), (1, 6, 11, 3, 4, 7)),
     ((('a', 8, 0), ('a', 2, 1), ('a', 11, 0)), (4, None, None, None), (None, None, None), (6, 4, 12, 7, 9, 4))),
    (((('s', 11, 10, 1, 3), ('s', 9, 8, 0, 1, 9, 0)), (7, 11, None, None), (None, None, None), (4, 7, 1, 4, 11, 16)),
     ((('s', 4, 5, 1, 2, 2, 1), ('t', 5), ('t', 3)), (2, None, None, None), (None, None, None), (0, 1, 17, 2, 6, 15))),
    (((('t', 0), ('a', 2, 1)), (None, None, None, None), (None, None, None), (5, 6, 12, 0, 3, 2)),
     ((('a', 5, 0), ('s', 2, 3, 1, 0, 3, 0), ('s', 5, 10, 0, 5, 8, 1)), (None, None, None, None), (None, None, None), (4, 6, 2, 7, 9, 2))),
    (((), (2, None, None, None), (None, None, None), (0, 3, 2, 4, 2, 14)),
     ((('a', 3, 0), ('a', 11, 1), ('a', 8, 1)), (11, None, None, None), (None, None, None), (4, 9, 11, 4, 11, 13))),
    (((('a', 9, 1),), (None, None, None, None), (None, None, None), (7, 11, 13, 3, 4, 12)),
     ((('t', 2),), (None, None, None, None), (None, None, None), (4, 11, 13, 1, 6, 14))),
    (((('s', 9, 8, 1, 1, 2, 1),), (None, None, None, None), (None, None, None), (4, 7, 2, 0, 1, 9)),
     ((), (8, None, None, None), (4, None, None), (0, 2, 11, 11, 8, 14))),
    (((('a', 10, 0), ('a', 8, 0)), (None, None, None, None), (None, None, None), (5, 11, 7, 3, 4, 9)),
     ((('a', 5, 1), ('s', 5, 10, 1, 5, 11, 1)), (5, None, None, None), (None, None, None), (5, 0, 13, 2, 7, 5))),
    (((('a', 10, 1), ('t', 5), ('t', 3)), (10, None, None, None), (7, None, None), (10, 0, 12, 3, 4, 15)),
     ((), (None, None, None, None), (13, None, None), (2, 11, 12, 11, 5, 15))),
    (((), (9, None, None, None), (12, None, None), (2, 9, 11, 2, 9, 13)),
     ((('a', 10, 0), ('a', 3, 1)), (None, None, None, None), (12, None, None), (1, 5, 3, 5, 0, 14))),
    (((), (None, None, None, None), (None, None, None), (5, 10, 15, 5, 6, 13)),
     ((('t', 4),), (3, None, None, None), (1, 14, None), (0, 3, 16, 2, 8, 17))),
    (((), (None, None, None, None), (15, 5, 13), (1, 2, 10, 2, 10, 16)),
     ((), (None, None, None, None), (16, 2, None), (8, 9, 5, 6, 11, 8))),
    (((('a', 8, 1),), (None, None, None, None), (1, 16, None), (3, 6, 17, 2, 3, 8)),
     ((), (None, None, None, None), (None, None, None), (5, 3, 17, 6, 7, 3))),
    (((), (8, None, None, None), (2, 3, None), (4, 11, 8, 9, 8, 17)),
     ((('a', 10, 1),), (10, None, None, None), (5, 17, 6), (3, 10, 15, 0, 8, 10))),
    (((), (None, None, None, None), (4, 11, 8), (6, 0, 10, 9, 0, 14)),
     ((), (None, None, None, None), (7, 15, None), (8, 11, 3, 9, 0, 10))),
)

TAIL = (
    (17, 6, 10, 9, 0, 14),
    (8, 11, 3, 9, 0, 10),
)

SLOTS = len(OFFSETS[0])
EXTRA = len(SHARED[0])
HELD = SLOTS + EXTRA
NONE = 31
GROUP = 64


def words(values, bits=5):
    each = 30 // bits
    return [sum(v * (1 << bits * k) for k, v in enumerate(values[s:s + each])) for s in range(0, len(values), each)]


def lookup(packed, n, bits=5):
    each = 30 // bits
    word = packed[0]
    for k, w in enumerate(packed[1:], 1):
        word = jnp.where(n >= each * k, w, word)
    return lax.rem(lax.shift_right_logical(word, bits * lax.rem(n, each)), 1 << bits)


def of_core(core, lists, bits=5):
    return [jnp.where(core == 0, jnp.asarray(a, jnp.int32), jnp.asarray(b, jnp.int32))
            for a, b in zip(*(words(v, bits) for v in lists))]


def column(which, place, k):
    return [NONE if pair[which][place][k] is None else pair[which][place][k] for pair in STEPS]


def kernel(chunks, emb_ref, lab_ref, out_ref, emb, ids, buf, labels, label_rows, row_best, column_best, outgoing,
           incoming, load_sem, send_sem, recv_sem, give_sem, take_sem, label_send, label_recv, label_give,
           label_take, result_send, result_recv):
    rows, width = emb.shape
    part = rows // chunks
    load = pltpu.make_async_copy(emb_ref, emb, load_sem.at[0])
    load.start()
    load_ids = pltpu.make_async_copy(lab_ref, ids, load_sem.at[1])
    load_ids.start()
    gx = lax.axis_index("grp")
    mem = lax.axis_index("mem")
    core = lax.rem(mem, 2)
    other = 1 - core
    gy = lax.rem(mem // 2, SIDE)
    gz = mem // (2 * SIDE)

    def at(offset, on):
        x, y, z = (lax.rem(g + k, SIDE) for g, k in zip((gx, gy, gz), offset))
        return (x, (z * SIDE + y) * 2 + on)

    near = [at(direction, core) for direction in DIRS]
    barrier = pltpu.get_barrier_semaphore()
    for device in near:
        pl.semaphore_signal(barrier, inc=1, device_id=device, device_id_type=MESH)
    pl.semaphore_signal(barrier, inc=1, device_id=(gx, mem + 1 - 2 * core), device_id_type=MESH)

    def chunk_of(slot, h):
        return buf.at[slot, pl.ds(h * part, part)]

    def relay(source, target, h, direction):
        return pltpu.make_async_remote_copy(
            src_ref=chunk_of(source, h), dst_ref=chunk_of(target, h),
            send_sem=send_sem.at[target, h], recv_sem=recv_sem.at[target, h],
            device_id=near[direction], device_id_type=MESH)

    def relay_label(source, target, direction):
        return pltpu.make_async_remote_copy(
            src_ref=labels.at[source], dst_ref=labels.at[target],
            send_sem=label_send.at[target], recv_sem=label_recv.at[target],
            device_id=near[direction], device_id_type=MESH)

    def send(source, target, h, direction):
        if h == 0:
            relay_label(source, target, direction).start()
        relay(source, target, h, direction).start()

    def share(slot, k, h):
        return pltpu.make_async_remote_copy(
            src_ref=chunk_of(slot, h), dst_ref=chunk_of(SLOTS + k, h),
            send_sem=give_sem.at[k, h], recv_sem=take_sem.at[k, h],
            device_id=(gx, mem + 1 - 2 * core), device_id_type=MESH)

    def share_label(slot, k):
        return pltpu.make_async_remote_copy(
            src_ref=labels.at[slot], dst_ref=labels.at[SLOTS + k],
            send_sem=label_give.at[k], recv_sem=label_take.at[k],
            device_id=(gx, mem + 1 - 2 * core), device_id_type=MESH)

    def give(which, slot, h):
        if slot in SHARED[1 - which]:
            k = SHARED[1 - which].index(slot)
            if h == 0:
                share_label(slot, k).start()
            share(slot, k, h).start()

    homes = []
    for which in (0, 1):
        offsets = OFFSETS[which] + tuple(OFFSETS[1 - which][k] for k in SHARED[which])
        homes.append([at([SIDE - k for k in o], which if n < SLOTS else 1 - which) for n, o in enumerate(offsets)])
    home_x, home_mem = (of_core(core, [[h[k] for h in held] for held in homes]) for k in (0, 1))

    load_ids.wait()
    labels[0] = ids[...].astype(jnp.float32)
    load.wait()
    for h in range(chunks):
        e = emb[pl.ds(h * part, part)]
        squares = jnp.sum(e * e, axis=1, keepdims=True)
        buf[0, pl.ds(h * part, part)] = (e * lax.rsqrt(squares + 1e-06)).astype(jnp.bfloat16)
        if h == 0:
            pl.semaphore_wait(barrier, len(DIRS) + 1)
        for which in (0, 1):
            @pl.when(core == which)
            def _(which=which, h=h):
                for move in FIRST_SENDS[which]:
                    if move[2] == h:
                        send(*move)

    for which in (0, 1):
        @pl.when(core == which)
        def _(which=which):
            for h in range(chunks):
                give(which, 0, h)

    def clear(slot, carry):
        column_best[slot] = jnp.full(column_best.shape[1:], FILL, jnp.float32)

        @pl.when(slot < SLOTS)
        def _():
            row_best[slot] = jnp.full(row_best.shape[1:], FILL, jnp.float32)
        return carry

    lax.fori_loop(0, HELD, clear, 0)

    def spread(slot):
        label_rows[slot] = jnp.broadcast_to(labels[slot], (128, rows)).T

    def tile(left, right, own=False):
        sims = lax.dot_general(jnp.concatenate([buf[a] for a in left], axis=0), buf[right], (((1,), (1,)), ((), ())),
                               preferred_element_type=jnp.float32)
        names = labels[right]
        lanes = [slice(k, k + 128) for k in range(0, rows, 128)]
        high = [column_best[right, :, k] for k in lanes]
        for n, a in enumerate(left):
            for r in range(0, rows, GROUP):
                mine = label_rows[a, pl.ds(r, GROUP)]
                top = row_best[a, pl.ds(r, GROUP)]
                for m, k in enumerate(lanes):
                    keep = mine == names[:, k]
                    if own:
                        keep = keep & (lax.broadcasted_iota(jnp.int32, (GROUP, 128), 0) + r
                                       != lax.broadcasted_iota(jnp.int32, (GROUP, 128), 1) + m * 128)
                    scores = jnp.where(keep, sims[n * rows + r:n * rows + r + GROUP, k], FILL)
                    top = jnp.maximum(top, scores)
                    high[m] = jnp.maximum(high[m], jnp.max(scores.reshape(GROUP // 8, 8, 128), axis=0))
                row_best[a, pl.ds(r, GROUP)] = top
        for m, k in enumerate(lanes):
            column_best[right, :, k] = high[m]

    def answer(slot):
        return pltpu.make_async_remote_copy(
            src_ref=outgoing.at[slot], dst_ref=incoming.at[slot],
            send_sem=result_send.at[slot], recv_sem=result_recv,
            device_id=(lookup(home_x, slot), lookup(home_mem, slot)), device_id_type=MESH)

    def finish(slot):
        by_column = jnp.max(column_best[slot], axis=0, keepdims=True)

        @pl.when(slot < SLOTS)
        def _():
            outgoing[slot] = jnp.maximum(by_column, jnp.max(row_best[slot].T, axis=0, keepdims=True))

        @pl.when(slot >= SLOTS)
        def _():
            outgoing[slot] = by_column

        @pl.when(slot > 0)
        def _():
            answer(slot).start()

    def arrived(which, slot, h):
        pltpu.make_async_copy(chunk_of(slot, h), chunk_of(slot, h), recv_sem.at[slot, h]).wait()
        if h == 0:
            pltpu.make_async_copy(labels.at[slot], labels.at[slot], label_recv.at[slot]).wait()
        give(which, slot, h)

    def taken(k):
        for h in range(chunks):
            pltpu.make_async_copy(chunk_of(SLOTS + k, h), chunk_of(SLOTS + k, h), take_sem.at[k, h]).wait()
        pltpu.make_async_copy(labels.at[SLOTS + k], labels.at[SLOTS + k], label_take.at[k]).wait()

    def sent(slot, h):
        relay(0, slot, h, 0).wait_send()

    def moves(n):
        for which in (0, 1):
            todo = STEPS[n][which][0]
            if todo:
                @pl.when(core == which)
                def _(which=which, todo=todo):
                    for op in todo:
                        if op[0] == "a":
                            arrived(which, *op[1:])
                        elif op[0] == "t":
                            taken(op[1])
                        else:
                            if len(op) > 5:
                                sent(*op[5:])
                            send(*op[1:5])

    def table(place):
        return [of_core(core, [column(w, place, k) for w in (0, 1)]) for k in range(len(STEPS[0][0][place]))]

    to_open, to_finish, to_compare = table(1), table(2), table(3)
    spread(0)
    tile((0,), 0, own=True)

    def step(n, carry):
        for g in range(0, len(STEPS), 6):
            @pl.when(lax.div(n, 6) == g // 6)
            def _(g=g):
                for k in range(g, min(g + 6, len(STEPS))):
                    @pl.when(n == k)
                    def _(k=k):
                        moves(k)
        for listed, act in ((to_open, spread), (to_finish, finish)):
            for packed in listed:
                slot = lookup(packed, n)

                @pl.when(slot != NONE)
                def _(slot=slot, act=act):
                    act(slot)
        units = [lookup(packed, n) for packed in to_compare]
        for k in range(0, len(units), 3):
            tile(units[k:k + 2], units[k + 2])
        return carry

    lax.fori_loop(0, len(STEPS), step, 0)
    left = max(len(t) for t in TAIL)
    ends = of_core(core, [(list(t) + [NONE] * left)[:left] for t in TAIL])
    ended = [lookup(ends, n) for n in range(left)]
    for slot in ended:
        held = jnp.where(slot == NONE, 0, slot)
        by_row = jnp.max(row_best[jnp.minimum(held, SLOTS - 1)].T, axis=0, keepdims=True)
        by_column = jnp.max(column_best[held], axis=0, keepdims=True)
        outgoing[held] = jnp.where(held < SLOTS, jnp.maximum(by_row, by_column), by_column)
    for slot in ended:
        @pl.when((slot != NONE) & (slot > 0))
        def _(slot=slot):
            answer(slot).start()
    incoming[0] = outgoing[0]

    for which in (0, 1):
        @pl.when(core == which)
        def _(which=which):
            for move in LAST_SENDS[which]:
                sent(*move)
    for k in range(EXTRA):
        for h in range(chunks):
            share(0, k, h).wait_send()
        share_label(0, k).wait_send()
    for slot in range(1, SLOTS):
        relay_label(0, slot, 0).wait_send()
    for slot in range(1, HELD):
        answer(slot).wait_send()
    rest = incoming.at[pl.ds(1, HELD - 1)]
    pltpu.make_async_copy(rest, rest, result_recv).wait()
    out_ref[...] = jnp.max(incoming[...], axis=0).reshape(rows)


def body(embeddings, cluster_ids):
    rows, width = embeddings.shape
    chunks = 1 + max(h for sends in LAST_SENDS for _, h in sends)
    dma = pltpu.SemaphoreType.DMA
    return pl.pallas_call(
        functools.partial(kernel, chunks),
        out_shape=jax.ShapeDtypeStruct((rows,), jnp.float32),
        in_specs=[pl.BlockSpec(memory_space=pl.ANY), pl.BlockSpec(memory_space=pl.ANY)],
        out_specs=pl.BlockSpec(memory_space=pltpu.VMEM),
        scratch_shapes=[
            pltpu.VMEM((rows, width), jnp.float32),
            pltpu.VMEM((1, rows), jnp.int32),
            pltpu.VMEM((HELD, rows, width), jnp.bfloat16),
            pltpu.VMEM((HELD, 1, rows), jnp.float32),
            pltpu.VMEM((SLOTS, rows, 128), jnp.float32),
            pltpu.VMEM((SLOTS, rows, 128), jnp.float32),
            pltpu.VMEM((HELD, 8, rows), jnp.float32),
            pltpu.VMEM((HELD, 1, rows), jnp.float32),
            pltpu.VMEM((HELD, 1, rows), jnp.float32),
            dma((2,)), dma((SLOTS, chunks)), dma((SLOTS, chunks)), dma((EXTRA, chunks)), dma((EXTRA, chunks)),
            dma((SLOTS,)), dma((SLOTS,)), dma((EXTRA,)), dma((EXTRA,)), dma((HELD,)), dma,
        ],
        compiler_params=pltpu.CompilerParams(
            collective_id=0, has_side_effects=True, vmem_limit_bytes=VMEM_BYTES),
    )(embeddings, cluster_ids.reshape(1, rows))


def solution(mesh):
    return jax.shard_map(
        body,
        mesh=mesh,
        in_specs=(P(("grp", "mem"), None), P(("grp", "mem"), None)),
        out_specs=P(("grp", "mem")),
        check_vma=False,
    )
```
